512 devices in a mesh: face: 8 (over y), row: 8 (over z_hi, core), col: 8 (over z_lo, x).
Axes of the slice: x: 4, y: 8, z: 8 (z_hi: 4, z_lo: 2; z = z_hi * 2 + z_lo), core: 2. Of those that a mesh axis runs over, the one named last changes fastest.
Arguments:
- block_in: bfloat16 [8, 64, 64, 1024], P('face', None, 'row', 'col'), may hold values from -6 to 6
- hidden_state: bfloat16 [8, 64, 64, 1024], P('face', None, 'row', 'col'), may hold values from -0.8984375 to 0.8984375
- state_cotangent: bfloat16 [8, 64, 64, 1024], P('face', None, 'row', 'col'), may hold values from -6 to 6
- kernel: float32 [64, 49], replicated, may hold values from -0.875 to 0.875
- expand_weight: bfloat16 [64, 256], replicated, may hold values from -0.75 to 0.75
- reduce_weight: bfloat16 [256, 64], replicated, may hold values from -0.375 to 0.375
- gates_weight: bfloat16 [128, 128], replicated, may hold values from -0.5 to 0.5
- candidate_weight: bfloat16 [128, 64], replicated, may hold values from -0.5 to 0.5
- seam_face: int32 [8, 4], replicated, may hold values from 0 to 7, as said below
- seam_code: int32 [8, 4], replicated, may hold values from 0 to 3, as said below
Outputs:
- next_state: bfloat16 [8, 64, 64, 1024], P('face', None, 'row', 'col')
- grad_input: bfloat16 [8, 64, 64, 1024], P('face', None, 'row', 'col')
- grad_state: bfloat16 [8, 64, 64, 1024], P('face', None, 'row', 'col')
- grad_kernel: float32 [64, 49], replicated
- grad_expand: float32 [64, 256], replicated
- grad_reduce: float32 [256, 64], replicated
- grad_gates: float32 [128, 128], replicated
- grad_candidate: float32 [128, 64], replicated
The draws below stay inside these ranges and needn't reach their ends.
Inputs may be any that keep to these rules, and one draw needn't show every extreme that they name: `seam_face`: column s holds, for every face, the partner face across its seam s (0 north, 1 south, 2 west, 3 east); each column is a permutation of the 8 faces. `seam_code`: bit 0 set: the partner's edge is on the same side as this one (a half turn), else on the opposite side; bit 1 set: the seam runs in reverse order along the edge. Each of the four codes appears 8 times.
All inputs are finite; a program needn't handle non-finite values.
Results may differ from the reference program's by a relative error of at most 0.019.
Values may be sent and summed in bfloat16 or wider, within the bound.
A program may use at most 64 MiB of HBM per device.

```python
import math
import jax
import jax.numpy as jnp
from jax import lax

C = 64
EXPAND = 256
KSIDE = 7
RIM = 3
TILE_ROWS = 8
TILE_COLS = 128
FACES = 8
FACE_ROWS = 64
FACE_COLS = 1024
CELLS = 524288
N_ROW = 8
N_COL = 8


def draw_seam_face(key, part):
    key = jax.random.fold_in(key, 11)
    columns = [jax.random.permutation(jax.random.fold_in(key, side_number), FACES) for side_number in range(4)]
    return jnp.stack(columns, axis=1).astype(jnp.int32)


def draw_seam_code(key, part):
    key = jax.random.fold_in(key, 12)
    shuffled = jax.random.permutation(key, FACES * 4)
    return (shuffled % 4).reshape(FACES, 4).astype(jnp.int32)


def steps_of(stream_key, dims, cuts, low, high):
    level = 1.0
    for position, parts in cuts:
        heights = jax.random.uniform(jax.random.fold_in(jax.random.fold_in(stream_key, 6), position), (parts,), jnp.float32, low / len(cuts), high / len(cuts))
        level = level * jnp.repeat(jnp.exp(heights), dims[position] // parts).reshape((-1,) + (1,) * (len(dims) - 1 - position))
    return level


def normal_values(key, extent, deviation, bound, pieces=(), kind=jnp.bfloat16):
    drawn = deviation * jax.random.normal(key, extent, jnp.float32)
    if pieces:
        drawn = drawn * steps_of(key, extent, pieces, -0.22, 0.18)
    return jnp.clip(drawn, -bound, bound).astype(kind)


def setup_inputs(seed: int = 0) -> dict:
    key_of = jax.random.split(jax.random.key(seed), 11)
    block_in = normal_values(key_of[0], (FACES, C, FACE_ROWS, FACE_COLS), 1.0, 6.0, ((0, 8), (2, 8), (3, 8)))
    hidden_state = jnp.clip(jax.random.uniform(key_of[1], (FACES, C, FACE_ROWS, FACE_COLS), jnp.float32, -0.8984375, 0.8984375) * steps_of(key_of[1], (FACES, C, FACE_ROWS, FACE_COLS), ((0, 8), (2, 8), (3, 8)), -0.4, 0.0), -0.8984375, 0.8984375).astype(jnp.bfloat16)
    state_cotangent = normal_values(key_of[2], (FACES, C, FACE_ROWS, FACE_COLS), 1.0, 6.0, ((0, 8), (2, 8), (3, 8)))
    kernel = normal_values(key_of[3], (C, KSIDE * KSIDE), (KSIDE * KSIDE) ** -0.5, 0.875, (), jnp.float32)
    expand_weight = normal_values(key_of[4], (C, EXPAND), C ** -0.5, 0.75)
    reduce_weight = normal_values(key_of[5], (EXPAND, C), EXPAND ** -0.5, 0.375)
    gates_weight = normal_values(key_of[6], (2 * C, 2 * C), (2 * C) ** -0.5, 0.5)
    candidate_weight = normal_values(key_of[7], (2 * C, C), (2 * C) ** -0.5, 0.5)
    seam_face = draw_seam_face(jax.random.fold_in(key_of[10], 71), 0)
    seam_code = draw_seam_code(jax.random.fold_in(key_of[10], 71), 0)
    return {"block_in": block_in, "hidden_state": hidden_state, "state_cotangent": state_cotangent, "kernel": kernel, "expand_weight": expand_weight, "reduce_weight": reduce_weight, "gates_weight": gates_weight, "candidate_weight": candidate_weight, "seam_face": seam_face, "seam_code": seam_code}


def contract(weight, values):
    return jnp.dot(weight.astype(jnp.bfloat16).T, values, preferred_element_type=jnp.float32)

def block_step(padded, center, prior_state, kernel, expand_weight, reduce_weight, gates_weight, candidate_weight):
    channels, height, tile_width = center.shape
    cell_count = height * tile_width
    source = padded.astype(jnp.float32)
    summed = jnp.zeros((channels, height, tile_width), jnp.float32)
    for offset in range(KSIDE * KSIDE):
        shift_row = offset // KSIDE
        shift_col = offset % KSIDE
        summed = summed + kernel[:, offset][:, None, None] * source[:, shift_row:shift_row + height, shift_col:shift_col + tile_width]
    flattened = summed.reshape(channels, cell_count)
    average = lax.optimization_barrier(jnp.mean(flattened, axis=0))
    centered = flattened - average
    variance = lax.optimization_barrier(jnp.mean(centered * centered, axis=0))
    normed = (centered * lax.rsqrt(variance + 1e-06)).astype(jnp.bfloat16)
    hidden = contract(expand_weight, normed)
    activated = jax.nn.gelu(hidden, approximate=False).astype(jnp.bfloat16)
    mixed_out = contract(reduce_weight, activated)
    output = (center.reshape(channels, cell_count).astype(jnp.float32) + mixed_out).astype(jnp.bfloat16)
    previous = prior_state.reshape(channels, cell_count)
    previous_float = previous.astype(jnp.float32)
    gate_values = jax.nn.sigmoid(contract(gates_weight, jnp.concatenate([output, previous], axis=0)))
    update = gate_values[:channels]
    reset_gate = gate_values[channels:]
    reset_state = (reset_gate * previous_float).astype(jnp.bfloat16)
    proposal = jnp.tanh(contract(candidate_weight, jnp.concatenate([output, reset_state], axis=0)))
    result = ((1.0 - update) * previous_float + update * proposal).astype(jnp.bfloat16)
    return result.reshape(channels, height, tile_width)

def seam_fill(near, far, seam_face, seam_code, side_number, depth_axis, length_axis):
    partner = seam_face[:, side_number]
    code_value = seam_code[:, side_number]
    same_side = (code_value % 2 == 1)[:, None, None, None]
    reverse_flag = (code_value // 2 == 1)[:, None, None, None]
    near_copy = jnp.take(near, partner, axis=0)
    far_copy = jnp.take(far, partner, axis=0)
    chosen = jnp.where(same_side, jnp.flip(near_copy, depth_axis), far_copy)
    return jnp.where(reverse_flag, jnp.flip(chosen, length_axis), chosen)

def pad_rows(values, seam_face, seam_code):
    top_rows = values[:, :, :RIM, :]
    bottom_rows = values[:, :, -RIM:, :]
    north = seam_fill(top_rows, bottom_rows, seam_face, seam_code, 0, 2, 3)
    south = seam_fill(bottom_rows, top_rows, seam_face, seam_code, 1, 2, 3)
    return jnp.concatenate([north, values, south], axis=2)

def pad_columns(values, seam_face, seam_code):
    left_columns = values[:, :, :, :RIM]
    right_columns = values[:, :, :, -RIM:]
    west = seam_fill(left_columns, right_columns, seam_face, seam_code, 2, 3, 2)
    east = seam_fill(right_columns, left_columns, seam_face, seam_code, 3, 3, 2)
    return jnp.concatenate([west, values, east], axis=3)

def windows(values, axis_number, tile_count, length, rim_width):
    moved_axis = jnp.moveaxis(values, axis_number, 0)
    trailing = moved_axis.shape[1:]
    span = tile_count * length
    upper_rim = moved_axis[:span].reshape((tile_count, length) + trailing)[:, :rim_width]
    middle = moved_axis[rim_width:rim_width + span].reshape((tile_count, length) + trailing)
    lower_rim = moved_axis[2 * rim_width:2 * rim_width + span].reshape((tile_count, length) + trailing)[:, length - rim_width:]
    joined = jnp.concatenate([upper_rim, middle, lower_rim], axis=1)
    return jnp.moveaxis(joined, (0, 1), (axis_number, axis_number + 1))

def all_windows(padded):
    by_rows = windows(padded, 2, N_ROW, TILE_ROWS, RIM)
    by_both = windows(by_rows, 4, N_COL, TILE_COLS, RIM)
    ordered = jnp.transpose(by_both, (0, 2, 4, 1, 3, 5))
    return ordered.reshape((-1, C, TILE_ROWS + 2 * RIM, TILE_COLS + 2 * RIM))

def split_tiles(values):
    shaped = values.reshape((FACES, C, N_ROW, TILE_ROWS, N_COL, TILE_COLS))
    return jnp.transpose(shaped, (0, 2, 4, 1, 3, 5)).reshape((-1, C, TILE_ROWS, TILE_COLS))

def join_tiles(tiles):
    shaped = tiles.reshape((FACES, N_ROW, N_COL, C, TILE_ROWS, TILE_COLS))
    return jnp.transpose(shaped, (0, 3, 1, 4, 2, 5)).reshape((FACES, C, FACE_ROWS, FACE_COLS))

def reference(block_in, hidden_state, state_cotangent, kernel, expand_weight, reduce_weight, gates_weight, candidate_weight, seam_face, seam_code):

    def window_tiles(values):
        return all_windows(pad_columns(pad_rows(values, seam_face, seam_code), seam_face, seam_code))
    windows_all = window_tiles(block_in)
    centers = split_tiles(block_in)
    priors = split_tiles(hidden_state)
    cotangents = split_tiles(state_cotangent)
    expand_float = expand_weight.astype(jnp.float32)
    reduce_float = reduce_weight.astype(jnp.float32)
    gates_float = gates_weight.astype(jnp.float32)
    candidate_float = candidate_weight.astype(jnp.float32)

    def one_tile(tile_items):
        window, center, prior_state, cotangent = tile_items
        next_tile, pullback = jax.vjp(block_step, window, center, prior_state, kernel, expand_float, reduce_float, gates_float, candidate_float)
        return (next_tile,) + tuple(pullback(cotangent))
    results = lax.map(one_tile, (windows_all, centers, priors, cotangents))
    grad_scale = 1.0 / math.sqrt(CELLS)
    unused, unpad_back = jax.vjp(window_tiles, block_in.astype(jnp.float32))
    from_windows = unpad_back(results[1].astype(jnp.float32))[0]
    grad_input = (from_windows + join_tiles(results[2].astype(jnp.float32))).astype(jnp.bfloat16)
    return (join_tiles(results[0]), grad_input, join_tiles(results[3]), lax.optimization_barrier(jnp.sum(results[4], axis=0)) * grad_scale, lax.optimization_barrier(jnp.sum(results[5], axis=0)) * grad_scale, lax.optimization_barrier(jnp.sum(results[6], axis=0)) * grad_scale, lax.optimization_barrier(jnp.sum(results[7], axis=0)) * grad_scale, lax.optimization_barrier(jnp.sum(results[8], axis=0)) * grad_scale)
```

```python
import functools
import math

import jax
import jax.numpy as jnp
import numpy as np
from jax import lax
from jax.experimental import pallas as pl
from jax.experimental.pallas import tpu as pltpu
from jax.sharding import PartitionSpec as P

AXES = ("face", "row", "col")
CH = 64
HID = 256
KS = 7
RIM = 3
TR = 8
TC = 128
PR = TR + 2 * RIM
PACK_ROWS = 512
BF = jnp.bfloat16
F32 = jnp.float32
MESH = pl.DeviceIdType.MESH
VMEM = pl.BlockSpec(memory_space=pltpu.VMEM)
SMEM = pl.BlockSpec(memory_space=pltpu.SMEM)
LIMIT = 40 * 1024 * 1024


def spread_matrix():
    table = np.zeros((TC, PR * TC), np.float32)
    for row in range(PR):
        for i in range(6):
            table[row * 8 + i, row * TC + (i - RIM) % TC] = 1.0
    return table


def turn_matrices():
    table = np.zeros((4, TC, TC), np.float32)
    for code in range(4):
        for row in range(PR):
            for i in range(6):
                to_row = PR - 1 - row if code >= 2 else row
                to_i = 5 - i if code % 2 else i
                table[code, row * 8 + i, to_row * 8 + to_i] = 1.0
    return table


def dot(a, b):
    return jnp.dot(a, b, preferred_element_type=F32)


def dot_nt(a, b):
    return lax.dot_general(a, b, (((1,), (1,)), ((), ())), preferred_element_type=F32)


def send(src, dst, send_sem, recv_sem, device):
    return pltpu.make_async_remote_copy(
        src_ref=src,
        dst_ref=dst,
        send_sem=send_sem,
        recv_sem=recv_sem,
        device_id=device,
        device_id_type=MESH,
    )


def partner_of(seam_face, side, face, count):
    found = jnp.int32(0)
    for other in range(count):
        found = jnp.where(seam_face[other, side] == face, other, found)
    return found


def kind_of(side_bit, code):
    odd = lax.rem(code, 2)
    return jnp.where(side_bit == 0, 1 - odd, odd)


class Place:
    def __init__(self, dims):
        self.nf, self.nr, self.nc = dims
        self.f = lax.axis_index("face")
        self.r = lax.axis_index("row")
        self.c = lax.axis_index("col")
        self.top = self.r == 0
        self.bottom = self.r == self.nr - 1
        self.left = self.c == 0
        self.right = self.c == self.nc - 1
        self.row_edge = jnp.logical_or(self.top, self.bottom)
        self.col_edge = jnp.logical_or(self.left, self.right)
        self.row_kind = jnp.where(self.top, 0, 1)
        self.col_kind = jnp.where(self.left, 0, 1)

    def at(self, f=None, r=None, c=None):
        return (
            self.f if f is None else f,
            self.r if r is None else r,
            self.c if c is None else c,
        )

    def row_group(self):
        other_r = self.nr - 1 - self.r
        other_c = self.nc - 1 - self.c
        return [
            (self.at(c=other_c), self.row_kind * 2 + 1, self.row_kind * 2 + 1),
            (self.at(r=other_r), self.row_kind * 2, (1 - self.row_kind) * 2),
            (self.at(r=other_r, c=other_c), self.row_kind * 2 + 1, (1 - self.row_kind) * 2 + 1),
        ]

    def col_group(self):
        other_r = self.nr - 1 - self.r
        other_c = self.nc - 1 - self.c
        return [
            (self.at(r=other_r), self.col_kind * 2 + 1, self.col_kind * 2 + 1),
            (self.at(c=other_c), self.col_kind * 2, (1 - self.col_kind) * 2),
            (self.at(r=other_r, c=other_c), self.col_kind * 2 + 1, (1 - self.col_kind) * 2 + 1),
        ]

    def ring(self, axis):
        index, count = {"face": (self.f, self.nf), "row": (self.r, self.nr), "col": (self.c, self.nc)}[axis]
        out = []
        for step in range(1, count):
            other = lax.rem(index + step, count)
            out.append((other, self.at(**{axis[0]: other}), step))
        return out


def start_group(group, src, slots, sems, back):
    for i, (device, slot, unused) in enumerate(group):
        send(src, slots.at[slot], sems.at[back, i], sems.at[back + 1, slot], device).start()


def wait_group(group, src, slots, sems, back):
    for i, (device, unused, slot) in enumerate(group):
        send(src, slots.at[slot], sems.at[back, i], sems.at[back + 1, slot], device).wait_recv()


def done_group(group, src, slots, sems, back):
    for i, (device, unused, slot) in enumerate(group):
        send(src, slots.at[slot], sems.at[back, i], sems.at[back + 1, slot], device).wait_send()


def start_ring(ring, me, src_of, slots, sems):
    for other, device, step in ring:
        send(src_of(other), slots.at[me], sems.at[0, step], sems.at[1, me], device).start()


def wait_ring(ring, src_of, slots, sems):
    for other, device, step in ring:
        send(src_of(other), slots.at[other], sems.at[0, step], sems.at[1, other], device).wait_recv()


def done_ring(ring, src_of, slots, sems):
    for other, device, step in ring:
        send(src_of(other), slots.at[other], sems.at[0, step], sems.at[1, other], device).wait_send()


def greet(barrier, device):
    pl.semaphore_signal(barrier, inc=1, device_id=device, device_id_type=MESH)


def gather_kernel(
    dims,
    x_ref,
    spread_ref,
    turn_ref,
    flip_ref,
    sf,
    sc,
    xw_out,
    halo_out,
    xw,
    strips,
    chosen,
    faces,
    pack,
    sides,
    col_strips,
    col_chosen,
    col_faces,
    near,
    group_sem,
    row_face_sem,
    col_face_sem,
):
    at = Place(dims)
    nf, nr, nc = dims
    edge = jnp.logical_or(at.row_edge, at.col_edge)
    barrier = pltpu.get_barrier_semaphore()
    expected = (
        jnp.where(at.top, 0, 1)
        + jnp.where(at.bottom, 0, 1)
        + jnp.where(at.left, 0, 1)
        + jnp.where(at.right, 0, 1)
        + jnp.where(at.row_edge, 3, 0)
        + jnp.where(at.col_edge, 3, 0)
        + jnp.where(edge, nf - 1, 0)
    )
    above = at.at(r=jnp.maximum(at.r - 1, 0))
    below = at.at(r=jnp.minimum(at.r + 1, nr - 1))
    before = at.at(c=jnp.maximum(at.c - 1, 0))
    after = at.at(c=jnp.minimum(at.c + 1, nc - 1))
    has_above = jnp.logical_not(at.top)
    has_below = jnp.logical_not(at.bottom)
    has_before = jnp.logical_not(at.left)
    has_after = jnp.logical_not(at.right)
    for present, device in ((has_above, above), (has_below, below), (has_before, before), (has_after, after)):

        @pl.when(present)
        def _(device=device):
            greet(barrier, device)

    @pl.when(at.row_edge)
    def _():
        for device, unused, unused2 in at.row_group():
            greet(barrier, device)

    @pl.when(at.col_edge)
    def _():
        for device, unused, unused2 in at.col_group():
            greet(barrier, device)

    @pl.when(edge)
    def _():
        for unused, device, unused2 in at.ring("face"):
            greet(barrier, device)

    xw[RIM : RIM + TR] = x_ref[...]
    pl.semaphore_wait(barrier, expected)

    def to_above():
        return send(xw.at[pl.ds(RIM, RIM)], xw.at[pl.ds(RIM + TR, RIM)], near.at[0, 0], near.at[1, 0], above)

    def to_below():
        return send(xw.at[pl.ds(TR, RIM)], xw.at[pl.ds(0, RIM)], near.at[0, 1], near.at[1, 1], below)

    def own_edge():
        return xw.at[pl.ds(jnp.where(at.top, RIM, TR), RIM)]

    @pl.when(at.row_edge)
    def _():
        start_group(at.row_group(), own_edge(), strips, group_sem, 0)

    @pl.when(has_above)
    def _():
        to_above().start()

    @pl.when(has_below)
    def _():
        to_below().start()

    @pl.when(at.row_edge)
    def _():
        group = at.row_group()
        strips[at.row_kind * 2] = own_edge()[...]
        wait_group(group, own_edge(), strips, group_sem, 0)
        taker = partner_of(sf, at.row_kind, at.f, nf)
        code = sc[taker, at.row_kind]
        wanted = kind_of(at.row_kind, code) * 2 + code // 2
        picked = strips[wanted]
        chosen[...] = picked
        ring = at.ring("face")
        start_ring(ring, at.f, lambda other: chosen, faces, row_face_sem)
        faces[at.f] = picked
        wait_ring(ring, lambda other: chosen, faces, row_face_sem)
        code = sc[at.f, at.row_kind]
        strip = faces[sf[at.f, at.row_kind]].astype(F32)
        turned = jnp.concatenate([strip[2:3], strip[1:2], strip[0:1]], axis=0)
        strip = jnp.where(lax.rem(code, 2) == 1, turned, strip)
        mirrored = dot(strip.reshape(RIM * CH, TC).astype(BF), flip_ref[...]).reshape(RIM, CH, TC)
        strip = jnp.where(code >= 2, mirrored, strip)
        xw[pl.ds(jnp.where(at.top, 0, RIM + TR), RIM)] = strip.astype(BF)

    @pl.when(has_below)
    def _():
        to_above().wait_recv()

    @pl.when(has_above)
    def _():
        to_below().wait_recv()

    flat = jnp.concatenate([xw[row] for row in range(PR)], axis=1)
    pack[...] = dot_nt(flat, spread_ref[...]).astype(BF)

    def to_before():
        return send(pack, sides.at[1], near.at[0, 2], near.at[1, 2], before)

    def to_after():
        return send(pack, sides.at[0], near.at[0, 3], near.at[1, 3], after)

    @pl.when(at.col_edge)
    def _():
        start_group(at.col_group(), pack, col_strips, group_sem, 2)

    @pl.when(has_before)
    def _():
        to_before().start()

    @pl.when(has_after)
    def _():
        to_after().start()

    xw_out[...] = xw[...]

    @pl.when(at.col_edge)
    def _():
        group = at.col_group()
        col_strips[at.col_kind * 2] = pack[...]
        wait_group(group, pack, col_strips, group_sem, 2)
        taker = partner_of(sf, at.col_kind + 2, at.f, nf)
        code = sc[taker, at.col_kind + 2]
        wanted = kind_of(at.col_kind, code) * 2 + code // 2
        picked = col_strips[wanted]
        col_chosen[...] = picked
        ring = at.ring("face")
        start_ring(ring, at.f, lambda other: col_chosen, col_faces, col_face_sem)
        col_faces[at.f] = picked
        wait_ring(ring, lambda other: col_chosen, col_faces, col_face_sem)
        code = sc[at.f, at.col_kind + 2]
        strip = col_faces[sf[at.f, at.col_kind + 2]]
        sides[at.col_kind] = dot(strip, turn_ref[code]).astype(BF)

    @pl.when(has_after)
    def _():
        to_before().wait_recv()

    @pl.when(has_before)
    def _():
        to_after().wait_recv()

    place = lax.rem(lax.broadcasted_iota(jnp.int32, (CH, TC), 1), 8)
    halo_out[...] = jnp.where(place < RIM, sides[0].astype(F32), sides[1].astype(F32)).astype(BF)

    @pl.when(has_above)
    def _():
        to_above().wait_send()

    @pl.when(has_below)
    def _():
        to_below().wait_send()

    @pl.when(has_before)
    def _():
        to_before().wait_send()

    @pl.when(has_after)
    def _():
        to_after().wait_send()

    @pl.when(at.row_edge)
    def _():
        done_group(at.row_group(), own_edge(), strips, group_sem, 0)
        done_ring(at.ring("face"), lambda other: chosen, faces, row_face_sem)

    @pl.when(at.col_edge)
    def _():
        done_group(at.col_group(), pack, col_strips, group_sem, 2)
        done_ring(at.ring("face"), lambda other: col_chosen, col_faces, col_face_sem)


def tile_kernel(
    xw_ref,
    halo_ref,
    prior_ref,
    cot_ref,
    kernel_ref,
    we_ref,
    wr_ref,
    wg_ref,
    wc_ref,
    spread_ref,
    next_ref,
    prior_grad_ref,
    main_ref,
    rim_ref,
    grads_ref,
    xf,
    ef,
    shifted,
    taps,
    summed,
    back,
    prior,
    cot,
    after,
    prior_grad,
    edge_grad,
    ge,
    gr,
    gg,
    gc,
):
    xf[...] = xw_ref[...].astype(F32)
    ends = dot(halo_ref[...], spread_ref[...])
    for row in range(PR):
        ef[row] = ends[:, row * TC : (row + 1) * TC]
    prior[...] = prior_ref[...].astype(F32).reshape(CH * TR, TC)
    cot[...] = cot_ref[...].astype(F32).reshape(CH * TR, TC)
    lane = lax.broadcasted_iota(jnp.int32, (8, TC), 1)

    def forward(g, carry):
        part = pl.ds(pl.multiple_of(g * 8, 8), 8)
        values = kernel_ref[part, :]
        total = [jnp.zeros((8, TC), F32)] * TR
        for b in range(KS):
            d = b - RIM
            rows = []
            for row in range(PR):
                value = xf[row, part, :]
                if d > 0:
                    value = jnp.where(lane < d, ef[row, part, :], value)
                elif d < 0:
                    value = jnp.where(lane >= TC + d, ef[row, part, :], value)
                if d:
                    value = pltpu.roll(value, (-d) % TC, 1)
                shifted[b, row, part, :] = value
                rows.append(value)
            for a in range(KS):
                tap = a * KS + b
                weight = jnp.broadcast_to(values[:, tap : tap + 1], (8, TC))
                taps[tap, part, :] = weight
                for y in range(TR):
                    total[y] = total[y] + weight * rows[y + a]
        for y in range(TR):
            summed[y, part, :] = total[y]
        return carry

    lax.fori_loop(0, CH // 8, forward, 0)

    we = we_ref[...]
    wr = wr_ref[...]
    wg = wg_ref[...]
    wc = wc_ref[...]
    we_t = we.T
    wr_t = wr.T
    wg_t = wg.T
    wc_t = wc.T
    for ref in (ge, gr, gg, gc):
        ref[...] = jnp.zeros_like(ref)

    def chunk(i, carry):
        r0 = i * 2

        def pair(load):
            return jnp.concatenate([load(r0), load(r0 + 1)], axis=1)

        s = pair(lambda y: summed[y])
        center = s - jnp.mean(s, axis=0, keepdims=True)
        scale = lax.rsqrt(jnp.mean(center * center, axis=0, keepdims=True) + 1e-06)
        unit = center * scale
        normed = unit.astype(BF)
        hidden = dot(we_t, normed)
        acts = []
        slopes = []
        for start in range(0, HID, 32):
            h = hidden[start : start + 32]
            cdf = 0.5 + 0.5 * lax.erf(h * math.sqrt(0.5))
            acts.append((h * cdf).astype(BF))
            slopes.append(cdf + h * (jnp.exp(-0.5 * h * h) * (1.0 / math.sqrt(2.0 * math.pi))))
        act = jnp.concatenate(acts, axis=0)
        slope = jnp.concatenate(slopes, axis=0)
        out = (pair(lambda y: xf[RIM + y]) + dot(wr_t, act)).astype(BF)
        before = pair(lambda y: prior[pl.ds(y, CH, stride=TR), :])
        joined = jnp.concatenate([out, before.astype(BF)], axis=0)
        gates = jax.nn.sigmoid(dot(wg_t, joined))
        update = gates[:CH]
        reset = gates[CH:]
        joined_reset = jnp.concatenate([out, (reset * before).astype(BF)], axis=0)
        proposal = jnp.tanh(dot(wc_t, joined_reset))
        result = (1.0 - update) * before + update * proposal
        g = pair(lambda y: cot[pl.ds(y, CH, stride=TR), :])
        d_cand = (g * update * (1.0 - proposal * proposal)).astype(BF)
        d_joined_reset = dot(wc, d_cand)
        d_reset = d_joined_reset[CH:]
        d_gates = jnp.concatenate(
            [
                g * (proposal - before) * (update * (1.0 - update)),
                d_reset * before * (reset * (1.0 - reset)),
            ],
            axis=0,
        ).astype(BF)
        d_joined = dot(wg, d_gates)
        d_out = (d_joined_reset[:CH] + d_joined[:CH]).astype(BF)
        d_prior = g * (1.0 - update) + d_reset * reset + d_joined[CH:]
        d_hidden = (dot(wr, d_out) * slope).astype(BF)
        d_normed = dot(we, d_hidden)
        ge[...] += dot_nt(normed, d_hidden)
        gr[...] += dot_nt(d_out, act)
        gg[...] += dot_nt(joined, d_gates)
        gc[...] += dot_nt(d_cand, joined_reset)
        d_summed = scale * (
            d_normed
            - jnp.mean(d_normed, axis=0, keepdims=True)
            - unit * jnp.mean(d_normed * unit, axis=0, keepdims=True)
        )
        d_center = d_out.astype(F32)
        for j in range(2):
            y = r0 + j
            cut = slice(j * TC, (j + 1) * TC)
            back[y] = d_summed[:, cut]
            main_ref[RIM + y] = d_center[:, cut]
            after[pl.ds(y, CH, stride=TR), :] = result[:, cut]
            prior_grad[pl.ds(y, CH, stride=TR), :] = d_prior[:, cut]
        return carry

    lax.fori_loop(0, TR // 2, chunk, 0)
    next_ref[...] = after[...].reshape(CH, TR, TC).astype(BF)
    prior_grad_ref[...] = prior_grad[...].reshape(CH, TR, TC).astype(BF)
    grads_ref[0:64] = ge[:, :TC].astype(BF)
    grads_ref[64:128] = ge[:, TC:].astype(BF)
    grads_ref[128:192] = gr[:, :TC].astype(BF)
    grads_ref[192:256] = gr[:, TC:].astype(BF)
    grads_ref[256:384] = gg[...].astype(BF)
    grads_ref[384:448] = gc[...].astype(BF)

    def backward(g, carry):
        part = pl.ds(pl.multiple_of(g * 8, 8), 8)
        rows = [back[y, part, :] for y in range(TR)]
        inner = [jnp.zeros((8, TC), F32)] * PR
        outer = [jnp.zeros((8, TC), F32)] * PR
        kernel_grad = jnp.zeros((8, TC), F32)
        for b in range(KS):
            d = b - RIM
            columns = [None] * PR
            for a in range(KS):
                tap = a * KS + b
                weight = taps[tap, part, :]
                terms = None
                for y in range(TR):
                    product = weight * rows[y]
                    columns[y + a] = product if columns[y + a] is None else columns[y + a] + product
                    term = rows[y] * shifted[b, y + a, part, :]
                    terms = term if terms is None else terms + term
                kernel_grad = jnp.where(lane == tap, jnp.sum(terms, axis=1, keepdims=True), kernel_grad)
            for row in range(PR):
                if d == 0:
                    inner[row] = inner[row] + columns[row]
                    continue
                moved = pltpu.roll(columns[row], d % TC, 1)
                wrapped = lane < d if d > 0 else lane >= TC + d
                inner[row] = inner[row] + jnp.where(wrapped, 0.0, moved)
                outer[row] = outer[row] + jnp.where(wrapped, moved, 0.0)
        for row in range(PR):
            if RIM <= row < RIM + TR:
                main_ref[row, part, :] = main_ref[row, part, :] + inner[row]
            else:
                main_ref[row, part, :] = inner[row]
            edge_grad[row, part, :] = outer[row]
        gc[part, :] = kernel_grad
        return carry

    lax.fori_loop(0, CH // 8, backward, 0)
    grads_ref[448:512] = gc[...].astype(BF)
    flat = jnp.concatenate([edge_grad[row] for row in range(PR)], axis=1).astype(BF)
    rim_ref[...] = dot_nt(flat, spread_ref[...]).astype(BF)


def return_kernel(
    dims,
    main_ref,
    rim_ref,
    grads_ref,
    spread_ref,
    turn_ref,
    flip_ref,
    sf,
    sc,
    input_out,
    grads_out,
    total,
    edges,
    sides,
    col_faces,
    col_chosen,
    col_strips,
    row_sides,
    row_faces,
    row_chosen,
    row_strips,
    a1,
    a2_src,
    a2,
    a3_src,
    a3,
    a4_src,
    a4,
    a5_src,
    a5,
    near,
    group_sem,
    col_face_sem,
    row_face_sem,
    s1,
    s2,
    s3,
    s4,
    s5,
):
    at = Place(dims)
    nf, nr, nc = dims
    part1 = PACK_ROWS // nf
    part2 = part1 // nc
    barrier = pltpu.get_barrier_semaphore()
    face_ring = at.ring("face")
    row_ring = at.ring("row")
    col_ring = at.ring("col")
    for ring in (face_ring, row_ring, col_ring):
        for unused, device, unused2 in ring:
            greet(barrier, device)
    corner = at.at(r=nr - 1 - at.r, c=nc - 1 - at.c)
    any_edge = jnp.logical_or(at.row_edge, at.col_edge)

    @pl.when(any_edge)
    def _():
        greet(barrier, corner)

    pl.semaphore_wait(barrier, nf + nr + nc - 3 + jnp.where(any_edge, 1, 0))

    above = at.at(r=jnp.maximum(at.r - 1, 0))
    below = at.at(r=jnp.minimum(at.r + 1, nr - 1))
    before = at.at(c=jnp.maximum(at.c - 1, 0))
    after = at.at(c=jnp.minimum(at.c + 1, nc - 1))
    has_above = jnp.logical_not(at.top)
    has_below = jnp.logical_not(at.bottom)
    has_before = jnp.logical_not(at.left)
    has_after = jnp.logical_not(at.right)

    def to_before():
        return send(rim_ref, sides.at[1], near.at[0, 2], near.at[1, 2], before)

    def to_after():
        return send(rim_ref, sides.at[0], near.at[0, 3], near.at[1, 3], after)

    @pl.when(at.col_edge)
    def _():
        start_ring(face_ring, at.f, lambda other: rim_ref, col_faces, col_face_sem)

    @pl.when(has_before)
    def _():
        to_before().start()

    @pl.when(has_after)
    def _():
        to_after().start()

    def piece1(other):
        return grads_ref.at[pl.ds(pl.multiple_of(other * part1, part1), part1)]

    start_ring(face_ring, at.f, piece1, a1, s1)
    a1[at.f] = piece1(at.f)[...]

    place = lax.rem(lax.broadcasted_iota(jnp.int32, (CH, TC), 1), 8)
    low = place < RIM

    @pl.when(at.col_edge)
    def _():
        side = at.col_kind + 2
        col_faces[at.f] = rim_ref[...]
        wait_ring(face_ring, lambda other: rim_ref, col_faces, col_face_sem)
        taker = partner_of(sf, side, at.f, nf)
        strip = col_faces[taker].astype(F32)
        strip = jnp.where(low == at.left, strip, 0.0).astype(BF)
        turned = dot(strip, turn_ref[sc[taker, side]]).astype(BF)
        col_chosen[...] = turned
        start_group(at.col_group(), col_chosen, col_strips, group_sem, 0)
        col_strips[at.col_kind * 2] = turned

    wait_ring(face_ring, piece1, a1, s1)
    partial = a1[0].astype(F32)
    for other in range(1, nf):
        partial = partial + a1[other].astype(F32)
    a2_src[...] = partial

    def piece2(other):
        return a2_src.at[pl.ds(pl.multiple_of(other * part2, part2), part2)]

    start_ring(col_ring, at.c, piece2, a2, s2)
    a2[at.c] = piece2(at.c)[...]

    def seam_total(strips, kind, first_side):
        gathered = None
        for side_bit in range(2):
            taker = partner_of(sf, first_side + side_bit, at.f, nf)
            code = sc[taker, first_side + side_bit]
            mine = kind_of(side_bit, code) == kind
            for mirror in range(2):
                use = jnp.logical_and(mine, code // 2 == mirror)
                term = jnp.where(use, strips[side_bit * 2 + mirror].astype(F32), 0.0)
                gathered = term if gathered is None else gathered + term
        return gathered

    @pl.when(at.col_edge)
    def _():
        wait_group(at.col_group(), col_chosen, col_strips, group_sem, 0)
        sides[at.col_kind] = seam_total(col_strips, at.col_kind, 2).astype(BF)

    @pl.when(has_after)
    def _():
        to_before().wait_recv()

    @pl.when(has_before)
    def _():
        to_after().wait_recv()

    rim = jnp.where(low, sides[1].astype(F32), sides[0].astype(F32)).astype(BF)
    spread = dot(rim, spread_ref[...])
    for row in range(PR):
        total[row] = main_ref[row] + spread[:, row * TC : (row + 1) * TC]
    edges[0] = total[0:RIM].astype(BF)
    edges[1] = total[RIM + TR : PR].astype(BF)

    def to_above():
        return send(edges.at[0], row_sides.at[1], near.at[0, 0], near.at[1, 0], above)

    def to_below():
        return send(edges.at[1], row_sides.at[0], near.at[0, 1], near.at[1, 1], below)

    def own_edge():
        return edges.at[at.row_kind]

    @pl.when(at.row_edge)
    def _():
        start_ring(face_ring, at.f, lambda other: own_edge(), row_faces, row_face_sem)

    @pl.when(has_above)
    def _():
        to_above().start()

    @pl.when(has_below)
    def _():
        to_below().start()

    wait_ring(col_ring, piece2, a2, s2)
    partial = a2[0]
    for other in range(1, nc):
        partial = partial + a2[other]
    a3_src[...] = partial
    start_ring(row_ring, at.r, lambda other: a3_src, a3, s3)
    a3[at.r] = partial

    @pl.when(at.row_edge)
    def _():
        row_faces[at.f] = own_edge()[...]
        wait_ring(face_ring, lambda other: own_edge(), row_faces, row_face_sem)
        taker = partner_of(sf, at.row_kind, at.f, nf)
        code = sc[taker, at.row_kind]
        strip = row_faces[taker].astype(F32)
        turned = jnp.concatenate([strip[2:3], strip[1:2], strip[0:1]], axis=0)
        strip = jnp.where(lax.rem(code, 2) == 1, turned, strip)
        mirrored = dot(strip.reshape(RIM * CH, TC).astype(BF), flip_ref[...]).reshape(RIM, CH, TC)
        strip = jnp.where(code >= 2, mirrored, strip).astype(BF)
        row_chosen[...] = strip
        start_group(at.row_group(), row_chosen, row_strips, group_sem, 2)
        row_strips[at.row_kind * 2] = strip

    wait_ring(row_ring, lambda other: a3_src, a3, s3)
    partial = a3[0]
    for other in range(1, nr):
        partial = partial + a3[other]
    a4_src[...] = partial
    start_ring(col_ring, at.c, lambda other: a4_src, a4, s4)
    a4[at.c] = partial

    @pl.when(at.row_edge)
    def _():
        wait_group(at.row_group(), row_chosen, row_strips, group_sem, 2)
        gathered = seam_total(row_strips, at.row_kind, 0)
        spot = pl.ds(jnp.where(at.top, RIM, TR), RIM)
        total[spot] = total[spot] + gathered

    @pl.when(has_below)
    def _():
        to_above().wait_recv()
        total[TR : TR + RIM] = total[TR : TR + RIM] + row_sides[1].astype(F32)

    @pl.when(has_above)
    def _():
        to_below().wait_recv()
        total[RIM : 2 * RIM] = total[RIM : 2 * RIM] + row_sides[0].astype(F32)

    wait_ring(col_ring, lambda other: a4_src, a4, s4)
    full = jnp.concatenate([a4[other] for other in range(nc)], axis=0).astype(BF)
    a5_src[...] = full
    start_ring(face_ring, at.f, lambda other: a5_src, a5, s5)
    a5[at.f] = full
    input_out[...] = total[RIM : RIM + TR].astype(BF)
    wait_ring(face_ring, lambda other: a5_src, a5, s5)
    for other in range(nf):
        grads_out[other * part1 : (other + 1) * part1] = a5[other]

    @pl.when(has_above)
    def _():
        to_above().wait_send()

    @pl.when(has_below)
    def _():
        to_below().wait_send()

    @pl.when(has_before)
    def _():
        to_before().wait_send()

    @pl.when(has_after)
    def _():
        to_after().wait_send()

    @pl.when(at.col_edge)
    def _():
        done_ring(face_ring, lambda other: rim_ref, col_faces, col_face_sem)
        done_group(at.col_group(), col_chosen, col_strips, group_sem, 0)

    @pl.when(at.row_edge)
    def _():
        done_ring(face_ring, lambda other: own_edge(), row_faces, row_face_sem)
        done_group(at.row_group(), row_chosen, row_strips, group_sem, 2)

    done_ring(face_ring, piece1, a1, s1)
    done_ring(col_ring, piece2, a2, s2)
    done_ring(row_ring, lambda other: a3_src, a3, s3)
    done_ring(col_ring, lambda other: a4_src, a4, s4)
    done_ring(face_ring, lambda other: a5_src, a5, s5)


def tile_step(xw, halo, prior, cot, kernel, we, wr, wg, wc, spread):
    tile = jax.ShapeDtypeStruct((CH, TR, TC), BF)
    wide = (PR, CH, TC)
    return pl.pallas_call(
        tile_kernel,
        out_shape=(
            tile,
            tile,
            jax.ShapeDtypeStruct(wide, F32),
            jax.ShapeDtypeStruct((CH, TC), BF),
            jax.ShapeDtypeStruct((PACK_ROWS, TC), BF),
        ),
        in_specs=[VMEM] * 10,
        out_specs=(VMEM,) * 5,
        scratch_shapes=[
            pltpu.VMEM(wide, F32),
            pltpu.VMEM(wide, F32),
            pltpu.VMEM((KS,) + wide, F32),
            pltpu.VMEM((KS * KS, CH, TC), F32),
            pltpu.VMEM((TR, CH, TC), F32),
            pltpu.VMEM((TR, CH, TC), F32),
            pltpu.VMEM((CH * TR, TC), F32),
            pltpu.VMEM((CH * TR, TC), F32),
            pltpu.VMEM((CH * TR, TC), F32),
            pltpu.VMEM((CH * TR, TC), F32),
            pltpu.VMEM(wide, F32),
            pltpu.VMEM((CH, HID), F32),
            pltpu.VMEM((CH, HID), F32),
            pltpu.VMEM((2 * CH, 2 * CH), F32),
            pltpu.VMEM((CH, 2 * CH), F32),
        ],
        compiler_params=pltpu.CompilerParams(vmem_limit_bytes=LIMIT),
        name="tile_step",
    )(xw, halo, prior, cot, kernel, we, wr, wg, wc, spread)


def dma(*shape):
    return pltpu.SemaphoreType.DMA(shape)


def gather_halos(dims, rows, spread, turn, flip, sf, sc):
    nf = dims[0]
    strip = (RIM, CH, TC)
    return pl.pallas_call(
        functools.partial(gather_kernel, dims),
        out_shape=(
            jax.ShapeDtypeStruct((PR, CH, TC), BF),
            jax.ShapeDtypeStruct((CH, TC), BF),
        ),
        in_specs=[VMEM] * 4 + [SMEM] * 2,
        out_specs=(VMEM, VMEM),
        scratch_shapes=[
            pltpu.VMEM((PR, CH, TC), BF),
            pltpu.VMEM((4,) + strip, BF),
            pltpu.VMEM(strip, BF),
            pltpu.VMEM((nf,) + strip, BF),
            pltpu.VMEM((CH, TC), BF),
            pltpu.VMEM((2, CH, TC), BF),
            pltpu.VMEM((4, CH, TC), BF),
            pltpu.VMEM((CH, TC), BF),
            pltpu.VMEM((nf, CH, TC), BF),
            dma(2, 4),
            dma(4, 4),
            dma(2, nf),
            dma(2, nf),
        ],
        compiler_params=pltpu.CompilerParams(
            collective_id=0, has_side_effects=True, vmem_limit_bytes=LIMIT
        ),
        name="gather_halos",
    )(rows, spread, turn, flip, sf, sc)


def return_grads(dims, main, rim, grads, spread, turn, flip, sf, sc):
    nf, nr, nc = dims
    strip = (RIM, CH, TC)
    part1 = PACK_ROWS // nf
    part2 = part1 // nc
    return pl.pallas_call(
        functools.partial(return_kernel, dims),
        out_shape=(
            jax.ShapeDtypeStruct((TR, CH, TC), BF),
            jax.ShapeDtypeStruct((PACK_ROWS, TC), BF),
        ),
        in_specs=[VMEM] * 6 + [SMEM] * 2,
        out_specs=(VMEM, VMEM),
        scratch_shapes=[
            pltpu.VMEM((PR, CH, TC), F32),
            pltpu.VMEM((2,) + strip, BF),
            pltpu.VMEM((2, CH, TC), BF),
            pltpu.VMEM((nf, CH, TC), BF),
            pltpu.VMEM((CH, TC), BF),
            pltpu.VMEM((4, CH, TC), BF),
            pltpu.VMEM((2,) + strip, BF),
            pltpu.VMEM((nf,) + strip, BF),
            pltpu.VMEM(strip, BF),
            pltpu.VMEM((4,) + strip, BF),
            pltpu.VMEM((nf, part1, TC), BF),
            pltpu.VMEM((part1, TC), F32),
            pltpu.VMEM((nc, part2, TC), F32),
            pltpu.VMEM((part2, TC), F32),
            pltpu.VMEM((nr, part2, TC), F32),
            pltpu.VMEM((part2, TC), F32),
            pltpu.VMEM((nc, part2, TC), F32),
            pltpu.VMEM((part1, TC), BF),
            pltpu.VMEM((nf, part1, TC), BF),
            dma(2, 4),
            dma(4, 4),
            dma(2, nf),
            dma(2, nf),
            dma(2, nf),
            dma(2, nc),
            dma(2, nr),
            dma(2, nc),
            dma(2, nf),
        ],
        compiler_params=pltpu.CompilerParams(
            collective_id=1, has_side_effects=True, vmem_limit_bytes=LIMIT
        ),
        name="return_grads",
    )(main, rim, grads, spread, turn, flip, sf, sc)


def body(dims, cell_total, block_in, hidden_state, state_cotangent, kernel, we, wr, wg, wc, sf, sc):
    spread = jnp.asarray(spread_matrix(), BF)
    turn = jnp.asarray(turn_matrices(), BF)
    flip = jnp.asarray(np.eye(TC, dtype=np.float32)[::-1].copy(), BF)
    rows = jnp.transpose(block_in[0], (1, 0, 2))
    xw, halo = gather_halos(dims, rows, spread, turn, flip, sf, sc)
    next_state, prior_grad, main, rim, grads = tile_step(
        xw, halo, hidden_state[0], state_cotangent[0], kernel, we, wr, wg, wc, spread
    )
    input_grad, summed = return_grads(dims, main, rim, grads, spread, turn, flip, sf, sc)
    summed = summed.astype(F32) * (1.0 / math.sqrt(cell_total))
    halves = summed.reshape(8, CH, TC)
    return (
        next_state[None],
        jnp.transpose(input_grad, (1, 0, 2))[None],
        prior_grad[None],
        halves[7][:, : KS * KS],
        jnp.concatenate([halves[0], halves[1]], axis=1),
        jnp.concatenate([halves[2], halves[3]], axis=1).T,
        summed[256:384],
        halves[6].T,
    )


def solution(mesh):
    dims = tuple(mesh.shape[name] for name in AXES)
    cell_total = dims[0] * dims[1] * dims[2] * TR * TC
    tiles = P("face", None, "row", "col")
    return jax.shard_map(
        functools.partial(body, dims, cell_total),
        mesh=mesh,
        in_specs=(tiles,) * 3 + (P(),) * 7,
        out_specs=(tiles,) * 3 + (P(),) * 5,
        check_vma=False,
    )
```

```python
import functools
import math

import jax
import jax.numpy as jnp
from jax import lax
from jax.experimental import pallas as pl
from jax.experimental.pallas import tpu as pltpu
from jax.sharding import PartitionSpec as P

AXES = ("face", "row", "col")
CH = 64
HID = 256
KS = 7
RIM = 3
TR = 8
TC = 128
PR = TR + 2 * RIM
PACK_ROWS = 512
BF = jnp.bfloat16
F32 = jnp.float32
MESH = pl.DeviceIdType.MESH
VMEM = pl.BlockSpec(memory_space=pltpu.VMEM)
SMEM = pl.BlockSpec(memory_space=pltpu.SMEM)
LIMIT = 40 * 1024 * 1024


def spread_block(row):
    source = lax.broadcasted_iota(jnp.int32, (TC, TC), 0)
    lane = lax.broadcasted_iota(jnp.int32, (TC, TC), 1)
    place = jnp.where(lane >= TC - RIM, lane - (TC - RIM), jnp.where(lane < RIM, lane + RIM, -TC * 8))
    return jnp.where(source == row * 8 + place, 1.0, 0.0).astype(BF)


def turn_matrix(code):
    source = lax.broadcasted_iota(jnp.int32, (TC, TC), 0)
    lane = lax.broadcasted_iota(jnp.int32, (TC, TC), 1)
    row = lane // 8
    place = lane % 8
    from_row = jnp.where(code >= 2, PR - 1 - row, row)
    from_place = jnp.where(code % 2 == 1, 5 - place, place)
    used = jnp.logical_and(place < 2 * RIM, row < PR)
    return jnp.where(jnp.where(used, from_row * 8 + from_place, -1) == source, 1.0, 0.0).astype(BF)


def flip_matrix():
    source = lax.broadcasted_iota(jnp.int32, (TC, TC), 0)
    lane = lax.broadcasted_iota(jnp.int32, (TC, TC), 1)
    return jnp.where(source == TC - 1 - lane, 1.0, 0.0).astype(BF)


def dot(a, b):
    return jnp.dot(a, b, preferred_element_type=F32)


def dot_nt(a, b):
    return lax.dot_general(a, b, (((1,), (1,)), ((), ())), preferred_element_type=F32)


def send(src, dst, send_sem, recv_sem, device):
    return pltpu.make_async_remote_copy(
        src_ref=src,
        dst_ref=dst,
        send_sem=send_sem,
        recv_sem=recv_sem,
        device_id=device,
        device_id_type=MESH,
    )


def partner_of(seam_face, side, face, count):
    found = jnp.int32(0)
    for other in range(count):
        found = jnp.where(seam_face[side, other] == face, other, found)
    return found


def kind_of(side_bit, code):
    odd = lax.rem(code, 2)
    return jnp.where(side_bit == 0, 1 - odd, odd)


class Place:
    def __init__(self, dims):
        self.nf, self.nr, self.nc = dims
        self.f = lax.axis_index("face")
        self.r = lax.axis_index("row")
        self.c = lax.axis_index("col")
        self.top = self.r == 0
        self.bottom = self.r == self.nr - 1
        self.left = self.c == 0
        self.right = self.c == self.nc - 1
        self.row_edge = jnp.logical_or(self.top, self.bottom)
        self.col_edge = jnp.logical_or(self.left, self.right)
        self.row_kind = jnp.where(self.top, 0, 1)
        self.col_kind = jnp.where(self.left, 0, 1)

    def at(self, f=None, r=None, c=None):
        return (
            self.f if f is None else f,
            self.r if r is None else r,
            self.c if c is None else c,
        )

    def row_group(self):
        other_r = self.nr - 1 - self.r
        other_c = self.nc - 1 - self.c
        return [
            (self.at(c=other_c), self.row_kind * 2 + 1, self.row_kind * 2 + 1),
            (self.at(r=other_r), self.row_kind * 2, (1 - self.row_kind) * 2),
            (self.at(r=other_r, c=other_c), self.row_kind * 2 + 1, (1 - self.row_kind) * 2 + 1),
        ]

    def col_group(self):
        other_r = self.nr - 1 - self.r
        other_c = self.nc - 1 - self.c
        return [
            (self.at(r=other_r), self.col_kind * 2 + 1, self.col_kind * 2 + 1),
            (self.at(c=other_c), self.col_kind * 2, (1 - self.col_kind) * 2),
            (self.at(r=other_r, c=other_c), self.col_kind * 2 + 1, (1 - self.col_kind) * 2 + 1),
        ]

    def ring(self, axis):
        index, count = {"face": (self.f, self.nf), "row": (self.r, self.nr), "col": (self.c, self.nc)}[axis]
        out = []
        for step in range(1, count):
            other = lax.rem(index + step, count)
            out.append((other, self.at(**{axis[0]: other}), step))
        return out


def start_group(group, src, slots, sems, back):
    for i, (device, slot, unused) in enumerate(group):
        send(src, slots.at[slot], sems.at[back, i], sems.at[back + 1, slot], device).start()


def wait_group(group, src, slots, sems, back):
    for i, (device, unused, slot) in enumerate(group):
        send(src, slots.at[slot], sems.at[back, i], sems.at[back + 1, slot], device).wait_recv()


def done_group(group, src, slots, sems, back):
    for i, (device, unused, slot) in enumerate(group):
        send(src, slots.at[slot], sems.at[back, i], sems.at[back + 1, slot], device).wait_send()


def start_ring(ring, me, src_of, slots, sems):
    for other, device, step in ring:
        send(src_of(other), slots.at[me], sems.at[0, step], sems.at[1, me], device).start()


def wait_ring(ring, src_of, slots, sems):
    for other, device, step in ring:
        send(src_of(other), slots.at[other], sems.at[0, step], sems.at[1, other], device).wait_recv()


def done_ring(ring, src_of, slots, sems):
    for other, device, step in ring:
        send(src_of(other), slots.at[other], sems.at[0, step], sems.at[1, other], device).wait_send()


def greet(barrier, device):
    pl.semaphore_signal(barrier, inc=1, device_id=device, device_id_type=MESH)


def oriented(strip, code, flip):
    turned = jnp.concatenate([strip[2:3], strip[1:2], strip[0:1]], axis=0)
    strip = jnp.where(code % 2 == 1, turned, strip)
    mirrored = dot(strip.reshape(RIM * CH, TC).astype(BF), flip).reshape(RIM, CH, TC)
    return jnp.where(code >= 2, mirrored, strip).astype(BF)


def step_kernel(
    dims,
    x_ref,
    prior_ref,
    cot_ref,
    kernel_ref,
    we_ref,
    wr_ref,
    wg_ref,
    wc_ref,
    sf,
    sc,
    next_out,
    prior_out,
    input_out,
    grads_out,
    natural,
    xw,
    strips,
    chosen,
    faces,
    pack,
    sides,
    col_strips,
    col_chosen,
    col_faces,
    spread,
    halo,
    xf,
    ef,
    shifted,
    taps,
    summed,
    back,
    prior,
    cot,
    total,
    edge_grad,
    ge,
    gr,
    gg,
    gc,
    grads,
    rim,
    edges,
    rim_sides,
    rim_faces,
    rim_chosen,
    rim_strips,
    row_sides,
    row_faces,
    row_chosen,
    row_strips,
    a1,
    a2_src,
    a2,
    a3_src,
    a3,
    a4_src,
    a4,
    a5_src,
    a5,
    near,
    group_sem,
    row_face_sem,
    col_face_sem,
    near_back,
    group_back,
    rim_face_sem,
    row_back_sem,
    s1,
    s2,
    s3,
    s4,
    s5,
):
    at = Place(dims)
    nf, nr, nc = dims
    part1 = PACK_ROWS // nf
    part2 = part1 // nc
    face_ring = at.ring("face")
    row_ring = at.ring("row")
    col_ring = at.ring("col")
    row_group = at.row_group()
    col_group = at.col_group()
    barrier = pltpu.get_barrier_semaphore()
    for ring in (face_ring, row_ring, col_ring):
        for unused, device, unused2 in ring:
            greet(barrier, device)
    corner = at.at(r=nr - 1 - at.r, c=nc - 1 - at.c)
    any_edge = jnp.logical_or(at.row_edge, at.col_edge)

    @pl.when(any_edge)
    def _():
        greet(barrier, corner)

    above = at.at(r=jnp.maximum(at.r - 1, 0))
    below = at.at(r=jnp.minimum(at.r + 1, nr - 1))
    before = at.at(c=jnp.maximum(at.c - 1, 0))
    after = at.at(c=jnp.minimum(at.c + 1, nc - 1))
    has_above = jnp.logical_not(at.top)
    has_below = jnp.logical_not(at.bottom)
    has_before = jnp.logical_not(at.left)
    has_after = jnp.logical_not(at.right)

    natural[...] = x_ref[...].astype(F32).reshape(CH * TR, TC)
    for y in range(TR):
        xw[RIM + y] = natural[pl.ds(y, CH, stride=TR), :].astype(BF)
    for row in range(PR):
        spread[:, row * TC : (row + 1) * TC] = spread_block(row)
    prior[...] = prior_ref[...].astype(F32).reshape(CH * TR, TC)
    cot[...] = cot_ref[...].astype(F32).reshape(CH * TR, TC)
    for ref in (ge, gr, gg, gc):
        ref[...] = jnp.zeros_like(ref)
    flip = flip_matrix()
    pl.semaphore_wait(barrier, nf + nr + nc - 3 + jnp.where(any_edge, 1, 0))

    def to_above():
        return send(xw.at[pl.ds(RIM, RIM)], xw.at[pl.ds(RIM + TR, RIM)], near.at[0, 0], near.at[1, 0], above)

    def to_below():
        return send(xw.at[pl.ds(TR, RIM)], xw.at[pl.ds(0, RIM)], near.at[0, 1], near.at[1, 1], below)

    def own_edge():
        return xw.at[pl.ds(jnp.where(at.top, RIM, TR), RIM)]

    @pl.when(at.row_edge)
    def _():
        start_group(row_group, own_edge(), strips, group_sem, 0)

    @pl.when(has_above)
    def _():
        to_above().start()

    @pl.when(has_below)
    def _():
        to_below().start()

    @pl.when(at.row_edge)
    def _():
        strips[at.row_kind * 2] = own_edge()[...]
        wait_group(row_group, own_edge(), strips, group_sem, 0)
        taker = partner_of(sf, at.row_kind, at.f, nf)
        code = sc[at.row_kind, taker]
        picked = strips[kind_of(at.row_kind, code) * 2 + code // 2]
        chosen[...] = picked
        start_ring(face_ring, at.f, lambda other: chosen, faces, row_face_sem)
        faces[at.f] = picked
        wait_ring(face_ring, lambda other: chosen, faces, row_face_sem)
        strip = oriented(faces[sf[at.row_kind, at.f]].astype(F32), sc[at.row_kind, at.f], flip)
        xw[pl.ds(jnp.where(at.top, 0, RIM + TR), RIM)] = strip

    @pl.when(has_below)
    def _():
        to_above().wait_recv()

    @pl.when(has_above)
    def _():
        to_below().wait_recv()

    flat = jnp.concatenate([xw[row] for row in range(PR)], axis=1)
    pack[...] = dot_nt(flat, spread[...]).astype(BF)

    def to_before():
        return send(pack, sides.at[1], near.at[0, 2], near.at[1, 2], before)

    def to_after():
        return send(pack, sides.at[0], near.at[0, 3], near.at[1, 3], after)

    @pl.when(at.col_edge)
    def _():
        start_group(col_group, pack, col_strips, group_sem, 2)

    @pl.when(has_before)
    def _():
        to_before().start()

    @pl.when(has_after)
    def _():
        to_after().start()

    xf[...] = xw[...].astype(F32)

    @pl.when(at.col_edge)
    def _():
        side = at.col_kind + 2
        col_strips[at.col_kind * 2] = pack[...]
        wait_group(col_group, pack, col_strips, group_sem, 2)
        code = sc[side, partner_of(sf, side, at.f, nf)]
        picked = col_strips[kind_of(at.col_kind, code) * 2 + code // 2]
        col_chosen[...] = picked
        start_ring(face_ring, at.f, lambda other: col_chosen, col_faces, col_face_sem)
        col_faces[at.f] = picked
        wait_ring(face_ring, lambda other: col_chosen, col_faces, col_face_sem)
        strip = col_faces[sf[side, at.f]]
        sides[at.col_kind] = dot(strip, turn_matrix(sc[side, at.f])).astype(BF)

    @pl.when(has_after)
    def _():
        to_before().wait_recv()

    @pl.when(has_before)
    def _():
        to_after().wait_recv()

    place = lax.broadcasted_iota(jnp.int32, (CH, TC), 1) % 8
    low = place < RIM
    halo[...] = jnp.where(low, sides[0].astype(F32), sides[1].astype(F32)).astype(BF)

    ends = dot(halo[...], spread[...])
    for row in range(PR):
        ef[row] = ends[:, row * TC : (row + 1) * TC]
    lane = lax.broadcasted_iota(jnp.int32, (PR, 8, TC), 2)
    lane2 = lax.broadcasted_iota(jnp.int32, (8, TC), 1)
    kernel_t = kernel_ref[...].T
    gc[:, 0 : KS * KS] = kernel_t

    def forward(g, carry):
        part = pl.ds(pl.multiple_of(g * 8, 8), 8)
        values = gc[part, :]
        sums = jnp.zeros((TR, 8, TC), F32)
        inside = xf[:, part, :]
        outside = ef[:, part, :]
        for b in range(KS):
            d = b - RIM
            rows = inside
            if d:
                wrapped = lane < d if d > 0 else lane >= TC + d
                rows = pltpu.roll(jnp.where(wrapped, outside, inside), (-d) % TC, 2)
            shifted[b, :, part, :] = rows
            for a in range(KS):
                tap = a * KS + b
                weight = jnp.broadcast_to(values[:, tap : tap + 1], (8, TC))
                taps[tap, part, :] = weight
                sums = sums + weight[None] * rows[a : a + TR]
        summed[:, part, :] = sums
        return carry

    lax.fori_loop(0, CH // 8, forward, 0)
    gc[...] = jnp.zeros_like(gc)

    we = we_ref[...]
    wr_t = wr_ref[...]
    wg = wg_ref[...]
    wc_t = wc_ref[...]
    we_t = we.T
    wr = wr_t.T
    wg_t = wg.T
    wc = wc_t.T

    def chunk(i, carry):
        r0 = i * 2

        def pair(load):
            return jnp.concatenate([load(r0), load(r0 + 1)], axis=1)

        s = pair(lambda y: summed[y])
        center = s - jnp.mean(s, axis=0, keepdims=True)
        scale = lax.rsqrt(jnp.mean(center * center, axis=0, keepdims=True) + 1e-06)
        unit = center * scale
        normed = unit.astype(BF)
        hidden = dot(we_t, normed)
        acts = []
        slopes = []
        for start in range(0, HID, 32):
            h = hidden[start : start + 32]
            cdf = 0.5 + 0.5 * lax.erf(h * math.sqrt(0.5))
            acts.append((h * cdf).astype(BF))
            slopes.append(cdf + h * (jnp.exp(-0.5 * h * h) * (1.0 / math.sqrt(2.0 * math.pi))))
        act = jnp.concatenate(acts, axis=0)
        slope = jnp.concatenate(slopes, axis=0)
        out = (pair(lambda y: xf[RIM + y]) + dot(wr_t, act)).astype(BF)
        earlier = pair(lambda y: prior[pl.ds(y, CH, stride=TR), :])
        joined = jnp.concatenate([out, earlier.astype(BF)], axis=0)
        gates = jax.nn.sigmoid(dot(wg_t, joined))
        update = gates[:CH]
        reset = gates[CH:]
        joined_reset = jnp.concatenate([out, (reset * earlier).astype(BF)], axis=0)
        proposal = jnp.tanh(dot(wc_t, joined_reset))
        result = (1.0 - update) * earlier + update * proposal
        g = pair(lambda y: cot[pl.ds(y, CH, stride=TR), :])
        d_cand = (g * update * (1.0 - proposal * proposal)).astype(BF)
        d_joined_reset = dot(wc, d_cand)
        d_reset = d_joined_reset[CH:]
        d_gates = jnp.concatenate(
            [
                g * (proposal - earlier) * (update * (1.0 - update)),
                d_reset * earlier * (reset * (1.0 - reset)),
            ],
            axis=0,
        ).astype(BF)
        d_joined = dot(wg, d_gates)
        d_out = (d_joined_reset[:CH] + d_joined[:CH]).astype(BF)
        d_prior = g * (1.0 - update) + d_reset * reset + d_joined[CH:]
        d_hidden = (dot(wr, d_out) * slope).astype(BF)
        d_normed = dot(we, d_hidden)
        ge[...] += dot_nt(normed, d_hidden)
        gr[...] += dot_nt(d_out, act)
        gg[...] += dot_nt(joined, d_gates)
        gc[...] += dot_nt(d_cand, joined_reset)
        d_summed = scale * (
            d_normed
            - jnp.mean(d_normed, axis=0, keepdims=True)
            - unit * jnp.mean(d_normed * unit, axis=0, keepdims=True)
        )
        d_center = d_out.astype(F32)
        for j in range(2):
            y = r0 + j
            cut = slice(j * TC, (j + 1) * TC)
            back[y] = d_summed[:, cut]
            total[RIM + y] = d_center[:, cut]
            next_out[y] = result[:, cut].astype(BF)
            prior_out[y] = d_prior[:, cut].astype(BF)
        return carry

    lax.fori_loop(0, TR // 2, chunk, 0)
    grads[0:64] = ge[:, :TC].astype(BF)
    grads[64:128] = ge[:, TC:].astype(BF)
    grads[128:192] = gr[:, :TC].astype(BF)
    grads[192:256] = gr[:, TC:].astype(BF)
    grads[256:384] = gg[...].astype(BF)
    grads[384:448] = gc[...].astype(BF)

    def piece1(other):
        return grads.at[pl.ds(pl.multiple_of(other * part1, part1), part1)]

    def start_shares(wanted):
        for other, device, step in face_ring:

            @pl.when((other == nf - 1) == wanted)
            def _(other=other, device=device, step=step):
                send(piece1(other), a1.at[at.f], s1.at[0, step], s1.at[1, at.f], device).start()

    start_shares(False)

    def backward_kernel(g, carry):
        part = pl.ds(pl.multiple_of(g * 8, 8), 8)
        rows = back[:, part, :]
        found = jnp.zeros((8, TC), F32)
        for b in range(KS):
            for a in range(KS):
                terms = jnp.sum(rows * shifted[b, a : a + TR, part, :], axis=0)
                found = jnp.where(lane2 == a * KS + b, jnp.sum(terms, axis=1, keepdims=True), found)
        gc[part, :] = found
        return carry

    lax.fori_loop(0, CH // 8, backward_kernel, 0)
    grads[448:512] = gc[...].astype(BF)
    start_shares(True)
    a1[at.f] = piece1(at.f)[...]

    def backward(g, carry):
        part = pl.ds(pl.multiple_of(g * 8, 8), 8)
        rows = back[:, part, :]
        inner = jnp.zeros((PR, 8, TC), F32)
        outer = jnp.zeros((PR, 8, TC), F32)
        for b in range(KS):
            d = b - RIM
            columns = [None] * PR
            for a in range(KS):
                product = taps[a * KS + b, part, :][None] * rows
                for y in range(TR):
                    columns[y + a] = product[y] if columns[y + a] is None else columns[y + a] + product[y]
            moved = jnp.stack(columns)
            if d == 0:
                inner = inner + moved
                continue
            moved = pltpu.roll(moved, d % TC, 2)
            wrapped = lane < d if d > 0 else lane >= TC + d
            inner = inner + jnp.where(wrapped, 0.0, moved)
            outer = outer + jnp.where(wrapped, moved, 0.0)
        total[0:RIM, part, :] = inner[0:RIM]
        total[RIM : RIM + TR, part, :] = total[RIM : RIM + TR, part, :] + inner[RIM : RIM + TR]
        total[RIM + TR :, part, :] = inner[RIM + TR :]
        edge_grad[:, part, :] = outer
        return carry

    lax.fori_loop(0, CH // 8, backward, 0)
    flat = jnp.concatenate([edge_grad[row] for row in range(PR)], axis=1).astype(BF)
    rim[...] = dot_nt(flat, spread[...]).astype(BF)

    def rim_before():
        return send(rim, rim_sides.at[1], near_back.at[0, 2], near_back.at[1, 2], before)

    def rim_after():
        return send(rim, rim_sides.at[0], near_back.at[0, 3], near_back.at[1, 3], after)

    @pl.when(at.col_edge)
    def _():
        start_ring(face_ring, at.f, lambda other: rim, rim_faces, rim_face_sem)

    @pl.when(has_before)
    def _():
        rim_before().start()

    @pl.when(has_after)
    def _():
        rim_after().start()

    wait_ring(face_ring, piece1, a1, s1)
    partial = a1[0].astype(F32)
    for other in range(1, nf):
        partial = partial + a1[other].astype(F32)
    a2_src[...] = partial

    def piece2(other):
        return a2_src.at[pl.ds(pl.multiple_of(other * part2, part2), part2)]

    start_ring(col_ring, at.c, piece2, a2, s2)
    a2[at.c] = piece2(at.c)[...]

    @pl.when(at.col_edge)
    def _():
        side = at.col_kind + 2
        rim_faces[at.f] = rim[...]
        wait_ring(face_ring, lambda other: rim, rim_faces, rim_face_sem)
        taker = partner_of(sf, side, at.f, nf)
        strip = rim_faces[taker].astype(F32)
        strip = jnp.where(low == at.left, strip, 0.0).astype(BF)
        turned = dot(strip, turn_matrix(sc[side, taker])).astype(BF)
        rim_chosen[...] = turned
        start_group(col_group, rim_chosen, rim_strips, group_back, 0)
        rim_strips[at.col_kind * 2] = turned

    wait_ring(col_ring, piece2, a2, s2)
    partial = a2[0]
    for other in range(1, nc):
        partial = partial + a2[other]
    a3_src[...] = partial
    start_ring(row_ring, at.r, lambda other: a3_src, a3, s3)
    a3[at.r] = partial

    def seam_total(slots, kind, first_side):
        gathered = None
        for side_bit in range(2):
            taker = partner_of(sf, first_side + side_bit, at.f, nf)
            code = sc[first_side + side_bit, taker]
            mine = kind_of(side_bit, code) == kind
            for mirror in range(2):
                use = jnp.logical_and(mine, code // 2 == mirror)
                term = jnp.where(use, slots[side_bit * 2 + mirror].astype(F32), 0.0)
                gathered = term if gathered is None else gathered + term
        return gathered

    @pl.when(at.col_edge)
    def _():
        wait_group(col_group, rim_chosen, rim_strips, group_back, 0)
        rim_sides[at.col_kind] = seam_total(rim_strips, at.col_kind, 2).astype(BF)

    @pl.when(has_after)
    def _():
        rim_before().wait_recv()

    @pl.when(has_before)
    def _():
        rim_after().wait_recv()

    returned = jnp.where(low, rim_sides[1].astype(F32), rim_sides[0].astype(F32)).astype(BF)
    ends = dot(returned, spread[...])
    for row in range(PR):
        total[row] = total[row] + ends[:, row * TC : (row + 1) * TC]
    edges[0] = total[0:RIM].astype(BF)
    edges[1] = total[RIM + TR : PR].astype(BF)

    def grad_above():
        return send(edges.at[0], row_sides.at[1], near_back.at[0, 0], near_back.at[1, 0], above)

    def grad_below():
        return send(edges.at[1], row_sides.at[0], near_back.at[0, 1], near_back.at[1, 1], below)

    def own_grad():
        return edges.at[at.row_kind]

    @pl.when(at.row_edge)
    def _():
        start_ring(face_ring, at.f, lambda other: own_grad(), row_faces, row_back_sem)

    @pl.when(has_above)
    def _():
        grad_above().start()

    @pl.when(has_below)
    def _():
        grad_below().start()

    wait_ring(row_ring, lambda other: a3_src, a3, s3)
    partial = a3[0]
    for other in range(1, nr):
        partial = partial + a3[other]
    a4_src[...] = partial
    start_ring(col_ring, at.c, lambda other: a4_src, a4, s4)
    a4[at.c] = partial

    @pl.when(at.row_edge)
    def _():
        row_faces[at.f] = own_grad()[...]
        wait_ring(face_ring, lambda other: own_grad(), row_faces, row_back_sem)
        taker = partner_of(sf, at.row_kind, at.f, nf)
        strip = oriented(row_faces[taker].astype(F32), sc[at.row_kind, taker], flip_matrix())
        row_chosen[...] = strip
        start_group(row_group, row_chosen, row_strips, group_back, 2)
        row_strips[at.row_kind * 2] = strip

    wait_ring(col_ring, lambda other: a4_src, a4, s4)
    full = jnp.concatenate([a4[other] for other in range(nc)], axis=0).astype(BF)
    a5_src[...] = full
    start_ring(face_ring, at.f, lambda other: a5_src, a5, s5)
    a5[at.f] = full

    @pl.when(has_below)
    def _():
        grad_above().wait_recv()
        total[TR : TR + RIM] = total[TR : TR + RIM] + row_sides[1].astype(F32)

    @pl.when(has_above)
    def _():
        grad_below().wait_recv()
        total[RIM : 2 * RIM] = total[RIM : 2 * RIM] + row_sides[0].astype(F32)

    @pl.when(at.row_edge)
    def _():
        wait_group(row_group, row_chosen, row_strips, group_back, 2)
        gathered = seam_total(row_strips, at.row_kind, 0)
        spot = pl.ds(jnp.where(at.top, RIM, TR), RIM)
        total[spot] = total[spot] + gathered

    input_out[...] = total[RIM : RIM + TR].astype(BF)
    wait_ring(face_ring, lambda other: a5_src, a5, s5)
    for other in range(nf):
        grads_out[other * part1 : (other + 1) * part1] = a5[other]

    @pl.when(has_above)
    def _():
        to_above().wait_send()
        grad_above().wait_send()

    @pl.when(has_below)
    def _():
        to_below().wait_send()
        grad_below().wait_send()

    @pl.when(has_before)
    def _():
        to_before().wait_send()
        rim_before().wait_send()

    @pl.when(has_after)
    def _():
        to_after().wait_send()
        rim_after().wait_send()

    @pl.when(at.row_edge)
    def _():
        done_group(row_group, own_edge(), strips, group_sem, 0)
        done_ring(face_ring, lambda other: chosen, faces, row_face_sem)
        done_ring(face_ring, lambda other: own_grad(), row_faces, row_back_sem)
        done_group(row_group, row_chosen, row_strips, group_back, 2)

    @pl.when(at.col_edge)
    def _():
        done_group(col_group, pack, col_strips, group_sem, 2)
        done_ring(face_ring, lambda other: col_chosen, col_faces, col_face_sem)
        done_ring(face_ring, lambda other: rim, rim_faces, rim_face_sem)
        done_group(col_group, rim_chosen, rim_strips, group_back, 0)

    done_ring(face_ring, piece1, a1, s1)
    done_ring(col_ring, piece2, a2, s2)
    done_ring(row_ring, lambda other: a3_src, a3, s3)
    done_ring(col_ring, lambda other: a4_src, a4, s4)
    done_ring(face_ring, lambda other: a5_src, a5, s5)


def finish_kernel(
    grad_scale,
    next_rows,
    prior_rows,
    input_rows,
    grads,
    next_out,
    input_out,
    prior_out,
    kernel_out,
    expand_out,
    reduce_out,
    gates_out,
    candidate_out,
    natural,
):
    for rows, out in ((next_rows, next_out), (input_rows, input_out), (prior_rows, prior_out)):
        for y in range(TR):
            natural[pl.ds(y, CH, stride=TR), :] = rows[y].astype(F32)
        out[...] = natural[...].reshape(CH, TR, TC).astype(BF)
    scaled = grads[...].astype(F32) * grad_scale
    expand_out[:, :TC] = scaled[0:64]
    expand_out[:, TC:] = scaled[64:128]
    reduce_out[:, :TC] = scaled[128:192]
    reduce_out[:, TC:] = scaled[192:256]
    gates_out[...] = scaled[256:384]
    candidate_out[...] = scaled[384:448]
    kernel_out[...] = scaled[448:512].T[: KS * KS]


def dma(*shape):
    return pltpu.SemaphoreType.DMA(shape)


def whole_step(dims, x, prior, cot, kernel_t, we, wr_t, wg, wc_t, sf, sc):
    nf, nr, nc = dims
    part1 = PACK_ROWS // nf
    part2 = part1 // nc
    wide = (PR, CH, TC)
    tile = (TR, CH, TC)
    strip = (RIM, CH, TC)
    flat = (CH * TR, TC)
    edge = (CH, TC)
    rows = jax.ShapeDtypeStruct(tile, BF)
    bf16_scratch = [
        wide,
        (4,) + strip,
        strip,
        (nf,) + strip,
        edge,
        (2,) + edge,
        (4,) + edge,
        edge,
        (nf,) + edge,
        (TC, PR * TC),
        edge,
    ]
    f32_scratch = [
        wide,
        wide,
        (KS,) + wide,
        (KS * KS, CH, TC),
        tile,
        tile,
        flat,
        flat,
        wide,
        wide,
        (CH, HID),
        (CH, HID),
        (2 * CH, 2 * CH),
        (CH, 2 * CH),
    ]
    back_scratch = [
        (PACK_ROWS, TC),
        edge,
        (2,) + strip,
        (2,) + edge,
        (nf,) + edge,
        edge,
        (4,) + edge,
        (2,) + strip,
        (nf,) + strip,
        strip,
        (4,) + strip,
        (nf, part1, TC),
    ]
    sum_scratch = [(part1, TC), (nc, part2, TC), (part2, TC), (nr, part2, TC), (part2, TC), (nc, part2, TC)]
    return pl.pallas_call(
        functools.partial(step_kernel, dims),
        out_shape=(rows, rows, rows, jax.ShapeDtypeStruct((PACK_ROWS, TC), BF)),
        in_specs=[VMEM] * 8 + [SMEM] * 2,
        out_specs=(VMEM,) * 4,
        scratch_shapes=[pltpu.VMEM(flat, F32)]
        + [pltpu.VMEM(shape, BF) for shape in bf16_scratch]
        + [pltpu.VMEM(shape, F32) for shape in f32_scratch]
        + [pltpu.VMEM(shape, BF) for shape in back_scratch]
        + [pltpu.VMEM(shape, F32) for shape in sum_scratch]
        + [pltpu.VMEM((part1, TC), BF), pltpu.VMEM((nf, part1, TC), BF)]
        + [dma(2, 4), dma(4, 4), dma(2, nf), dma(2, nf)]
        + [dma(2, 4), dma(4, 4), dma(2, nf), dma(2, nf)]
        + [dma(2, nf), dma(2, nc), dma(2, nr), dma(2, nc), dma(2, nf)],
        compiler_params=pltpu.CompilerParams(
            collective_id=0, has_side_effects=True, vmem_limit_bytes=LIMIT
        ),
        name="whole_step",
    )(x, prior, cot, kernel_t, we, wr_t, wg, wc_t, sf, sc)


def finish(grad_scale, next_rows, prior_rows, input_rows, grads):
    tile = jax.ShapeDtypeStruct((CH, TR, TC), BF)
    shapes = ((KS * KS, CH), (CH, HID), (CH, HID), (2 * CH, 2 * CH), (CH, 2 * CH))
    return pl.pallas_call(
        functools.partial(finish_kernel, grad_scale),
        out_shape=(tile,) * 3 + tuple(jax.ShapeDtypeStruct(shape, F32) for shape in shapes),
        in_specs=[VMEM] * 4,
        out_specs=(VMEM,) * 8,
        scratch_shapes=[pltpu.VMEM((CH * TR, TC), F32)],
        compiler_params=pltpu.CompilerParams(vmem_limit_bytes=LIMIT),
        name="finish",
    )(next_rows, prior_rows, input_rows, grads)


def body(dims, cell_total, block_in, hidden_state, state_cotangent, kernel, we, wr, wg, wc, sf, sc):
    rows = whole_step(
        dims, block_in[0], hidden_state[0], state_cotangent[0], kernel.T, we, wr.T, wg, wc.T, sf.T, sc.T
    )
    done = finish(1.0 / math.sqrt(cell_total), *rows)
    return (
        done[0][None],
        done[1][None],
        done[2][None],
        done[3].T,
        done[4],
        done[5].T,
        done[6],
        done[7].T,
    )


def solution(mesh):
    dims = tuple(mesh.shape[name] for name in AXES)
    cell_total = dims[0] * dims[1] * dims[2] * TR * TC
    tiles = P("face", None, "row", "col")
    return jax.shard_map(
        functools.partial(body, dims, cell_total),
        mesh=mesh,
        in_specs=(tiles,) * 3 + (P(),) * 7,
        out_specs=(tiles,) * 3 + (P(),) * 5,
        check_vma=False,
    )
```

```python
import functools
import math

import jax
import jax.numpy as jnp
from jax import lax
from jax.experimental import pallas as pl
from jax.experimental.pallas import tpu as pltpu
from jax.sharding import PartitionSpec as P

AXES = ("face", "row", "col")
CH = 64
HID = 256
KS = 7
RIM = 3
TR = 8
TC = 128
PR = TR + 2 * RIM
PACK_ROWS = 512
BF = jnp.bfloat16
F32 = jnp.float32
MESH = pl.DeviceIdType.MESH
VMEM = pl.BlockSpec(memory_space=pltpu.VMEM)
HBM = pl.BlockSpec(memory_space=pltpu.HBM)
LIMIT = 60 * 1024 * 1024


def spread_block(row):
    source = lax.broadcasted_iota(jnp.int32, (TC, TC), 0)
    lane = lax.broadcasted_iota(jnp.int32, (TC, TC), 1)
    place = jnp.where(lane >= TC - RIM, lane - (TC - RIM), jnp.where(lane < RIM, lane + RIM, -TC * 8))
    return jnp.where(source == row * 8 + place, 1.0, 0.0).astype(BF)


def turn_matrix(code):
    source = lax.broadcasted_iota(jnp.int32, (TC, TC), 0)
    lane = lax.broadcasted_iota(jnp.int32, (TC, TC), 1)
    row = lane // 8
    place = lane % 8
    from_row = jnp.where(code >= 2, PR - 1 - row, row)
    from_place = jnp.where(code % 2 == 1, 5 - place, place)
    used = jnp.logical_and(place < 2 * RIM, row < PR)
    return jnp.where(jnp.where(used, from_row * 8 + from_place, -1) == source, 1.0, 0.0).astype(BF)


def flip_matrix():
    source = lax.broadcasted_iota(jnp.int32, (TC, TC), 0)
    lane = lax.broadcasted_iota(jnp.int32, (TC, TC), 1)
    return jnp.where(source == TC - 1 - lane, 1.0, 0.0).astype(BF)


def dot(a, b):
    return jnp.dot(a, b, preferred_element_type=F32)


def dot_nt(a, b):
    return lax.dot_general(a, b, (((1,), (1,)), ((), ())), preferred_element_type=F32)


def send(src, dst, send_sem, recv_sem, device):
    return pltpu.make_async_remote_copy(
        src_ref=src,
        dst_ref=dst,
        send_sem=send_sem,
        recv_sem=recv_sem,
        device_id=device,
        device_id_type=MESH,
    )


def partner_of(seam_face, side, face, count):
    found = jnp.int32(0)
    for other in range(count):
        found = jnp.where(seam_face[side, other] == face, other, found)
    return found


def kind_of(side_bit, code):
    odd = lax.rem(code, 2)
    return jnp.where(side_bit == 0, 1 - odd, odd)


def corner_of(sf, sc, face, v, h):
    beside = sf[h + 2, face]
    code = sc[h + 2, face]
    reverse = code // 2
    v_there = (v + reverse) % 2
    owner = sf[v_there, beside]
    code_there = sc[v_there, beside]
    reverse_there = code_there // 2
    block = kind_of(v_there, code_there) * 2 + (kind_of(h, code) + reverse_there) % 2
    return owner, block, (code_there + reverse) % 2, (code + reverse_there) % 2


def corner_lanes(lane, v, h, block, row_turn, col_turn):
    i = lane // 8 - jnp.where(v == 0, 0, RIM + TR)
    j = lane % 8 - jnp.where(h == 0, 0, RIM)
    inside = jnp.logical_and(
        jnp.logical_and(i >= 0, i < RIM), jnp.logical_and(j >= 0, j < RIM)
    )
    i = jnp.where(row_turn == 1, RIM - 1 - i, i)
    j = jnp.where(col_turn == 1, RIM - 1 - j, j)
    return jnp.where(inside, block * 32 + i * 8 + j, -1)


def one_hot(hit):
    return jnp.where(hit, 1.0, 0.0).astype(BF)


def block_lanes(lane, block, i):
    mine = jnp.logical_and(lane // 8 == block * 4 + i, lane % 8 < RIM)
    return jnp.where(mine, lane % 8 + jnp.where(block % 2 == 0, 0, TC - RIM), -1)


class Place:
    def __init__(self, dims):
        self.nf, self.nr, self.nc = dims
        self.f = lax.axis_index("face")
        self.r = lax.axis_index("row")
        self.c = lax.axis_index("col")
        self.top = self.r == 0
        self.bottom = self.r == self.nr - 1
        self.left = self.c == 0
        self.right = self.c == self.nc - 1
        self.row_edge = jnp.logical_or(self.top, self.bottom)
        self.col_edge = jnp.logical_or(self.left, self.right)
        self.row_kind = jnp.where(self.top, 0, 1)
        self.col_kind = jnp.where(self.left, 0, 1)

    def at(self, f=None, r=None, c=None):
        return (
            self.f if f is None else f,
            self.r if r is None else r,
            self.c if c is None else c,
        )

    def row_group(self):
        other_r = self.nr - 1 - self.r
        other_c = self.nc - 1 - self.c
        return [
            (self.at(c=other_c), self.row_kind * 2 + 1, self.row_kind * 2 + 1),
            (self.at(r=other_r), self.row_kind * 2, (1 - self.row_kind) * 2),
            (self.at(r=other_r, c=other_c), self.row_kind * 2 + 1, (1 - self.row_kind) * 2 + 1),
        ]

    def col_group(self):
        other_r = self.nr - 1 - self.r
        other_c = self.nc - 1 - self.c
        return [
            (self.at(r=other_r), self.col_kind * 2 + 1, self.col_kind * 2 + 1),
            (self.at(c=other_c), self.col_kind * 2, (1 - self.col_kind) * 2),
            (self.at(r=other_r, c=other_c), self.col_kind * 2 + 1, (1 - self.col_kind) * 2 + 1),
        ]

    def ring(self, axis):
        index, count = {"face": (self.f, self.nf), "row": (self.r, self.nr), "col": (self.c, self.nc)}[axis]
        out = []
        for step in range(1, count):
            other = lax.rem(index + step, count)
            out.append((other, self.at(**{axis[0]: other}), step))
        return out


def start_group(group, src, slots, sems, back):
    for i, (device, slot, unused) in enumerate(group):
        send(src, slots.at[slot], sems.at[back, i], sems.at[back + 1, slot], device).start()


def wait_group(group, src, slots, sems, back):
    for i, (device, unused, slot) in enumerate(group):
        send(src, slots.at[slot], sems.at[back, i], sems.at[back + 1, slot], device).wait_recv()


def done_group(group, src, slots, sems, back):
    for i, (device, unused, slot) in enumerate(group):
        send(src, slots.at[slot], sems.at[back, i], sems.at[back + 1, slot], device).wait_send()


def start_ring(ring, me, src_of, slots, sems):
    for other, device, step in ring:
        send(src_of(other), slots.at[me], sems.at[0, step], sems.at[1, me], device).start()


def wait_ring(ring, src_of, slots, sems):
    for other, device, step in ring:
        send(src_of(other), slots.at[other], sems.at[0, step], sems.at[1, other], device).wait_recv()


def done_ring(ring, src_of, slots, sems):
    for other, device, step in ring:
        send(src_of(other), slots.at[other], sems.at[0, step], sems.at[1, other], device).wait_send()


def greet(barrier, device):
    pl.semaphore_signal(barrier, inc=1, device_id=device, device_id_type=MESH)


def oriented(strip, code, flip):
    turned = jnp.concatenate([strip[2:3], strip[1:2], strip[0:1]], axis=0)
    strip = jnp.where(code % 2 == 1, turned, strip)
    mirrored = dot(strip.reshape(RIM * CH, TC).astype(BF), flip).reshape(RIM, CH, TC)
    return jnp.where(code >= 2, mirrored, strip).astype(BF)


def step_kernel(
    dims,
    x_in,
    prior_in,
    cot_in,
    kernel_in,
    we_in,
    wr_in,
    wg_in,
    wc_in,
    sf_in,
    sc_in,
    next_out,
    prior_out,
    input_out,
    grads_out,
    x_ref,
    prior_ref,
    cot_ref,
    kernel_ref,
    we_ref,
    wr_ref,
    wg_ref,
    wc_ref,
    sf,
    sc,
    in_sem,
    sides_late,
    corner_pack,
    corner_faces,
    corner_out,
    corner_strips,
    corner_face_sem,
    corner_group_sem,
    pack_late,
    natural,
    xw,
    strips,
    chosen,
    faces,
    pack,
    sides,
    col_strips,
    col_chosen,
    col_faces,
    spread,
    halo,
    xf,
    ef,
    shifted,
    taps,
    summed,
    back,
    prior,
    cot,
    total,
    edge_grad,
    ge,
    gr,
    gg,
    gc,
    grads,
    rim,
    edges,
    rim_sides,
    rim_faces,
    rim_chosen,
    rim_strips,
    row_sides,
    row_faces,
    row_chosen,
    row_strips,
    a1,
    a2_src,
    a2,
    a3_src,
    a3,
    a4_src,
    a4,
    a5_src,
    a5,
    near,
    near_late,
    group_sem,
    row_face_sem,
    col_face_sem,
    near_back,
    group_back,
    rim_face_sem,
    row_back_sem,
    s1,
    s2,
    s3,
    s4,
    s5,
):
    held = (x_ref, prior_ref, cot_ref, kernel_ref, we_ref, wr_ref, wg_ref, wc_ref, sf, sc)
    given = (x_in, prior_in, cot_in, kernel_in, we_in, wr_in, wg_in, wc_in, sf_in, sc_in)
    loads = [
        pltpu.make_async_copy(source, target, in_sem.at[i])
        for i, (source, target) in enumerate(zip(given, held))
    ]
    for load in loads:
        load.start()
    for ref in (sides, sides_late, rim_sides):
        ref[...] = jnp.zeros_like(ref)
    at = Place(dims)
    nf, nr, nc = dims
    part1 = PACK_ROWS // nf
    part2 = part1 // nc
    face_ring = at.ring("face")
    row_ring = at.ring("row")
    col_ring = at.ring("col")
    row_group = at.row_group()
    col_group = at.col_group()
    barrier = pltpu.get_barrier_semaphore()
    for ring in (face_ring, row_ring, col_ring):
        for unused, device, unused2 in ring:
            greet(barrier, device)
    corner = at.at(r=nr - 1 - at.r, c=nc - 1 - at.c)
    any_edge = jnp.logical_or(at.row_edge, at.col_edge)

    @pl.when(any_edge)
    def _():
        greet(barrier, corner)

    above = at.at(r=jnp.maximum(at.r - 1, 0))
    below = at.at(r=jnp.minimum(at.r + 1, nr - 1))
    before = at.at(c=jnp.maximum(at.c - 1, 0))
    after = at.at(c=jnp.minimum(at.c + 1, nc - 1))
    has_above = jnp.logical_not(at.top)
    has_below = jnp.logical_not(at.bottom)
    has_before = jnp.logical_not(at.left)
    has_after = jnp.logical_not(at.right)

    for row in range(PR):
        spread[:, row * TC : (row + 1) * TC] = spread_block(row)
    for ref in (ge, gr, gg, gc):
        ref[...] = jnp.zeros_like(ref)
    flip = flip_matrix()
    edge_rows = jnp.zeros((RIM, CH, TC), BF)

    @pl.when(at.top)
    def _():
        xw[0:RIM] = edge_rows

    @pl.when(at.bottom)
    def _():
        xw[RIM + TR : PR] = edge_rows

    for load in loads:
        load.wait()
    natural[...] = x_ref[...].astype(F32).reshape(CH * TR, TC)
    for y in range(TR):
        xw[RIM + y] = natural[pl.ds(y, CH, stride=TR), :].astype(BF)
    prior[...] = prior_ref[...].astype(F32).reshape(CH * TR, TC)
    cot[...] = cot_ref[...].astype(F32).reshape(CH * TR, TC)
    pl.semaphore_wait(barrier, nf + nr + nc - 3 + jnp.where(any_edge, 1, 0))

    def to_above():
        return send(xw.at[pl.ds(RIM, RIM)], xw.at[pl.ds(RIM + TR, RIM)], near.at[0, 0], near.at[1, 0], above)

    def to_below():
        return send(xw.at[pl.ds(TR, RIM)], xw.at[pl.ds(0, RIM)], near.at[0, 1], near.at[1, 1], below)

    def own_edge():
        return xw.at[pl.ds(jnp.where(at.top, RIM, TR), RIM)]

    @pl.when(at.row_edge)
    def _():
        start_group(row_group, own_edge(), strips, group_sem, 0)

    @pl.when(has_above)
    def _():
        to_above().start()

    @pl.when(has_below)
    def _():
        to_below().start()

    is_corner = jnp.logical_and(at.row_edge, at.col_edge)

    @pl.when(has_below)
    def _():
        to_above().wait_recv()

    @pl.when(has_above)
    def _():
        to_below().wait_recv()

    flat = jnp.concatenate([xw[row] for row in range(PR)], axis=1)
    pack[...] = dot_nt(flat, spread[...]).astype(BF)

    def to_before():
        return send(pack, sides.at[1], near.at[0, 2], near.at[1, 2], before)

    def to_after():
        return send(pack, sides.at[0], near.at[0, 3], near.at[1, 3], after)

    @pl.when(at.col_edge)
    def _():
        start_group(col_group, pack, col_strips, group_sem, 2)

    @pl.when(has_before)
    def _():
        to_before().start()

    @pl.when(has_after)
    def _():
        to_after().start()

    @pl.when(at.row_edge)
    def _():
        strips[at.row_kind * 2] = own_edge()[...]
        wait_group(row_group, own_edge(), strips, group_sem, 0)
        taker = partner_of(sf, at.row_kind, at.f, nf)
        code = sc[at.row_kind, taker]
        picked = strips[kind_of(at.row_kind, code) * 2 + code // 2]
        chosen[...] = picked
        start_ring(face_ring, at.f, lambda other: chosen, faces, row_face_sem)
        faces[at.f] = picked

    @pl.when(is_corner)
    def _():
        source = lax.broadcasted_iota(jnp.int32, (TC, TC), 0)
        lanes = lax.broadcasted_iota(jnp.int32, (TC, TC), 1)
        blocks = jnp.zeros((CH, TC), F32)
        for slot in range(4):
            block = (slot // 2) * 2 + (at.col_kind + slot) % 2
            for i in range(RIM):
                blocks = blocks + dot(strips[slot, i], one_hot(block_lanes(lanes, block, i) == source))
        corner_pack[...] = blocks.astype(BF)
        start_ring(face_ring, at.f, lambda other: corner_pack, corner_faces, corner_face_sem)
        corner_faces[at.f] = blocks.astype(BF)

    @pl.when(at.col_edge)
    def _():
        side = at.col_kind + 2
        col_strips[at.col_kind * 2] = pack[...]
        wait_group(col_group, pack, col_strips, group_sem, 2)
        code = sc[side, partner_of(sf, side, at.f, nf)]
        picked = col_strips[kind_of(at.col_kind, code) * 2 + code // 2]
        col_chosen[...] = picked
        start_ring(face_ring, at.f, lambda other: col_chosen, col_faces, col_face_sem)
        col_faces[at.f] = picked

    def late_before():
        return send(pack_late, sides_late.at[1], near_late.at[0, 0], near_late.at[1, 0], before)

    def late_after():
        return send(pack_late, sides_late.at[0], near_late.at[0, 1], near_late.at[1, 1], after)

    @pl.when(at.row_edge)
    def _():
        wait_ring(face_ring, lambda other: chosen, faces, row_face_sem)
        strip = oriented(faces[sf[at.row_kind, at.f]].astype(F32), sc[at.row_kind, at.f], flip)
        xw[pl.ds(jnp.where(at.top, 0, RIM + TR), RIM)] = strip
        late = jnp.zeros((CH, TC), F32)
        source = lax.broadcasted_iota(jnp.int32, (TC, TC), 0)
        lanes = lax.broadcasted_iota(jnp.int32, (TC, TC), 1)
        first = jnp.where(at.top, 0, RIM + TR)
        for i in range(RIM):
            wanted = jnp.where(lanes % 8 < RIM, lanes % 8 + TC - RIM, lanes % 8 - RIM)
            wanted = jnp.where(
                jnp.logical_and(lanes // 8 == first + i, lanes % 8 < 2 * RIM), wanted, -1
            )
            late = late + dot(strip[i], one_hot(wanted == source))
        pack_late[...] = late.astype(BF)

        @pl.when(has_before)
        def _():
            late_before().start()

        @pl.when(has_after)
        def _():
            late_after().start()

    xf[...] = xw[...].astype(F32)

    @pl.when(at.col_edge)
    def _():
        side = at.col_kind + 2
        wait_ring(face_ring, lambda other: col_chosen, col_faces, col_face_sem)
        strip = col_faces[sf[side, at.f]]
        sides[at.col_kind] = dot(strip, turn_matrix(sc[side, at.f])).astype(BF)

    @pl.when(is_corner)
    def _():
        wait_ring(face_ring, lambda other: corner_pack, corner_faces, corner_face_sem)
        source = lax.broadcasted_iota(jnp.int32, (TC, TC), 0)
        lanes = lax.broadcasted_iota(jnp.int32, (TC, TC), 1)
        owner, block, row_turn, col_turn = corner_of(sf, sc, at.f, at.row_kind, at.col_kind)
        pick = one_hot(corner_lanes(lanes, at.row_kind, at.col_kind, block, row_turn, col_turn) == source)
        sides_late[at.col_kind] = dot(corner_faces[owner], pick).astype(BF)

    @pl.when(has_after)
    def _():
        to_before().wait_recv()

    @pl.when(has_before)
    def _():
        to_after().wait_recv()

    @pl.when(at.row_edge)
    def _():
        @pl.when(has_after)
        def _():
            late_before().wait_recv()

        @pl.when(has_before)
        def _():
            late_after().wait_recv()

    place = lax.broadcasted_iota(jnp.int32, (CH, TC), 1) % 8
    low = place < RIM
    halo[...] = (
        jnp.where(low, sides[0].astype(F32), sides[1].astype(F32))
        + jnp.where(low, sides_late[0].astype(F32), sides_late[1].astype(F32))
    ).astype(BF)

    ends = dot(halo[...], spread[...])
    for row in range(PR):
        ef[row] = ends[:, row * TC : (row + 1) * TC]
    lane = lax.broadcasted_iota(jnp.int32, (PR, 8, TC), 2)
    lane2 = lax.broadcasted_iota(jnp.int32, (8, TC), 1)
    kernel_t = kernel_ref[...].T
    gc[:, 0 : KS * KS] = kernel_t

    def forward(g, carry):
        part = pl.ds(pl.multiple_of(g * 8, 8), 8)
        values = gc[part, :]
        sums = jnp.zeros((TR, 8, TC), F32)
        inside = xf[:, part, :]
        outside = ef[:, part, :]
        for b in range(KS):
            d = b - RIM
            rows = inside
            if d:
                wrapped = lane < d if d > 0 else lane >= TC + d
                rows = pltpu.roll(jnp.where(wrapped, outside, inside), (-d) % TC, 2)
            shifted[b, :, part, :] = rows
            for a in range(KS):
                tap = a * KS + b
                weight = jnp.broadcast_to(values[:, tap : tap + 1], (8, TC))
                taps[tap, part, :] = weight
                sums = sums + weight[None] * rows[a : a + TR]
        summed[:, part, :] = sums
        return carry

    lax.fori_loop(0, CH // 8, forward, 0)
    gc[...] = jnp.zeros_like(gc)

    we = we_ref[...]
    wr_t = wr_ref[...]
    wg = wg_ref[...]
    wc_t = wc_ref[...]
    we_t = we.T
    wr = wr_t.T
    wg_t = wg.T
    wc = wc_t.T

    def chunk(i, carry):
        r0 = i * 2

        def pair(load):
            return jnp.concatenate([load(r0), load(r0 + 1)], axis=1)

        s = pair(lambda y: summed[y])
        center = s - jnp.mean(s, axis=0, keepdims=True)
        scale = lax.rsqrt(jnp.mean(center * center, axis=0, keepdims=True) + 1e-06)
        unit = center * scale
        normed = unit.astype(BF)
        hidden = dot(we_t, normed)
        acts = []
        slopes = []
        for start in range(0, HID, 32):
            h = hidden[start : start + 32]
            cdf = 0.5 + 0.5 * lax.erf(h * math.sqrt(0.5))
            acts.append((h * cdf).astype(BF))
            slopes.append(cdf + h * (jnp.exp(-0.5 * h * h) * (1.0 / math.sqrt(2.0 * math.pi))))
        act = jnp.concatenate(acts, axis=0)
        slope = jnp.concatenate(slopes, axis=0)
        out = (pair(lambda y: xf[RIM + y]) + dot(wr_t, act)).astype(BF)
        earlier = pair(lambda y: prior[pl.ds(y, CH, stride=TR), :])
        joined = jnp.concatenate([out, earlier.astype(BF)], axis=0)
        gates = jax.nn.sigmoid(dot(wg_t, joined))
        update = gates[:CH]
        reset = gates[CH:]
        joined_reset = jnp.concatenate([out, (reset * earlier).astype(BF)], axis=0)
        proposal = jnp.tanh(dot(wc_t, joined_reset))
        result = (1.0 - update) * earlier + update * proposal
        g = pair(lambda y: cot[pl.ds(y, CH, stride=TR), :])
        d_cand = (g * update * (1.0 - proposal * proposal)).astype(BF)
        d_joined_reset = dot(wc, d_cand)
        d_reset = d_joined_reset[CH:]
        d_gates = jnp.concatenate(
            [
                g * (proposal - earlier) * (update * (1.0 - update)),
                d_reset * earlier * (reset * (1.0 - reset)),
            ],
            axis=0,
        ).astype(BF)
        d_joined = dot(wg, d_gates)
        d_out = (d_joined_reset[:CH] + d_joined[:CH]).astype(BF)
        d_prior = g * (1.0 - update) + d_reset * reset + d_joined[CH:]
        d_hidden = (dot(wr, d_out) * slope).astype(BF)
        d_normed = dot(we, d_hidden)
        ge[...] += dot_nt(normed, d_hidden)
        gr[...] += dot_nt(d_out, act)
        gg[...] += dot_nt(joined, d_gates)
        gc[...] += dot_nt(d_cand, joined_reset)
        d_summed = scale * (
            d_normed
            - jnp.mean(d_normed, axis=0, keepdims=True)
            - unit * jnp.mean(d_normed * unit, axis=0, keepdims=True)
        )
        d_center = d_out.astype(F32)
        for j in range(2):
            y = r0 + j
            cut = slice(j * TC, (j + 1) * TC)
            back[y] = d_summed[:, cut]
            total[RIM + y] = d_center[:, cut]
            next_out[y] = result[:, cut].astype(BF)
            prior_out[y] = d_prior[:, cut].astype(BF)
        return carry

    lax.fori_loop(0, TR // 2, chunk, 0)
    grads[0:64] = ge[:, :TC].astype(BF)
    grads[64:128] = ge[:, TC:].astype(BF)
    grads[128:192] = gr[:, :TC].astype(BF)
    grads[192:256] = gr[:, TC:].astype(BF)
    grads[256:384] = gg[...].astype(BF)
    grads[384:448] = gc[...].astype(BF)

    def piece1(other):
        return grads.at[pl.ds(pl.multiple_of(other * part1, part1), part1)]

    def start_shares(wanted):
        for other, device, step in face_ring:

            @pl.when((other == nf - 1) == wanted)
            def _(other=other, device=device, step=step):
                send(piece1(other), a1.at[at.f], s1.at[0, step], s1.at[1, at.f], device).start()

    start_shares(False)

    def backward_kernel(g, carry):
        part = pl.ds(pl.multiple_of(g * 8, 8), 8)
        rows = back[:, part, :]
        found = jnp.zeros((8, TC), F32)
        for b in range(KS):
            for a in range(KS):
                terms = jnp.sum(rows * shifted[b, a : a + TR, part, :], axis=0)
                found = jnp.where(lane2 == a * KS + b, jnp.sum(terms, axis=1, keepdims=True), found)
        gc[part, :] = found
        return carry

    lax.fori_loop(0, CH // 8, backward_kernel, 0)
    grads[448:512] = gc[...].astype(BF)
    start_shares(True)
    a1[at.f] = piece1(at.f)[...]

    def backward(g, carry):
        part = pl.ds(pl.multiple_of(g * 8, 8), 8)
        rows = back[:, part, :]
        inner = jnp.zeros((PR, 8, TC), F32)
        outer = jnp.zeros((PR, 8, TC), F32)
        for b in range(KS):
            d = b - RIM
            columns = [None] * PR
            for a in range(KS):
                product = taps[a * KS + b, part, :][None] * rows
                for y in range(TR):
                    columns[y + a] = product[y] if columns[y + a] is None else columns[y + a] + product[y]
            moved = jnp.stack(columns)
            if d == 0:
                inner = inner + moved
                continue
            moved = pltpu.roll(moved, d % TC, 2)
            wrapped = lane < d if d > 0 else lane >= TC + d
            inner = inner + jnp.where(wrapped, 0.0, moved)
            outer = outer + jnp.where(wrapped, moved, 0.0)
        total[0:RIM, part, :] = inner[0:RIM]
        total[RIM : RIM + TR, part, :] = total[RIM : RIM + TR, part, :] + inner[RIM : RIM + TR]
        total[RIM + TR :, part, :] = inner[RIM + TR :]
        edge_grad[:, part, :] = outer
        return carry

    lax.fori_loop(0, CH // 8, backward, 0)
    flat = jnp.concatenate([edge_grad[row] for row in range(PR)], axis=1).astype(BF)
    rim[...] = dot_nt(flat, spread[...]).astype(BF)

    def rim_before():
        return send(rim, rim_sides.at[1], near_back.at[0, 2], near_back.at[1, 2], before)

    def rim_after():
        return send(rim, rim_sides.at[0], near_back.at[0, 3], near_back.at[1, 3], after)

    @pl.when(at.col_edge)
    def _():
        start_ring(face_ring, at.f, lambda other: rim, rim_faces, rim_face_sem)

    @pl.when(has_before)
    def _():
        rim_before().start()

    @pl.when(has_after)
    def _():
        rim_after().start()

    wait_ring(face_ring, piece1, a1, s1)
    partial = a1[0].astype(F32)
    for other in range(1, nf):
        partial = partial + a1[other].astype(F32)
    a2_src[...] = partial

    def piece2(other):
        return a2_src.at[pl.ds(pl.multiple_of(other * part2, part2), part2)]

    start_ring(col_ring, at.c, piece2, a2, s2)
    a2[at.c] = piece2(at.c)[...]

    @pl.when(has_after)
    def _():
        rim_before().wait_recv()

    @pl.when(has_before)
    def _():
        rim_after().wait_recv()

    def add_columns(packed):
        ends = dot(packed, spread[...])
        for row in range(PR):
            total[row] = total[row] + ends[:, row * TC : (row + 1) * TC]

    add_columns(jnp.where(low, rim_sides[1].astype(F32), rim_sides[0].astype(F32)).astype(BF))

    def own_grad():
        return edges.at[at.row_kind]

    @pl.when(at.row_edge)
    def _():
        edges[at.row_kind] = total[pl.ds(jnp.where(at.top, 0, RIM + TR), RIM)].astype(BF)
        start_ring(face_ring, at.f, lambda other: own_grad(), row_faces, row_back_sem)

    @pl.when(at.col_edge)
    def _():
        side = at.col_kind + 2
        rim_faces[at.f] = rim[...]
        wait_ring(face_ring, lambda other: rim, rim_faces, rim_face_sem)
        taker = partner_of(sf, side, at.f, nf)
        strip = rim_faces[taker].astype(F32)
        row = lax.broadcasted_iota(jnp.int32, (CH, TC), 1) // 8
        beyond = jnp.logical_or(
            jnp.logical_and(at.top, row < RIM), jnp.logical_and(at.bottom, row >= RIM + TR)
        )
        keep = jnp.logical_and(low == at.left, jnp.logical_not(beyond))
        strip = jnp.where(keep, strip, 0.0).astype(BF)
        turned = dot(strip, turn_matrix(sc[side, taker])).astype(BF)
        rim_chosen[...] = turned
        start_group(col_group, rim_chosen, rim_strips, group_back, 0)
        rim_strips[at.col_kind * 2] = turned

    @pl.when(is_corner)
    def _():
        source = lax.broadcasted_iota(jnp.int32, (TC, TC), 0)
        lanes = lax.broadcasted_iota(jnp.int32, (TC, TC), 1)
        blocks = jnp.zeros((CH, TC), F32)
        for other in range(nf):
            owner, block, row_turn, col_turn = corner_of(sf, sc, other, at.row_kind, at.col_kind)
            wanted = corner_lanes(source, at.row_kind, at.col_kind, block, row_turn, col_turn)
            wanted = jnp.where(owner == at.f, wanted, -1)
            blocks = blocks + dot(rim_faces[other], one_hot(wanted == lanes))
        corner_out[...] = blocks.astype(BF)
        start_group(row_group, corner_out, corner_strips, corner_group_sem, 0)
        corner_strips[at.row_kind * 2] = blocks.astype(BF)

    wait_ring(col_ring, piece2, a2, s2)
    partial = a2[0]
    for other in range(1, nc):
        partial = partial + a2[other]
    a3_src[...] = partial
    start_ring(row_ring, at.r, lambda other: a3_src, a3, s3)
    a3[at.r] = partial

    def seam_total(slots, kind, first_side):
        gathered = None
        for side_bit in range(2):
            taker = partner_of(sf, first_side + side_bit, at.f, nf)
            code = sc[first_side + side_bit, taker]
            mine = kind_of(side_bit, code) == kind
            for mirror in range(2):
                use = jnp.logical_and(mine, code // 2 == mirror)
                term = jnp.where(use, slots[side_bit * 2 + mirror].astype(F32), 0.0)
                gathered = term if gathered is None else gathered + term
        return gathered

    @pl.when(at.col_edge)
    def _():
        wait_group(col_group, rim_chosen, rim_strips, group_back, 0)
        back_rim = seam_total(rim_strips, at.col_kind, 2)
        add_columns(jnp.where(low == at.left, 0.0, back_rim).astype(BF))

    def grad_above():
        return send(edges.at[0], row_sides.at[1], near_back.at[0, 0], near_back.at[1, 0], above)

    def grad_below():
        return send(edges.at[1], row_sides.at[0], near_back.at[0, 1], near_back.at[1, 1], below)

    @pl.when(has_above)
    def _():
        edges[0] = total[0:RIM].astype(BF)
        grad_above().start()

    @pl.when(has_below)
    def _():
        edges[1] = total[RIM + TR : PR].astype(BF)
        grad_below().start()

    wait_ring(row_ring, lambda other: a3_src, a3, s3)
    partial = a3[0]
    for other in range(1, nr):
        partial = partial + a3[other]
    a4_src[...] = partial
    start_ring(col_ring, at.c, lambda other: a4_src, a4, s4)
    a4[at.c] = partial

    @pl.when(at.row_edge)
    def _():
        row_faces[at.f] = own_grad()[...]
        wait_ring(face_ring, lambda other: own_grad(), row_faces, row_back_sem)
        taker = partner_of(sf, at.row_kind, at.f, nf)
        strip = oriented(row_faces[taker].astype(F32), sc[at.row_kind, taker], flip_matrix())
        row_chosen[...] = strip
        start_group(row_group, row_chosen, row_strips, group_back, 2)
        row_strips[at.row_kind * 2] = strip

    wait_ring(col_ring, lambda other: a4_src, a4, s4)
    full = jnp.concatenate([a4[other] for other in range(nc)], axis=0).astype(BF)
    a5_src[...] = full
    start_ring(face_ring, at.f, lambda other: a5_src, a5, s5)
    a5[at.f] = full

    @pl.when(has_below)
    def _():
        grad_above().wait_recv()
        total[TR : TR + RIM] = total[TR : TR + RIM] + row_sides[1].astype(F32)

    @pl.when(has_above)
    def _():
        grad_below().wait_recv()
        total[RIM : 2 * RIM] = total[RIM : 2 * RIM] + row_sides[0].astype(F32)

    @pl.when(at.row_edge)
    def _():
        wait_group(row_group, row_chosen, row_strips, group_back, 2)
        gathered = seam_total(row_strips, at.row_kind, 0)
        spot = pl.ds(jnp.where(at.top, RIM, TR), RIM)
        total[spot] = total[spot] + gathered

    @pl.when(is_corner)
    def _():
        wait_group(row_group, corner_out, corner_strips, corner_group_sem, 0)
        blocks = corner_strips[0].astype(F32)
        for slot in range(1, 4):
            blocks = blocks + corner_strips[slot].astype(F32)
        source = lax.broadcasted_iota(jnp.int32, (TC, TC), 0)
        lanes = lax.broadcasted_iota(jnp.int32, (TC, TC), 1)
        first = jnp.where(at.top, RIM, TR)
        for i in range(RIM):
            wanted = block_lanes(source, at.row_kind * 2 + at.col_kind, i)
            total[first + i] = total[first + i] + dot(blocks.astype(BF), one_hot(wanted == lanes))

    input_out[...] = total[RIM : RIM + TR].astype(BF)
    wait_ring(face_ring, lambda other: a5_src, a5, s5)
    for other in range(nf):
        grads_out[other * part1 : (other + 1) * part1] = a5[other]

    @pl.when(has_above)
    def _():
        to_above().wait_send()
        grad_above().wait_send()

    @pl.when(has_below)
    def _():
        to_below().wait_send()
        grad_below().wait_send()

    @pl.when(has_before)
    def _():
        to_before().wait_send()
        rim_before().wait_send()

    @pl.when(has_after)
    def _():
        to_after().wait_send()
        rim_after().wait_send()

    @pl.when(at.row_edge)
    def _():
        done_group(row_group, own_edge(), strips, group_sem, 0)
        done_ring(face_ring, lambda other: chosen, faces, row_face_sem)
        done_ring(face_ring, lambda other: own_grad(), row_faces, row_back_sem)
        done_group(row_group, row_chosen, row_strips, group_back, 2)

        @pl.when(has_before)
        def _():
            late_before().wait_send()

        @pl.when(has_after)
        def _():
            late_after().wait_send()

    @pl.when(is_corner)
    def _():
        done_ring(face_ring, lambda other: corner_pack, corner_faces, corner_face_sem)
        done_group(row_group, corner_out, corner_strips, corner_group_sem, 0)

    @pl.when(at.col_edge)
    def _():
        done_group(col_group, pack, col_strips, group_sem, 2)
        done_ring(face_ring, lambda other: col_chosen, col_faces, col_face_sem)
        done_ring(face_ring, lambda other: rim, rim_faces, rim_face_sem)
        done_group(col_group, rim_chosen, rim_strips, group_back, 0)

    done_ring(face_ring, piece1, a1, s1)
    done_ring(col_ring, piece2, a2, s2)
    done_ring(row_ring, lambda other: a3_src, a3, s3)
    done_ring(col_ring, lambda other: a4_src, a4, s4)
    done_ring(face_ring, lambda other: a5_src, a5, s5)


def finish_kernel(
    grad_scale,
    next_rows,
    prior_rows,
    input_rows,
    grads,
    next_out,
    input_out,
    prior_out,
    kernel_out,
    expand_out,
    reduce_out,
    gates_out,
    candidate_out,
    natural,
):
    for rows, out in ((next_rows, next_out), (input_rows, input_out), (prior_rows, prior_out)):
        for y in range(TR):
            natural[pl.ds(y, CH, stride=TR), :] = rows[y].astype(F32)
        out[...] = natural[...].reshape(CH, TR, TC).astype(BF)
    scaled = grads[...].astype(F32) * grad_scale
    expand_out[:, :TC] = scaled[0:64]
    expand_out[:, TC:] = scaled[64:128]
    reduce_out[:, :TC] = scaled[128:192]
    reduce_out[:, TC:] = scaled[192:256]
    gates_out[...] = scaled[256:384]
    candidate_out[...] = scaled[384:448]
    kernel_out[...] = scaled[448:512].T[: KS * KS]


def dma(*shape):
    return pltpu.SemaphoreType.DMA(shape)


def whole_step(dims, *given):
    nf, nr, nc = dims
    part1 = PACK_ROWS // nf
    part2 = part1 // nc
    wide = (PR, CH, TC)
    tile = (TR, CH, TC)
    strip = (RIM, CH, TC)
    flat = (CH * TR, TC)
    edge = (CH, TC)
    rows = jax.ShapeDtypeStruct(tile, BF)
    bf16_scratch = [
        wide,
        (4,) + strip,
        strip,
        (nf,) + strip,
        edge,
        (2,) + edge,
        (4,) + edge,
        edge,
        (nf,) + edge,
        (TC, PR * TC),
        edge,
    ]
    f32_scratch = [
        wide,
        wide,
        (KS,) + wide,
        (KS * KS, CH, TC),
        tile,
        tile,
        flat,
        flat,
        wide,
        wide,
        (CH, HID),
        (CH, HID),
        (2 * CH, 2 * CH),
        (CH, 2 * CH),
    ]
    back_scratch = [
        (PACK_ROWS, TC),
        edge,
        (2,) + strip,
        (2,) + edge,
        (nf,) + edge,
        edge,
        (4,) + edge,
        (2,) + strip,
        (nf,) + strip,
        strip,
        (4,) + strip,
        (nf, part1, TC),
    ]
    sum_scratch = [(part1, TC), (nc, part2, TC), (part2, TC), (nr, part2, TC), (part2, TC), (nc, part2, TC)]
    return pl.pallas_call(
        functools.partial(step_kernel, dims),
        out_shape=(rows, rows, rows, jax.ShapeDtypeStruct((PACK_ROWS, TC), BF)),
        in_specs=[HBM] * 10,
        out_specs=(VMEM,) * 4,
        scratch_shapes=[pltpu.VMEM(value.shape, value.dtype) for value in given[:8]]
        + [pltpu.SMEM(value.shape, value.dtype) for value in given[8:]]
        + [dma(10)]
        + [pltpu.VMEM((2,) + edge, BF), pltpu.VMEM(edge, BF), pltpu.VMEM((nf,) + edge, BF)]
        + [pltpu.VMEM(edge, BF), pltpu.VMEM((4,) + edge, BF), dma(2, nf), dma(2, 4), pltpu.VMEM(edge, BF)]
        + [pltpu.VMEM(flat, F32)]
        + [pltpu.VMEM(shape, BF) for shape in bf16_scratch]
        + [pltpu.VMEM(shape, F32) for shape in f32_scratch]
        + [pltpu.VMEM(shape, BF) for shape in back_scratch]
        + [pltpu.VMEM(shape, F32) for shape in sum_scratch]
        + [pltpu.VMEM((part1, TC), BF), pltpu.VMEM((nf, part1, TC), BF)]
        + [dma(2, 4), dma(2, 2), dma(4, 4), dma(2, nf), dma(2, nf)]
        + [dma(2, 4), dma(4, 4), dma(2, nf), dma(2, nf)]
        + [dma(2, nf), dma(2, nc), dma(2, nr), dma(2, nc), dma(2, nf)],
        compiler_params=pltpu.CompilerParams(
            collective_id=0, has_side_effects=True, vmem_limit_bytes=LIMIT
        ),
        name="whole_step",
    )(*given)


def finish(grad_scale, next_rows, prior_rows, input_rows, grads):
    tile = jax.ShapeDtypeStruct((CH, TR, TC), BF)
    shapes = ((KS * KS, CH), (CH, HID), (CH, HID), (2 * CH, 2 * CH), (CH, 2 * CH))
    return pl.pallas_call(
        functools.partial(finish_kernel, grad_scale),
        out_shape=(tile,) * 3 + tuple(jax.ShapeDtypeStruct(shape, F32) for shape in shapes),
        in_specs=[VMEM] * 4,
        out_specs=(VMEM,) * 8,
        scratch_shapes=[pltpu.VMEM((CH * TR, TC), F32)],
        compiler_params=pltpu.CompilerParams(vmem_limit_bytes=LIMIT),
        name="finish",
    )(next_rows, prior_rows, input_rows, grads)


def body(dims, cell_total, block_in, hidden_state, state_cotangent, kernel, we, wr, wg, wc, sf, sc):
    rows = whole_step(
        dims, block_in[0], hidden_state[0], state_cotangent[0], kernel.T, we, wr.T, wg, wc.T, sf.T, sc.T
    )
    done = finish(1.0 / math.sqrt(cell_total), *rows)
    return (
        done[0][None],
        done[1][None],
        done[2][None],
        done[3].T,
        done[4],
        done[5].T,
        done[6],
        done[7].T,
    )


def solution(mesh):
    dims = tuple(mesh.shape[name] for name in AXES)
    cell_total = dims[0] * dims[1] * dims[2] * TR * TC
    tiles = P("face", None, "row", "col")
    return jax.shard_map(
        functools.partial(body, dims, cell_total),
        mesh=mesh,
        in_specs=(tiles,) * 3 + (P(),) * 7,
        out_specs=(tiles,) * 3 + (P(),) * 5,
        check_vma=False,
    )
```

```python
import functools
import math

import jax
import jax.numpy as jnp
from jax import lax
from jax.experimental import pallas as pl
from jax.experimental.pallas import tpu as pltpu
from jax.sharding import PartitionSpec as P

AXES = ("face", "row", "col")
CH = 64
HID = 256
KS = 7
RIM = 3
TR = 8
TC = 128
PR = TR + 2 * RIM
PACK_ROWS = 512
BF = jnp.bfloat16
F32 = jnp.float32
MESH = pl.DeviceIdType.MESH
VMEM = pl.BlockSpec(memory_space=pltpu.VMEM)
HBM = pl.BlockSpec(memory_space=pltpu.HBM)
LIMIT = 60 * 1024 * 1024


def spread_block(row):
    source = lax.broadcasted_iota(jnp.int32, (TC, TC), 0)
    lane = lax.broadcasted_iota(jnp.int32, (TC, TC), 1)
    place = jnp.where(lane >= TC - RIM, lane - (TC - RIM), jnp.where(lane < RIM, lane + RIM, -TC * 8))
    return jnp.where(source == row * 8 + place, 1.0, 0.0).astype(BF)


def turn_matrix(code):
    source = lax.broadcasted_iota(jnp.int32, (TC, TC), 0)
    lane = lax.broadcasted_iota(jnp.int32, (TC, TC), 1)
    row = lane // 8
    place = lane % 8
    from_row = jnp.where(code >= 2, PR - 1 - row, row)
    from_place = jnp.where(code % 2 == 1, 5 - place, place)
    used = jnp.logical_and(place < 2 * RIM, row < PR)
    return jnp.where(jnp.where(used, from_row * 8 + from_place, -1) == source, 1.0, 0.0).astype(BF)


def flip_matrix():
    source = lax.broadcasted_iota(jnp.int32, (TC, TC), 0)
    lane = lax.broadcasted_iota(jnp.int32, (TC, TC), 1)
    return jnp.where(source == TC - 1 - lane, 1.0, 0.0).astype(BF)


def dot(a, b):
    return jnp.dot(a, b, preferred_element_type=F32)


def dot_nt(a, b):
    return lax.dot_general(a, b, (((1,), (1,)), ((), ())), preferred_element_type=F32)


def send(src, dst, send_sem, recv_sem, device):
    return pltpu.make_async_remote_copy(
        src_ref=src,
        dst_ref=dst,
        send_sem=send_sem,
        recv_sem=recv_sem,
        device_id=device,
        device_id_type=MESH,
    )


def partner_of(seam_face, side, face, count):
    found = jnp.int32(0)
    for other in range(count):
        found = jnp.where(seam_face[side, other] == face, other, found)
    return found


def kind_of(side_bit, code):
    odd = lax.rem(code, 2)
    return jnp.where(side_bit == 0, 1 - odd, odd)


def corner_of(sf, sc, face, v, h):
    beside = sf[h + 2, face]
    code = sc[h + 2, face]
    reverse = code // 2
    v_there = (v + reverse) % 2
    owner = sf[v_there, beside]
    code_there = sc[v_there, beside]
    reverse_there = code_there // 2
    block = kind_of(v_there, code_there) * 2 + (kind_of(h, code) + reverse_there) % 2
    return owner, block, (code_there + reverse) % 2, (code + reverse_there) % 2


def corner_lanes(lane, v, h, block, row_turn, col_turn):
    i = lane // 8 - jnp.where(v == 0, 0, RIM + TR)
    j = lane % 8 - jnp.where(h == 0, 0, RIM)
    inside = jnp.logical_and(
        jnp.logical_and(i >= 0, i < RIM), jnp.logical_and(j >= 0, j < RIM)
    )
    i = jnp.where(row_turn == 1, RIM - 1 - i, i)
    j = jnp.where(col_turn == 1, RIM - 1 - j, j)
    return jnp.where(inside, block * 32 + i * 8 + j, -1)


def one_hot(hit):
    return jnp.where(hit, 1.0, 0.0).astype(BF)


def block_lanes(lane, block, i):
    mine = jnp.logical_and(lane // 8 == block * 4 + i, lane % 8 < RIM)
    return jnp.where(mine, lane % 8 + jnp.where(block % 2 == 0, 0, TC - RIM), -1)


class Place:
    def __init__(self, dims):
        self.nf, self.nr, self.nc = dims
        self.f = lax.axis_index("face")
        self.r = lax.axis_index("row")
        self.c = lax.axis_index("col")
        self.top = self.r == 0
        self.bottom = self.r == self.nr - 1
        self.left = self.c == 0
        self.right = self.c == self.nc - 1
        self.row_edge = jnp.logical_or(self.top, self.bottom)
        self.col_edge = jnp.logical_or(self.left, self.right)
        self.nx = self.nc // 2
        self.core = self.r % 2
        self.x = self.c % self.nx
        self.near = self.x * 2 + self.core
        self.z = (self.r // 2) * 2 + self.c // self.nx
        self.row_kind = jnp.where(self.top, 0, 1)
        self.col_kind = jnp.where(self.left, 0, 1)

    def at(self, f=None, r=None, c=None):
        return (
            self.f if f is None else f,
            self.r if r is None else r,
            self.c if c is None else c,
        )

    def row_group(self):
        other_r = self.nr - 1 - self.r
        other_c = self.nc - 1 - self.c
        return [
            (self.at(c=other_c), self.row_kind * 2 + 1, self.row_kind * 2 + 1),
            (self.at(r=other_r), self.row_kind * 2, (1 - self.row_kind) * 2),
            (self.at(r=other_r, c=other_c), self.row_kind * 2 + 1, (1 - self.row_kind) * 2 + 1),
        ]

    def col_group(self):
        other_r = self.nr - 1 - self.r
        other_c = self.nc - 1 - self.c
        return [
            (self.at(r=other_r), self.col_kind * 2 + 1, self.col_kind * 2 + 1),
            (self.at(c=other_c), self.col_kind * 2, (1 - self.col_kind) * 2),
            (self.at(r=other_r, c=other_c), self.col_kind * 2 + 1, (1 - self.col_kind) * 2 + 1),
        ]

    def ring(self, axis):
        index, count = {
            "face": (self.f, self.nf),
            "near": (self.near, self.nx * 2),
            "z": (self.z, self.nr),
        }[axis]
        out = []
        for step in range(1, count):
            other = lax.rem(index + step, count)
            if axis == "face":
                device = self.at(f=other)
            elif axis == "near":
                device = self.at(
                    r=self.r - self.core + other % 2, c=self.c - self.x + other // 2
                )
            else:
                device = self.at(
                    r=(other // 2) * 2 + self.core, c=(other % 2) * self.nx + self.x
                )
            out.append((other, device, step))
        return out


def start_group(group, src, slots, sems, back):
    for i, (device, slot, unused) in enumerate(group):
        send(src, slots.at[slot], sems.at[back, i], sems.at[back + 1, slot], device).start()


def wait_group(group, src, slots, sems, back):
    for i, (device, unused, slot) in enumerate(group):
        send(src, slots.at[slot], sems.at[back, i], sems.at[back + 1, slot], device).wait_recv()


def done_group(group, src, slots, sems, back):
    for i, (device, unused, slot) in enumerate(group):
        send(src, slots.at[slot], sems.at[back, i], sems.at[back + 1, slot], device).wait_send()


def start_ring(ring, me, src_of, slots, sems):
    for other, device, step in ring:
        send(src_of(other), slots.at[me], sems.at[0, step], sems.at[1, me], device).start()


def wait_ring(ring, src_of, slots, sems):
    for other, device, step in ring:
        send(src_of(other), slots.at[other], sems.at[0, step], sems.at[1, other], device).wait_recv()


def done_ring(ring, src_of, slots, sems):
    for other, device, step in ring:
        send(src_of(other), slots.at[other], sems.at[0, step], sems.at[1, other], device).wait_send()


def greet(barrier, device):
    pl.semaphore_signal(barrier, inc=1, device_id=device, device_id_type=MESH)


def oriented(strip, code, flip):
    turned = jnp.concatenate([strip[2:3], strip[1:2], strip[0:1]], axis=0)
    strip = jnp.where(code % 2 == 1, turned, strip)
    mirrored = dot(strip.reshape(RIM * CH, TC).astype(BF), flip).reshape(RIM, CH, TC)
    return jnp.where(code >= 2, mirrored, strip).astype(BF)


def step_kernel(
    dims,
    x_in,
    prior_in,
    cot_in,
    kernel_in,
    we_in,
    wr_in,
    wg_in,
    wc_in,
    sf_in,
    sc_in,
    next_out,
    prior_out,
    input_out,
    grads_out,
    x_ref,
    prior_ref,
    cot_ref,
    kernel_ref,
    we_ref,
    wr_ref,
    wg_ref,
    wc_ref,
    sf,
    sc,
    in_sem,
    sides_late,
    corner_pack,
    corner_faces,
    corner_out,
    corner_strips,
    corner_face_sem,
    corner_group_sem,
    pack_late,
    natural,
    xw,
    strips,
    chosen,
    faces,
    pack,
    sides,
    col_strips,
    col_chosen,
    col_faces,
    spread,
    halo,
    xf,
    ef,
    shifted,
    taps,
    summed,
    back,
    prior,
    cot,
    total,
    edge_grad,
    gc,
    grads,
    rim,
    edges,
    rim_sides,
    rim_faces,
    rim_chosen,
    rim_strips,
    row_sides,
    row_faces,
    row_chosen,
    row_strips,
    a1,
    a2_src,
    a2,
    a3_src,
    a3,
    a4_src,
    a4,
    near,
    near_late,
    group_sem,
    row_face_sem,
    col_face_sem,
    near_back,
    group_back,
    rim_face_sem,
    row_back_sem,
    s1,
    s2,
    s3,
    s4,
):
    held = (x_ref, prior_ref, cot_ref, kernel_ref, we_ref, wr_ref, wg_ref, wc_ref, sf, sc)
    given = (x_in, prior_in, cot_in, kernel_in, we_in, wr_in, wg_in, wc_in, sf_in, sc_in)
    loads = [
        pltpu.make_async_copy(source, target, in_sem.at[i])
        for i, (source, target) in enumerate(zip(given, held))
    ]
    for load in loads:
        load.start()
    for ref in (sides, sides_late, rim_sides):
        ref[...] = jnp.zeros_like(ref)
    at = Place(dims)
    nf, nr, nc = dims
    near_count = at.nx * 2
    part1 = PACK_ROWS // near_count
    face_ring = at.ring("face")
    near_ring = at.ring("near")
    z_ring = at.ring("z")
    row_group = at.row_group()
    col_group = at.col_group()
    barrier = pltpu.get_barrier_semaphore()
    for ring in (face_ring, near_ring, z_ring):
        for unused, device, unused2 in ring:
            greet(barrier, device)
    above = at.at(r=jnp.maximum(at.r - 1, 0))
    below = at.at(r=jnp.minimum(at.r + 1, nr - 1))
    before = at.at(c=jnp.maximum(at.c - 1, 0))
    after = at.at(c=jnp.minimum(at.c + 1, nc - 1))
    has_above = jnp.logical_not(at.top)
    has_below = jnp.logical_not(at.bottom)
    has_before = jnp.logical_not(at.left)
    has_after = jnp.logical_not(at.right)
    any_edge = jnp.logical_or(at.row_edge, at.col_edge)
    expected = nf + near_count + nr - 3
    for present, device in ((has_above, above), (has_below, below), (has_before, before), (has_after, after)):
        expected = expected + jnp.where(present, 1, 0)

        @pl.when(present)
        def _(device=device):
            greet(barrier, device)

    @pl.when(any_edge)
    def _():
        for device, unused, unused2 in row_group:
            greet(barrier, device)

    loads[0].wait()
    natural[...] = x_ref[...].astype(F32).reshape(CH * TR, TC)
    for y in range(TR):
        xw[RIM + y] = natural[pl.ds(y, CH, stride=TR), :].astype(BF)
    pl.semaphore_wait(barrier, expected + jnp.where(any_edge, 3, 0))

    def to_above():
        return send(xw.at[pl.ds(RIM, RIM)], xw.at[pl.ds(RIM + TR, RIM)], near.at[0, 0], near.at[1, 0], above)

    def to_below():
        return send(xw.at[pl.ds(TR, RIM)], xw.at[pl.ds(0, RIM)], near.at[0, 1], near.at[1, 1], below)

    def own_edge():
        return xw.at[pl.ds(jnp.where(at.top, RIM, TR), RIM)]

    @pl.when(at.row_edge)
    def _():
        start_group(row_group, own_edge(), strips, group_sem, 0)

    @pl.when(has_above)
    def _():
        to_above().start()

    @pl.when(has_below)
    def _():
        to_below().start()

    edge_rows = jnp.zeros((RIM, CH, TC), BF)

    @pl.when(at.top)
    def _():
        xw[0:RIM] = edge_rows

    @pl.when(at.bottom)
    def _():
        xw[RIM + TR : PR] = edge_rows

    for row in range(PR):
        spread[:, row * TC : (row + 1) * TC] = spread_block(row)
    flip = flip_matrix()
    for load in loads[1:]:
        load.wait()
    prior[...] = prior_ref[...].astype(F32).reshape(CH * TR, TC)
    cot[...] = cot_ref[...].astype(F32).reshape(CH * TR, TC)
    gc[:, 0 : KS * KS] = kernel_ref[...].T
    is_corner = jnp.logical_and(at.row_edge, at.col_edge)

    @pl.when(has_below)
    def _():
        to_above().wait_recv()

    @pl.when(has_above)
    def _():
        to_below().wait_recv()

    flat = jnp.concatenate([xw[row] for row in range(PR)], axis=1)
    pack[...] = dot_nt(flat, spread[...]).astype(BF)

    def to_before():
        return send(pack, sides.at[1], near.at[0, 2], near.at[1, 2], before)

    def to_after():
        return send(pack, sides.at[0], near.at[0, 3], near.at[1, 3], after)

    @pl.when(at.col_edge)
    def _():
        start_group(col_group, pack, col_strips, group_sem, 2)

    @pl.when(has_before)
    def _():
        to_before().start()

    @pl.when(has_after)
    def _():
        to_after().start()

    @pl.when(at.row_edge)
    def _():
        strips[at.row_kind * 2] = own_edge()[...]
        wait_group(row_group, own_edge(), strips, group_sem, 0)
        taker = partner_of(sf, at.row_kind, at.f, nf)
        code = sc[at.row_kind, taker]
        picked = strips[kind_of(at.row_kind, code) * 2 + code // 2]
        chosen[...] = picked
        start_ring(face_ring, at.f, lambda other: chosen, faces, row_face_sem)
        faces[at.f] = picked

    @pl.when(is_corner)
    def _():
        source = lax.broadcasted_iota(jnp.int32, (TC, TC), 0)
        lanes = lax.broadcasted_iota(jnp.int32, (TC, TC), 1)
        blocks = jnp.zeros((CH, TC), F32)
        for slot in range(4):
            block = (slot // 2) * 2 + (at.col_kind + slot) % 2
            for i in range(RIM):
                blocks = blocks + dot(strips[slot, i], one_hot(block_lanes(lanes, block, i) == source))
        corner_pack[...] = blocks.astype(BF)
        start_ring(face_ring, at.f, lambda other: corner_pack, corner_faces, corner_face_sem)
        corner_faces[at.f] = blocks.astype(BF)

    @pl.when(at.col_edge)
    def _():
        side = at.col_kind + 2
        col_strips[at.col_kind * 2] = pack[...]
        wait_group(col_group, pack, col_strips, group_sem, 2)
        code = sc[side, partner_of(sf, side, at.f, nf)]
        picked = col_strips[kind_of(at.col_kind, code) * 2 + code // 2]
        col_chosen[...] = picked
        start_ring(face_ring, at.f, lambda other: col_chosen, col_faces, col_face_sem)
        col_faces[at.f] = picked

    def late_before():
        return send(pack_late, sides_late.at[1], near_late.at[0, 0], near_late.at[1, 0], before)

    def late_after():
        return send(pack_late, sides_late.at[0], near_late.at[0, 1], near_late.at[1, 1], after)

    @pl.when(at.row_edge)
    def _():
        wait_ring(face_ring, lambda other: chosen, faces, row_face_sem)
        strip = oriented(faces[sf[at.row_kind, at.f]].astype(F32), sc[at.row_kind, at.f], flip)
        xw[pl.ds(jnp.where(at.top, 0, RIM + TR), RIM)] = strip
        late = jnp.zeros((CH, TC), F32)
        source = lax.broadcasted_iota(jnp.int32, (TC, TC), 0)
        lanes = lax.broadcasted_iota(jnp.int32, (TC, TC), 1)
        first = jnp.where(at.top, 0, RIM + TR)
        for i in range(RIM):
            wanted = jnp.where(lanes % 8 < RIM, lanes % 8 + TC - RIM, lanes % 8 - RIM)
            wanted = jnp.where(
                jnp.logical_and(lanes // 8 == first + i, lanes % 8 < 2 * RIM), wanted, -1
            )
            late = late + dot(strip[i], one_hot(wanted == source))
        pack_late[...] = late.astype(BF)

        @pl.when(has_before)
        def _():
            late_before().start()

        @pl.when(has_after)
        def _():
            late_after().start()

    xf[...] = xw[...].astype(F32)

    @pl.when(at.col_edge)
    def _():
        side = at.col_kind + 2
        wait_ring(face_ring, lambda other: col_chosen, col_faces, col_face_sem)
        strip = col_faces[sf[side, at.f]]
        sides[at.col_kind] = dot(strip, turn_matrix(sc[side, at.f])).astype(BF)

    @pl.when(is_corner)
    def _():
        wait_ring(face_ring, lambda other: corner_pack, corner_faces, corner_face_sem)
        source = lax.broadcasted_iota(jnp.int32, (TC, TC), 0)
        lanes = lax.broadcasted_iota(jnp.int32, (TC, TC), 1)
        owner, block, row_turn, col_turn = corner_of(sf, sc, at.f, at.row_kind, at.col_kind)
        pick = one_hot(corner_lanes(lanes, at.row_kind, at.col_kind, block, row_turn, col_turn) == source)
        sides_late[at.col_kind] = dot(corner_faces[owner], pick).astype(BF)

    @pl.when(has_after)
    def _():
        to_before().wait_recv()

    @pl.when(has_before)
    def _():
        to_after().wait_recv()

    @pl.when(at.row_edge)
    def _():
        @pl.when(has_after)
        def _():
            late_before().wait_recv()

        @pl.when(has_before)
        def _():
            late_after().wait_recv()

    place = lax.broadcasted_iota(jnp.int32, (CH, TC), 1) % 8
    low = place < RIM
    halo[...] = (
        jnp.where(low, sides[0].astype(F32), sides[1].astype(F32))
        + jnp.where(low, sides_late[0].astype(F32), sides_late[1].astype(F32))
    ).astype(BF)

    ends = dot(halo[...], spread[...])
    for row in range(PR):
        ef[row] = ends[:, row * TC : (row + 1) * TC]
    lane = lax.broadcasted_iota(jnp.int32, (PR, 8, TC), 2)
    lane2 = lax.broadcasted_iota(jnp.int32, (8, TC), 1)

    def forward(g, carry):
        part = pl.ds(pl.multiple_of(g * 8, 8), 8)
        values = gc[part, :]
        sums = jnp.zeros((TR, 8, TC), F32)
        inside = xf[:, part, :]
        outside = ef[:, part, :]
        for b in range(KS):
            d = b - RIM
            rows = inside
            if d:
                wrapped = lane < d if d > 0 else lane >= TC + d
                rows = pltpu.roll(jnp.where(wrapped, outside, inside), (-d) % TC, 2)
            shifted[b, :, part, :] = rows
            for a in range(KS):
                tap = a * KS + b
                weight = jnp.broadcast_to(values[:, tap : tap + 1], (8, TC))
                taps[tap, part, :] = weight
                sums = sums + weight[None] * rows[a : a + TR]
        summed[:, part, :] = sums
        return carry

    lax.fori_loop(0, CH // 8, forward, 0)
    we = we_ref[...]
    wr_t = wr_ref[...]
    wg = wg_ref[...]
    wc_t = wc_ref[...]
    we_t = we.T
    wr = wr_t.T
    wg_t = wg.T
    wc = wc_t.T

    def cells(load):
        return jnp.concatenate([load(y) for y in range(TR)], axis=1)

    s = cells(lambda y: summed[y])
    center = s - jnp.mean(s, axis=0, keepdims=True)
    scale = lax.rsqrt(jnp.mean(center * center, axis=0, keepdims=True) + 1e-06)
    unit = center * scale
    normed = unit.astype(BF)
    hidden = dot(we_t, normed)
    acts = []
    slopes = []
    for start in range(0, HID, 32):
        h = hidden[start : start + 32]
        cdf = 0.5 + 0.5 * lax.erf(h * math.sqrt(0.5))
        acts.append((h * cdf).astype(BF))
        slopes.append(cdf + h * (jnp.exp(-0.5 * h * h) * (1.0 / math.sqrt(2.0 * math.pi))))
    act = jnp.concatenate(acts, axis=0)
    slope = jnp.concatenate(slopes, axis=0)
    out = (cells(lambda y: xf[RIM + y]) + dot(wr_t, act)).astype(BF)
    earlier = cells(lambda y: prior[pl.ds(y, CH, stride=TR), :])
    joined = jnp.concatenate([out, earlier.astype(BF)], axis=0)
    gates = jax.nn.sigmoid(dot(wg_t, joined))
    update = gates[:CH]
    reset = gates[CH:]
    joined_reset = jnp.concatenate([out, (reset * earlier).astype(BF)], axis=0)
    proposal = jnp.tanh(dot(wc_t, joined_reset))
    result = (1.0 - update) * earlier + update * proposal
    g = cells(lambda y: cot[pl.ds(y, CH, stride=TR), :])
    d_cand = (g * update * (1.0 - proposal * proposal)).astype(BF)
    d_joined_reset = dot(wc, d_cand)
    d_reset = d_joined_reset[CH:]
    d_gates = jnp.concatenate(
        [
            g * (proposal - earlier) * (update * (1.0 - update)),
            d_reset * earlier * (reset * (1.0 - reset)),
        ],
        axis=0,
    ).astype(BF)
    d_joined = dot(wg, d_gates)
    d_out = (d_joined_reset[:CH] + d_joined[:CH]).astype(BF)
    d_prior = g * (1.0 - update) + d_reset * reset + d_joined[CH:]
    d_hidden = (dot(wr, d_out) * slope).astype(BF)
    d_normed = dot(we, d_hidden)
    d_expand = dot_nt(normed, d_hidden).astype(BF)
    d_reduce = dot_nt(d_out, act).astype(BF)
    grads[0:64] = d_expand[:, :TC]
    grads[64:128] = d_expand[:, TC:]
    grads[128:192] = d_reduce[:, :TC]
    grads[192:256] = d_reduce[:, TC:]
    grads[256:384] = dot_nt(joined, d_gates).astype(BF)
    grads[384:448] = dot_nt(d_cand, joined_reset).astype(BF)
    d_summed = scale * (
        d_normed
        - jnp.mean(d_normed, axis=0, keepdims=True)
        - unit * jnp.mean(d_normed * unit, axis=0, keepdims=True)
    )
    d_center = d_out.astype(F32)
    for y in range(TR):
        cut = slice(y * TC, (y + 1) * TC)
        back[y] = d_summed[:, cut]
        total[RIM + y] = d_center[:, cut]
        next_out[y] = result[:, cut].astype(BF)
        prior_out[y] = d_prior[:, cut].astype(BF)

    def piece1(other):
        return grads.at[pl.ds(pl.multiple_of(other * part1, part1), part1)]

    def start_shares(wanted):
        for other, device, step in near_ring:

            @pl.when((other == near_count - 1) == wanted)
            def _(other=other, device=device, step=step):
                send(piece1(other), a1.at[at.near], s1.at[0, step], s1.at[1, at.near], device).start()

    def summed_slots(slots, count):
        partial = slots[0].astype(F32)
        for other in range(1, count):
            partial = partial + slots[other].astype(F32)
        return partial.astype(BF)

    start_shares(False)

    def backward_kernel(g, carry):
        part = pl.ds(pl.multiple_of(g * 8, 8), 8)
        rows = back[:, part, :]
        found = jnp.zeros((8, TC), F32)
        for b in range(KS):
            for a in range(KS):
                terms = jnp.sum(rows * shifted[b, a : a + TR, part, :], axis=0)
                found = jnp.where(lane2 == a * KS + b, jnp.sum(terms, axis=1, keepdims=True), found)
        gc[part, :] = found
        return carry

    lax.fori_loop(0, CH // 8, backward_kernel, 0)
    grads[448:512] = gc[...].astype(BF)
    start_shares(True)
    a1[at.near] = piece1(at.near)[...]

    def backward(g, carry):
        part = pl.ds(pl.multiple_of(g * 8, 8), 8)
        rows = back[:, part, :]
        inner = jnp.zeros((PR, 8, TC), F32)
        outer = jnp.zeros((PR, 8, TC), F32)
        for b in range(KS):
            d = b - RIM
            columns = [None] * PR
            for a in range(KS):
                product = taps[a * KS + b, part, :][None] * rows
                for y in range(TR):
                    columns[y + a] = product[y] if columns[y + a] is None else columns[y + a] + product[y]
            moved = jnp.stack(columns)
            if d == 0:
                inner = inner + moved
                continue
            moved = pltpu.roll(moved, d % TC, 2)
            wrapped = lane < d if d > 0 else lane >= TC + d
            inner = inner + jnp.where(wrapped, 0.0, moved)
            outer = outer + jnp.where(wrapped, moved, 0.0)
        total[0:RIM, part, :] = inner[0:RIM]
        total[RIM : RIM + TR, part, :] = total[RIM : RIM + TR, part, :] + inner[RIM : RIM + TR]
        total[RIM + TR :, part, :] = inner[RIM + TR :]
        edge_grad[:, part, :] = outer
        return carry

    lax.fori_loop(0, CH // 8, backward, 0)
    flat = jnp.concatenate([edge_grad[row] for row in range(PR)], axis=1).astype(BF)
    rim[...] = dot_nt(flat, spread[...]).astype(BF)

    def rim_before():
        return send(rim, rim_sides.at[1], near_back.at[0, 2], near_back.at[1, 2], before)

    def rim_after():
        return send(rim, rim_sides.at[0], near_back.at[0, 3], near_back.at[1, 3], after)

    @pl.when(at.col_edge)
    def _():
        start_ring(face_ring, at.f, lambda other: rim, rim_faces, rim_face_sem)

    @pl.when(has_before)
    def _():
        rim_before().start()

    @pl.when(has_after)
    def _():
        rim_after().start()

    wait_ring(near_ring, piece1, a1, s1)
    partial = summed_slots(a1, near_count)
    a2_src[...] = partial
    start_ring(face_ring, at.f, lambda other: a2_src, a2, s2)
    a2[at.f] = partial

    @pl.when(has_after)
    def _():
        rim_before().wait_recv()

    @pl.when(has_before)
    def _():
        rim_after().wait_recv()

    def add_columns(packed):
        ends = dot(packed, spread[...])
        for row in range(PR):
            total[row] = total[row] + ends[:, row * TC : (row + 1) * TC]

    add_columns(jnp.where(low, rim_sides[1].astype(F32), rim_sides[0].astype(F32)).astype(BF))

    def own_grad():
        return edges.at[at.row_kind]

    @pl.when(at.row_edge)
    def _():
        edges[at.row_kind] = total[pl.ds(jnp.where(at.top, 0, RIM + TR), RIM)].astype(BF)
        start_ring(face_ring, at.f, lambda other: own_grad(), row_faces, row_back_sem)

    @pl.when(at.col_edge)
    def _():
        side = at.col_kind + 2
        rim_faces[at.f] = rim[...]
        wait_ring(face_ring, lambda other: rim, rim_faces, rim_face_sem)
        taker = partner_of(sf, side, at.f, nf)
        strip = rim_faces[taker].astype(F32)
        row = lax.broadcasted_iota(jnp.int32, (CH, TC), 1) // 8
        beyond = jnp.logical_or(
            jnp.logical_and(at.top, row < RIM), jnp.logical_and(at.bottom, row >= RIM + TR)
        )
        keep = jnp.logical_and(low == at.left, jnp.logical_not(beyond))
        strip = jnp.where(keep, strip, 0.0).astype(BF)
        turned = dot(strip, turn_matrix(sc[side, taker])).astype(BF)
        rim_chosen[...] = turned
        start_group(col_group, rim_chosen, rim_strips, group_back, 0)
        rim_strips[at.col_kind * 2] = turned

    @pl.when(is_corner)
    def _():
        source = lax.broadcasted_iota(jnp.int32, (TC, TC), 0)
        lanes = lax.broadcasted_iota(jnp.int32, (TC, TC), 1)
        blocks = jnp.zeros((CH, TC), F32)
        for other in range(nf):
            owner, block, row_turn, col_turn = corner_of(sf, sc, other, at.row_kind, at.col_kind)
            wanted = corner_lanes(source, at.row_kind, at.col_kind, block, row_turn, col_turn)
            wanted = jnp.where(owner == at.f, wanted, -1)
            blocks = blocks + dot(rim_faces[other], one_hot(wanted == lanes))
        corner_out[...] = blocks.astype(BF)
        start_group(row_group, corner_out, corner_strips, corner_group_sem, 0)
        corner_strips[at.row_kind * 2] = blocks.astype(BF)

    wait_ring(face_ring, lambda other: a2_src, a2, s2)
    partial = summed_slots(a2, nf)
    a3_src[...] = partial
    start_ring(z_ring, at.z, lambda other: a3_src, a3, s3)
    a3[at.z] = partial

    def seam_total(slots, kind, first_side):
        gathered = None
        for side_bit in range(2):
            taker = partner_of(sf, first_side + side_bit, at.f, nf)
            code = sc[first_side + side_bit, taker]
            mine = kind_of(side_bit, code) == kind
            for mirror in range(2):
                use = jnp.logical_and(mine, code // 2 == mirror)
                term = jnp.where(use, slots[side_bit * 2 + mirror].astype(F32), 0.0)
                gathered = term if gathered is None else gathered + term
        return gathered

    @pl.when(at.col_edge)
    def _():
        wait_group(col_group, rim_chosen, rim_strips, group_back, 0)
        back_rim = seam_total(rim_strips, at.col_kind, 2)
        add_columns(jnp.where(low == at.left, 0.0, back_rim).astype(BF))

    def grad_above():
        return send(edges.at[0], row_sides.at[1], near_back.at[0, 0], near_back.at[1, 0], above)

    def grad_below():
        return send(edges.at[1], row_sides.at[0], near_back.at[0, 1], near_back.at[1, 1], below)

    @pl.when(has_above)
    def _():
        edges[0] = total[0:RIM].astype(BF)
        grad_above().start()

    @pl.when(has_below)
    def _():
        edges[1] = total[RIM + TR : PR].astype(BF)
        grad_below().start()

    @pl.when(at.row_edge)
    def _():
        row_faces[at.f] = own_grad()[...]
        wait_ring(face_ring, lambda other: own_grad(), row_faces, row_back_sem)
        taker = partner_of(sf, at.row_kind, at.f, nf)
        strip = oriented(row_faces[taker].astype(F32), sc[at.row_kind, taker], flip_matrix())
        row_chosen[...] = strip
        start_group(row_group, row_chosen, row_strips, group_back, 2)
        row_strips[at.row_kind * 2] = strip

    wait_ring(z_ring, lambda other: a3_src, a3, s3)
    partial = summed_slots(a3, nr)
    a4_src[...] = partial
    start_ring(near_ring, at.near, lambda other: a4_src, a4, s4)
    a4[at.near] = partial

    @pl.when(has_below)
    def _():
        grad_above().wait_recv()
        total[TR : TR + RIM] = total[TR : TR + RIM] + row_sides[1].astype(F32)

    @pl.when(has_above)
    def _():
        grad_below().wait_recv()
        total[RIM : 2 * RIM] = total[RIM : 2 * RIM] + row_sides[0].astype(F32)

    @pl.when(at.row_edge)
    def _():
        wait_group(row_group, row_chosen, row_strips, group_back, 2)
        gathered = seam_total(row_strips, at.row_kind, 0)
        spot = pl.ds(jnp.where(at.top, RIM, TR), RIM)
        total[spot] = total[spot] + gathered

    @pl.when(is_corner)
    def _():
        wait_group(row_group, corner_out, corner_strips, corner_group_sem, 0)
        blocks = corner_strips[0].astype(F32)
        for slot in range(1, 4):
            blocks = blocks + corner_strips[slot].astype(F32)
        source = lax.broadcasted_iota(jnp.int32, (TC, TC), 0)
        lanes = lax.broadcasted_iota(jnp.int32, (TC, TC), 1)
        first = jnp.where(at.top, RIM, TR)
        for i in range(RIM):
            wanted = block_lanes(source, at.row_kind * 2 + at.col_kind, i)
            total[first + i] = total[first + i] + dot(blocks.astype(BF), one_hot(wanted == lanes))

    input_out[...] = total[RIM : RIM + TR].astype(BF)
    wait_ring(near_ring, lambda other: a4_src, a4, s4)
    for other in range(near_count):
        grads_out[other * part1 : (other + 1) * part1] = a4[other]

    @pl.when(has_above)
    def _():
        to_above().wait_send()
        grad_above().wait_send()

    @pl.when(has_below)
    def _():
        to_below().wait_send()
        grad_below().wait_send()

    @pl.when(has_before)
    def _():
        to_before().wait_send()
        rim_before().wait_send()

    @pl.when(has_after)
    def _():
        to_after().wait_send()
        rim_after().wait_send()

    @pl.when(at.row_edge)
    def _():
        done_group(row_group, own_edge(), strips, group_sem, 0)
        done_ring(face_ring, lambda other: chosen, faces, row_face_sem)
        done_ring(face_ring, lambda other: own_grad(), row_faces, row_back_sem)
        done_group(row_group, row_chosen, row_strips, group_back, 2)

        @pl.when(has_before)
        def _():
            late_before().wait_send()

        @pl.when(has_after)
        def _():
            late_after().wait_send()

    @pl.when(is_corner)
    def _():
        done_ring(face_ring, lambda other: corner_pack, corner_faces, corner_face_sem)
        done_group(row_group, corner_out, corner_strips, corner_group_sem, 0)

    @pl.when(at.col_edge)
    def _():
        done_group(col_group, pack, col_strips, group_sem, 2)
        done_ring(face_ring, lambda other: col_chosen, col_faces, col_face_sem)
        done_ring(face_ring, lambda other: rim, rim_faces, rim_face_sem)
        done_group(col_group, rim_chosen, rim_strips, group_back, 0)

    done_ring(near_ring, piece1, a1, s1)
    done_ring(face_ring, lambda other: a2_src, a2, s2)
    done_ring(z_ring, lambda other: a3_src, a3, s3)
    done_ring(near_ring, lambda other: a4_src, a4, s4)


def finish_kernel(
    grad_scale,
    next_rows,
    prior_rows,
    input_rows,
    grads,
    next_out,
    input_out,
    prior_out,
    kernel_out,
    expand_out,
    reduce_out,
    gates_out,
    candidate_out,
    natural,
):
    for rows, out in ((next_rows, next_out), (input_rows, input_out), (prior_rows, prior_out)):
        for y in range(TR):
            natural[pl.ds(y, CH, stride=TR), :] = rows[y].astype(F32)
        out[...] = natural[...].reshape(CH, TR, TC).astype(BF)
    scaled = grads[...].astype(F32) * grad_scale
    expand_out[:, :TC] = scaled[0:64]
    expand_out[:, TC:] = scaled[64:128]
    reduce_out[:, :TC] = scaled[128:192]
    reduce_out[:, TC:] = scaled[192:256]
    gates_out[...] = scaled[256:384]
    candidate_out[...] = scaled[384:448]
    kernel_out[...] = scaled[448:512].T[: KS * KS]


def dma(*shape):
    return pltpu.SemaphoreType.DMA(shape)


def whole_step(dims, *given):
    nf, nr, nc = dims
    near_count = nc // 2 * 2
    part1 = PACK_ROWS // near_count
    wide = (PR, CH, TC)
    tile = (TR, CH, TC)
    strip = (RIM, CH, TC)
    flat = (CH * TR, TC)
    edge = (CH, TC)
    rows = jax.ShapeDtypeStruct(tile, BF)
    bf16_scratch = [
        wide,
        (4,) + strip,
        strip,
        (nf,) + strip,
        edge,
        (2,) + edge,
        (4,) + edge,
        edge,
        (nf,) + edge,
        (TC, PR * TC),
        edge,
    ]
    f32_scratch = [
        wide,
        wide,
        (KS,) + wide,
        (KS * KS, CH, TC),
        tile,
        tile,
        flat,
        flat,
        wide,
        wide,
        (CH, TC),
    ]
    back_scratch = [
        (PACK_ROWS, TC),
        edge,
        (2,) + strip,
        (2,) + edge,
        (nf,) + edge,
        edge,
        (4,) + edge,
        (2,) + strip,
        (nf,) + strip,
        strip,
        (4,) + strip,
        (near_count, part1, TC),
        (part1, TC),
    ]
    share = (part1, TC)
    sum_scratch = [(nf,) + share, share, (nr,) + share, share, (near_count,) + share]
    return pl.pallas_call(
        functools.partial(step_kernel, dims),
        out_shape=(rows, rows, rows, jax.ShapeDtypeStruct((PACK_ROWS, TC), BF)),
        in_specs=[HBM] * 10,
        out_specs=(VMEM,) * 4,
        scratch_shapes=[pltpu.VMEM(value.shape, value.dtype) for value in given[:8]]
        + [pltpu.SMEM(value.shape, value.dtype) for value in given[8:]]
        + [dma(10)]
        + [pltpu.VMEM((2,) + edge, BF), pltpu.VMEM(edge, BF), pltpu.VMEM((nf,) + edge, BF)]
        + [pltpu.VMEM(edge, BF), pltpu.VMEM((4,) + edge, BF), dma(2, nf), dma(2, 4), pltpu.VMEM(edge, BF)]
        + [pltpu.VMEM(flat, F32)]
        + [pltpu.VMEM(shape, BF) for shape in bf16_scratch]
        + [pltpu.VMEM(shape, F32) for shape in f32_scratch]
        + [pltpu.VMEM(shape, BF) for shape in back_scratch]
        + [pltpu.VMEM(shape, BF) for shape in sum_scratch]
        + [dma(2, 4), dma(2, 2), dma(4, 4), dma(2, nf), dma(2, nf)]
        + [dma(2, 4), dma(4, 4), dma(2, nf), dma(2, nf)]
        + [dma(2, near_count), dma(2, nf), dma(2, nr), dma(2, near_count)],
        compiler_params=pltpu.CompilerParams(
            collective_id=0, has_side_effects=True, vmem_limit_bytes=LIMIT
        ),
        name="whole_step",
    )(*given)


def finish(grad_scale, next_rows, prior_rows, input_rows, grads):
    tile = jax.ShapeDtypeStruct((CH, TR, TC), BF)
    shapes = ((KS * KS, CH), (CH, HID), (CH, HID), (2 * CH, 2 * CH), (CH, 2 * CH))
    return pl.pallas_call(
        functools.partial(finish_kernel, grad_scale),
        out_shape=(tile,) * 3 + tuple(jax.ShapeDtypeStruct(shape, F32) for shape in shapes),
        in_specs=[VMEM] * 4,
        out_specs=(VMEM,) * 8,
        scratch_shapes=[pltpu.VMEM((CH * TR, TC), F32)],
        compiler_params=pltpu.CompilerParams(vmem_limit_bytes=LIMIT),
        name="finish",
    )(next_rows, prior_rows, input_rows, grads)


def body(dims, cell_total, block_in, hidden_state, state_cotangent, kernel, we, wr, wg, wc, sf, sc):
    rows = whole_step(
        dims, block_in[0], hidden_state[0], state_cotangent[0], kernel.T, we, wr.T, wg, wc.T, sf.T, sc.T
    )
    done = finish(1.0 / math.sqrt(cell_total), *rows)
    return (
        done[0][None],
        done[1][None],
        done[2][None],
        done[3].T,
        done[4],
        done[5].T,
        done[6],
        done[7].T,
    )


def solution(mesh):
    dims = tuple(mesh.shape[name] for name in AXES)
    cell_total = dims[0] * dims[1] * dims[2] * TR * TC
    tiles = P("face", None, "row", "col")
    return jax.shard_map(
        functools.partial(body, dims, cell_total),
        mesh=mesh,
        in_specs=(tiles,) * 3 + (P(),) * 7,
        out_specs=(tiles,) * 3 + (P(),) * 5,
        check_vma=False,
    )
```

```python
import functools
import math

import jax
import jax.numpy as jnp
from jax import lax
from jax.experimental import pallas as pl
from jax.experimental.pallas import tpu as pltpu
from jax.sharding import PartitionSpec as P

AXES = ("face", "row", "col")
CH = 64
HID = 256
KS = 7
RIM = 3
TR = 8
TC = 128
PR = TR + 2 * RIM
PACK_ROWS = 512
LATE_ROW = 448
BF = jnp.bfloat16
F32 = jnp.float32
MESH = pl.DeviceIdType.MESH
VMEM = pl.BlockSpec(memory_space=pltpu.VMEM)
HBM = pl.BlockSpec(memory_space=pltpu.HBM)
LIMIT = 60 * 1024 * 1024


def spread_block(row):
    source = lax.broadcasted_iota(jnp.int32, (TC, TC), 0)
    lane = lax.broadcasted_iota(jnp.int32, (TC, TC), 1)
    place = jnp.where(lane >= TC - RIM, lane - (TC - RIM), jnp.where(lane < RIM, lane + RIM, -TC * 8))
    return jnp.where(source == row * 8 + place, 1.0, 0.0).astype(BF)


def turn_matrix(code):
    source = lax.broadcasted_iota(jnp.int32, (TC, TC), 0)
    lane = lax.broadcasted_iota(jnp.int32, (TC, TC), 1)
    row = lane // 8
    place = lane % 8
    from_row = jnp.where(code >= 2, PR - 1 - row, row)
    from_place = jnp.where(code % 2 == 1, 5 - place, place)
    used = jnp.logical_and(place < 2 * RIM, row < PR)
    return jnp.where(jnp.where(used, from_row * 8 + from_place, -1) == source, 1.0, 0.0).astype(BF)


def flip_matrix():
    source = lax.broadcasted_iota(jnp.int32, (TC, TC), 0)
    lane = lax.broadcasted_iota(jnp.int32, (TC, TC), 1)
    return jnp.where(source == TC - 1 - lane, 1.0, 0.0).astype(BF)


def dot(a, b):
    return jnp.dot(a, b, preferred_element_type=F32)


def dot_nt(a, b):
    return lax.dot_general(a, b, (((1,), (1,)), ((), ())), preferred_element_type=F32)


def send(src, dst, send_sem, recv_sem, device):
    return pltpu.make_async_remote_copy(
        src_ref=src,
        dst_ref=dst,
        send_sem=send_sem,
        recv_sem=recv_sem,
        device_id=device,
        device_id_type=MESH,
    )


def partner_of(seam_face, side, face, count):
    found = jnp.int32(0)
    for other in range(count):
        found = jnp.where(seam_face[side, other] == face, other, found)
    return found


def kind_of(side_bit, code):
    odd = lax.rem(code, 2)
    return jnp.where(side_bit == 0, 1 - odd, odd)


def corner_of(sf, sc, face, v, h):
    beside = sf[h + 2, face]
    code = sc[h + 2, face]
    reverse = code // 2
    v_there = (v + reverse) % 2
    owner = sf[v_there, beside]
    code_there = sc[v_there, beside]
    reverse_there = code_there // 2
    block = kind_of(v_there, code_there) * 2 + (kind_of(h, code) + reverse_there) % 2
    return owner, block, (code_there + reverse) % 2, (code + reverse_there) % 2


def corner_lanes(lane, v, h, block, row_turn, col_turn):
    i = lane // 8 - jnp.where(v == 0, 0, RIM + TR)
    j = lane % 8 - jnp.where(h == 0, 0, RIM)
    inside = jnp.logical_and(
        jnp.logical_and(i >= 0, i < RIM), jnp.logical_and(j >= 0, j < RIM)
    )
    i = jnp.where(row_turn == 1, RIM - 1 - i, i)
    j = jnp.where(col_turn == 1, RIM - 1 - j, j)
    return jnp.where(inside, block * 32 + i * 8 + j, -1)


def one_hot(hit):
    return jnp.where(hit, 1.0, 0.0).astype(BF)


def block_lanes(lane, block, i):
    mine = jnp.logical_and(lane // 8 == block * 4 + i, lane % 8 < RIM)
    return jnp.where(mine, lane % 8 + jnp.where(block % 2 == 0, 0, TC - RIM), -1)


class Place:
    def __init__(self, dims):
        self.nf, self.nr, self.nc = dims
        self.f = lax.axis_index("face")
        self.r = lax.axis_index("row")
        self.c = lax.axis_index("col")
        self.top = self.r == 0
        self.bottom = self.r == self.nr - 1
        self.left = self.c == 0
        self.right = self.c == self.nc - 1
        self.row_edge = jnp.logical_or(self.top, self.bottom)
        self.col_edge = jnp.logical_or(self.left, self.right)
        self.core = self.r % 2
        self.near = self.c * 2 + self.core
        self.z = self.r // 2
        self.row_kind = jnp.where(self.top, 0, 1)
        self.col_kind = jnp.where(self.left, 0, 1)

    def at(self, f=None, r=None, c=None):
        return (
            self.f if f is None else f,
            self.r if r is None else r,
            self.c if c is None else c,
        )

    def row_group(self):
        other_r = self.nr - 1 - self.r
        other_c = self.nc - 1 - self.c
        return [
            (self.at(c=other_c), self.row_kind * 2 + 1, self.row_kind * 2 + 1),
            (self.at(r=other_r), self.row_kind * 2, (1 - self.row_kind) * 2),
            (self.at(r=other_r, c=other_c), self.row_kind * 2 + 1, (1 - self.row_kind) * 2 + 1),
        ]

    def col_group(self):
        other_r = self.nr - 1 - self.r
        other_c = self.nc - 1 - self.c
        return [
            (self.at(r=other_r), self.col_kind * 2 + 1, self.col_kind * 2 + 1),
            (self.at(c=other_c), self.col_kind * 2, (1 - self.col_kind) * 2),
            (self.at(r=other_r, c=other_c), self.col_kind * 2 + 1, (1 - self.col_kind) * 2 + 1),
        ]

    def ring(self, axis):
        index, count = {
            "face": (self.f, self.nf),
            "near": (self.near, self.nc * 2),
            "z": (self.z, self.nr // 2),
        }[axis]
        out = []
        for step in range(1, count):
            other = lax.rem(index + step, count)
            if axis == "face":
                device = self.at(f=other)
            elif axis == "near":
                device = self.at(r=self.r - self.core + other % 2, c=other // 2)
            else:
                device = self.at(r=other * 2 + self.core)
            out.append((other, device, step))
        return out


def start_group(group, src, slots, sems, back):
    for i, (device, slot, unused) in enumerate(group):
        send(src, slots.at[slot], sems.at[back, i], sems.at[back + 1, slot], device).start()


def wait_group(group, src, slots, sems, back):
    for i, (device, unused, slot) in enumerate(group):
        send(src, slots.at[slot], sems.at[back, i], sems.at[back + 1, slot], device).wait_recv()


def done_group(group, src, slots, sems, back):
    for i, (device, unused, slot) in enumerate(group):
        send(src, slots.at[slot], sems.at[back, i], sems.at[back + 1, slot], device).wait_send()


def start_ring(ring, me, src_of, slots, sems):
    for other, device, step in ring:
        send(src_of(other), slots.at[me], sems.at[0, step], sems.at[1, me], device).start()


def wait_ring(ring, src_of, slots, sems):
    for other, device, step in ring:
        send(src_of(other), slots.at[other], sems.at[0, step], sems.at[1, other], device).wait_recv()


def done_ring(ring, src_of, slots, sems):
    for other, device, step in ring:
        send(src_of(other), slots.at[other], sems.at[0, step], sems.at[1, other], device).wait_send()


def greet(barrier, device):
    pl.semaphore_signal(barrier, inc=1, device_id=device, device_id_type=MESH)


def oriented(strip, code, flip):
    turned = jnp.concatenate([strip[2:3], strip[1:2], strip[0:1]], axis=0)
    strip = jnp.where(code % 2 == 1, turned, strip)
    mirrored = dot(strip.reshape(RIM * CH, TC).astype(BF), flip).reshape(RIM, CH, TC)
    return jnp.where(code >= 2, mirrored, strip).astype(BF)


def step_kernel(
    dims,
    x_in,
    prior_in,
    cot_in,
    kernel_in,
    we_in,
    wr_in,
    wg_in,
    wc_in,
    sf_in,
    sc_in,
    next_out,
    prior_out,
    input_out,
    grads_out,
    x_ref,
    prior_ref,
    cot_ref,
    kernel_ref,
    we_ref,
    wr_ref,
    wg_ref,
    wc_ref,
    sf,
    sc,
    in_sem,
    sides_late,
    corner_pack,
    corner_faces,
    corner_out,
    corner_strips,
    corner_face_sem,
    corner_group_sem,
    pack_late,
    late_pick,
    turns,
    picks,
    natural,
    xw,
    strips,
    chosen,
    faces,
    pack,
    sides,
    col_strips,
    col_chosen,
    col_faces,
    spread,
    halo,
    xf,
    met,
    shifted,
    taps,
    summed,
    back,
    prior,
    cot,
    total,
    edge_back,
    gc,
    grads,
    rim,
    edges,
    rim_sides,
    rim_faces,
    rim_chosen,
    rim_strips,
    row_sides,
    row_faces,
    row_chosen,
    row_strips,
    a1,
    a2_src,
    a2,
    a3_src,
    a3,
    a4_src,
    a4,
    near,
    near_late,
    group_sem,
    row_face_sem,
    col_face_sem,
    near_back,
    group_back,
    rim_face_sem,
    row_back_sem,
    s1,
    s2,
    s3,
    s4,
):
    held = (x_ref, prior_ref, cot_ref, kernel_ref, we_ref, wr_ref, wg_ref, wc_ref, sf, sc)
    given = (x_in, prior_in, cot_in, kernel_in, we_in, wr_in, wg_in, wc_in, sf_in, sc_in)
    loads = [
        pltpu.make_async_copy(source, target, in_sem.at[i])
        for i, (source, target) in enumerate(zip(given, held))
    ]
    for load in loads:
        load.start()
    for ref in (sides, sides_late, rim_sides):
        ref[...] = jnp.zeros_like(ref)
    at = Place(dims)
    nf, nr, nc = dims
    near_count = nc * 2
    z_count = nr // 2
    part1 = PACK_ROWS // near_count
    face_ring = at.ring("face")
    near_ring = at.ring("near")
    z_ring = at.ring("z")
    row_group = at.row_group()
    col_group = at.col_group()
    barrier = pltpu.get_barrier_semaphore()
    for ring in (face_ring, near_ring, z_ring):
        for unused, device, unused2 in ring:
            greet(barrier, device)
    above = at.at(r=jnp.maximum(at.r - 1, 0))
    below = at.at(r=jnp.minimum(at.r + 1, nr - 1))
    before = at.at(c=jnp.maximum(at.c - 1, 0))
    after = at.at(c=jnp.minimum(at.c + 1, nc - 1))
    has_above = jnp.logical_not(at.top)
    has_below = jnp.logical_not(at.bottom)
    has_before = jnp.logical_not(at.left)
    has_after = jnp.logical_not(at.right)
    any_edge = jnp.logical_or(at.row_edge, at.col_edge)
    expected = nf + near_count + z_count - 3
    for present, device in ((has_above, above), (has_below, below), (has_before, before), (has_after, after)):
        expected = expected + jnp.where(present, 1, 0)

        @pl.when(present)
        def _(device=device):
            greet(barrier, device)

    @pl.when(any_edge)
    def _():
        for device, unused, unused2 in row_group:
            greet(barrier, device)

    loads[0].wait()
    natural[...] = x_ref[...].astype(F32).reshape(CH * TR, TC)
    for y in range(TR):
        xw[RIM + y] = natural[pl.ds(y, CH, stride=TR), :].astype(BF)
    pl.semaphore_wait(barrier, expected + jnp.where(any_edge, 3, 0))

    def to_above():
        return send(xw.at[pl.ds(RIM, RIM)], xw.at[pl.ds(RIM + TR, RIM)], near.at[0, 0], near.at[1, 0], above)

    def to_below():
        return send(xw.at[pl.ds(TR, RIM)], xw.at[pl.ds(0, RIM)], near.at[0, 1], near.at[1, 1], below)

    def own_edge():
        return xw.at[pl.ds(jnp.where(at.top, RIM, TR), RIM)]

    @pl.when(at.row_edge)
    def _():
        start_group(row_group, own_edge(), strips, group_sem, 0)

    @pl.when(has_above)
    def _():
        to_above().start()

    @pl.when(has_below)
    def _():
        to_below().start()

    edge_rows = jnp.zeros((RIM, CH, TC), BF)

    @pl.when(at.top)
    def _():
        xw[0:RIM] = edge_rows

    @pl.when(at.bottom)
    def _():
        xw[RIM + TR : PR] = edge_rows

    for row in range(PR):
        spread[:, row * TC : (row + 1) * TC] = spread_block(row)
    flip = flip_matrix()
    for load in loads[1:]:
        load.wait()
    prior[...] = prior_ref[...].astype(F32).reshape(CH * TR, TC)
    cot[...] = cot_ref[...].astype(F32).reshape(CH * TR, TC)
    gc[:, 0 : KS * KS] = kernel_ref[...].T
    is_corner = jnp.logical_and(at.row_edge, at.col_edge)

    @pl.when(has_below)
    def _():
        to_above().wait_recv()

    @pl.when(has_above)
    def _():
        to_below().wait_recv()

    flat = jnp.concatenate([xw[row] for row in range(PR)], axis=1)
    pack[...] = dot_nt(flat, spread[...]).astype(BF)

    def to_before():
        return send(pack, sides.at[1], near.at[0, 2], near.at[1, 2], before)

    def to_after():
        return send(pack, sides.at[0], near.at[0, 3], near.at[1, 3], after)

    @pl.when(at.col_edge)
    def _():
        start_group(col_group, pack, col_strips, group_sem, 2)

    @pl.when(has_before)
    def _():
        to_before().start()

    @pl.when(has_after)
    def _():
        to_after().start()

    lane = lax.broadcasted_iota(jnp.int32, (TR, 8, TC), 2)
    lane2 = lax.broadcasted_iota(jnp.int32, (8, TC), 1)
    xf[RIM : RIM + TR] = xw[RIM : RIM + TR].astype(F32)

    def moved_rows(rows, d):
        if d == 0:
            return rows
        inside = lane < TC - d if d > 0 else lane >= -d
        return jnp.where(inside[: rows.shape[0]], pltpu.roll(rows, (-d) % TC, 2), 0.0)

    def forward(g, carry):
        part = pl.ds(pl.multiple_of(g * 8, 8), 8)
        values = gc[part, :]
        sums = [jnp.zeros((8, TC), F32)] * TR
        own = xf[RIM : RIM + TR, part, :]
        for b in range(KS):
            rows = moved_rows(own, b - RIM)
            shifted[b, RIM : RIM + TR, part, :] = rows
            for a in range(KS):
                tap = a * KS + b
                weight = jnp.broadcast_to(values[:, tap : tap + 1], (8, TC))
                taps[tap, part, :] = weight
                low_y = max(0, RIM - a)
                high_y = min(TR, TR + RIM - a)
                product = weight[None] * rows[low_y + a - RIM : high_y + a - RIM]
                for y in range(low_y, high_y):
                    sums[y] = sums[y] + product[y - low_y]
        for y in range(TR):
            summed[y, part, :] = sums[y]
        return carry

    lax.fori_loop(0, CH // 8, forward, 0)

    @pl.when(at.row_edge)
    def _():
        strips[at.row_kind * 2] = own_edge()[...]
        wait_group(row_group, own_edge(), strips, group_sem, 0)
        taker = partner_of(sf, at.row_kind, at.f, nf)
        code = sc[at.row_kind, taker]
        picked = strips[kind_of(at.row_kind, code) * 2 + code // 2]
        chosen[...] = picked
        start_ring(face_ring, at.f, lambda other: chosen, faces, row_face_sem)
        faces[at.f] = picked

    @pl.when(is_corner)
    def _():
        source = lax.broadcasted_iota(jnp.int32, (TC, TC), 0)
        lanes = lax.broadcasted_iota(jnp.int32, (TC, TC), 1)
        blocks = jnp.zeros((CH, TC), F32)
        for slot in range(4):
            block = (slot // 2) * 2 + (at.col_kind + slot) % 2
            for i in range(RIM):
                blocks = blocks + dot(strips[slot, i], one_hot(block_lanes(lanes, block, i) == source))
        corner_pack[...] = blocks.astype(BF)
        start_ring(face_ring, at.f, lambda other: corner_pack, corner_faces, corner_face_sem)
        corner_faces[at.f] = blocks.astype(BF)

    @pl.when(at.col_edge)
    def _():
        side = at.col_kind + 2
        col_strips[at.col_kind * 2] = pack[...]
        wait_group(col_group, pack, col_strips, group_sem, 2)
        code = sc[side, partner_of(sf, side, at.f, nf)]
        picked = col_strips[kind_of(at.col_kind, code) * 2 + code // 2]
        col_chosen[...] = picked
        start_ring(face_ring, at.f, lambda other: col_chosen, col_faces, col_face_sem)
        col_faces[at.f] = picked

    def late_before():
        return send(pack_late, sides_late.at[1], near_late.at[0, 0], near_late.at[1, 0], before)

    def late_after():
        return send(pack_late, sides_late.at[0], near_late.at[0, 1], near_late.at[1, 1], after)

    @pl.when(at.col_edge)
    def _():
        side = at.col_kind + 2
        turns[0] = turn_matrix(sc[side, at.f])
        turns[1] = turn_matrix(sc[side, partner_of(sf, side, at.f, nf)])

    @pl.when(is_corner)
    def _():
        source = lax.broadcasted_iota(jnp.int32, (TC, TC), 0)
        lanes = lax.broadcasted_iota(jnp.int32, (TC, TC), 1)
        owner, block, row_turn, col_turn = corner_of(sf, sc, at.f, at.row_kind, at.col_kind)
        turns[2] = one_hot(
            corner_lanes(lanes, at.row_kind, at.col_kind, block, row_turn, col_turn) == source
        )
        for other in range(nf):
            owner, block, row_turn, col_turn = corner_of(sf, sc, other, at.row_kind, at.col_kind)
            wanted = corner_lanes(source, at.row_kind, at.col_kind, block, row_turn, col_turn)
            picks[other * TC : (other + 1) * TC, :] = one_hot(jnp.where(owner == at.f, wanted, -1) == lanes)

    @pl.when(at.row_edge)
    def _():
        code = sc[at.row_kind, at.f]
        source = lax.broadcasted_iota(jnp.int32, (TC, TC), 0)
        source = jnp.where(code >= 2, TC - 1 - source, source)
        lanes = lax.broadcasted_iota(jnp.int32, (TC, TC), 1)
        wanted = jnp.where(lanes % 8 < RIM, lanes % 8 + TC - RIM, lanes % 8 - RIM)
        wanted = jnp.where(lanes % 8 < 2 * RIM, wanted, -1)
        first = jnp.where(at.top, 0, RIM + TR)
        for i in range(RIM):
            here = jnp.where(code % 2 == 1, RIM - 1 - i, i)
            late_pick[i * TC : (i + 1) * TC, :] = one_hot(
                jnp.where(lanes // 8 == first + here, wanted, -1) == source
            )
        wait_ring(face_ring, lambda other: chosen, faces, row_face_sem)
        strip = faces[sf[at.row_kind, at.f]]
        flat = jnp.concatenate([strip[i] for i in range(RIM)], axis=1)
        pack_late[...] = dot(flat, late_pick[...]).astype(BF)

        @pl.when(has_before)
        def _():
            late_before().start()

        @pl.when(has_after)
        def _():
            late_after().start()

        xw[pl.ds(jnp.where(at.top, 0, RIM + TR), RIM)] = oriented(strip.astype(F32), code, flip)

    @pl.when(at.col_edge)
    def _():
        side = at.col_kind + 2
        wait_ring(face_ring, lambda other: col_chosen, col_faces, col_face_sem)
        strip = col_faces[sf[side, at.f]]
        sides[at.col_kind] = dot(strip, turns[0]).astype(BF)

    @pl.when(is_corner)
    def _():
        wait_ring(face_ring, lambda other: corner_pack, corner_faces, corner_face_sem)
        owner, unused, unused2, unused3 = corner_of(sf, sc, at.f, at.row_kind, at.col_kind)
        sides_late[at.col_kind] = dot(corner_faces[owner], turns[2]).astype(BF)

    @pl.when(has_after)
    def _():
        to_before().wait_recv()

    @pl.when(has_before)
    def _():
        to_after().wait_recv()

    @pl.when(at.row_edge)
    def _():
        @pl.when(has_after)
        def _():
            late_before().wait_recv()

        @pl.when(has_before)
        def _():
            late_after().wait_recv()

    place = lax.broadcasted_iota(jnp.int32, (CH, TC), 1) % 8
    low = place < RIM
    halo[...] = (
        jnp.where(low, sides[0].astype(F32), sides[1].astype(F32))
        + jnp.where(low, sides_late[0].astype(F32), sides_late[1].astype(F32))
    ).astype(BF)

    xf[0:RIM] = xw[0:RIM].astype(F32)
    xf[RIM + TR : PR] = xw[RIM + TR : PR].astype(F32)

    def forward_rows(g, carry):
        part = pl.ds(pl.multiple_of(g * 8, 8), 8)
        sums = [summed[y, part, :] for y in range(TR)]
        over = xf[0:RIM, part, :]
        under = xf[RIM + TR : PR, part, :]
        for b in range(KS):
            rows_over = moved_rows(over, b - RIM)
            rows_under = moved_rows(under, b - RIM)
            shifted[b, 0:RIM, part, :] = rows_over
            shifted[b, RIM + TR : PR, part, :] = rows_under
            for y in range(TR):
                for a in range(KS):
                    if y + a < RIM:
                        sums[y] = sums[y] + taps[a * KS + b, part, :] * rows_over[y + a]
                    elif y + a >= RIM + TR:
                        sums[y] = sums[y] + taps[a * KS + b, part, :] * rows_under[y + a - RIM - TR]
        for y in range(TR):
            summed[y, part, :] = sums[y]
        return carry

    lax.fori_loop(0, CH // 8, forward_rows, 0)

    def meets(b):
        if b < RIM:
            return jnp.logical_and(place >= b, place < RIM)
        return jnp.logical_and(place >= RIM, place < b)

    def exact_dot(product, values, other):
        high = values.astype(BF)
        return product(high, other) + product((values - high.astype(F32)).astype(BF), other)

    padding = halo[...].astype(F32)
    edge_cells = jnp.zeros((CH, TC), F32)
    for b in range(KS):
        if b == RIM:
            continue
        used = jnp.where(meets(b), padding, 0.0)
        for a in range(KS):
            tap = a * KS + b
            rolled = pltpu.roll(used, (RIM - a * 8 - b) % TC, 1)
            met[tap] = rolled
            edge_cells = edge_cells + taps[tap] * rolled
    ends = exact_dot(dot, edge_cells, spread[:, : TR * TC])

    we = we_ref[...]
    wr_t = wr_ref[...]
    wg = wg_ref[...]
    wc_t = wc_ref[...]
    we_t = we.T
    wr = wr_t.T
    wg_t = wg.T
    wc = wc_t.T

    def cells(load):
        return jnp.concatenate([load(y) for y in range(TR)], axis=1)

    s = cells(lambda y: summed[y]) + ends
    center = s - jnp.mean(s, axis=0, keepdims=True)
    scale = lax.rsqrt(jnp.mean(center * center, axis=0, keepdims=True) + 1e-06)
    unit = center * scale
    normed = unit.astype(BF)
    hidden = dot(we_t, normed)
    acts = []
    slopes = []
    for start in range(0, HID, 32):
        h = hidden[start : start + 32]
        cdf = 0.5 + 0.5 * lax.erf(h * math.sqrt(0.5))
        acts.append((h * cdf).astype(BF))
        slopes.append(cdf + h * (jnp.exp(-0.5 * h * h) * (1.0 / math.sqrt(2.0 * math.pi))))
    act = jnp.concatenate(acts, axis=0)
    slope = jnp.concatenate(slopes, axis=0)
    out = (cells(lambda y: xf[RIM + y]) + dot(wr_t, act)).astype(BF)
    earlier = cells(lambda y: prior[pl.ds(y, CH, stride=TR), :])
    joined = jnp.concatenate([out, earlier.astype(BF)], axis=0)
    gates = jax.nn.sigmoid(dot(wg_t, joined))
    update = gates[:CH]
    reset = gates[CH:]
    joined_reset = jnp.concatenate([out, (reset * earlier).astype(BF)], axis=0)
    proposal = jnp.tanh(dot(wc_t, joined_reset))
    result = (1.0 - update) * earlier + update * proposal
    g = cells(lambda y: cot[pl.ds(y, CH, stride=TR), :])
    d_cand = (g * update * (1.0 - proposal * proposal)).astype(BF)
    d_joined_reset = dot(wc, d_cand)
    d_reset = d_joined_reset[CH:]
    d_gates = jnp.concatenate(
        [
            g * (proposal - earlier) * (update * (1.0 - update)),
            d_reset * earlier * (reset * (1.0 - reset)),
        ],
        axis=0,
    ).astype(BF)
    d_joined = dot(wg, d_gates)
    d_out = (d_joined_reset[:CH] + d_joined[:CH]).astype(BF)
    d_prior = g * (1.0 - update) + d_reset * reset + d_joined[CH:]
    d_hidden = (dot(wr, d_out) * slope).astype(BF)
    d_normed = dot(we, d_hidden)
    d_expand = dot_nt(normed, d_hidden).astype(BF)
    d_reduce = dot_nt(d_out, act).astype(BF)
    grads[0:64] = d_expand[:, :TC]
    grads[64:128] = d_expand[:, TC:]
    grads[128:192] = d_reduce[:, :TC]
    grads[192:256] = d_reduce[:, TC:]
    grads[256:384] = dot_nt(joined, d_gates).astype(BF)
    grads[384:448] = dot_nt(d_cand, joined_reset).astype(BF)
    d_summed = scale * (
        d_normed
        - jnp.mean(d_normed, axis=0, keepdims=True)
        - unit * jnp.mean(d_normed * unit, axis=0, keepdims=True)
    )
    d_center = d_out.astype(F32)
    d_edge = exact_dot(dot_nt, d_summed, spread[:, : TR * TC])
    edge_back[...] = d_edge
    for y in range(TR):
        cut = slice(y * TC, (y + 1) * TC)
        back[y] = d_summed[:, cut]
        total[RIM + y] = d_center[:, cut]
        next_out[y] = result[:, cut].astype(BF)
        prior_out[y] = d_prior[:, cut].astype(BF)

    def piece1(other):
        return grads.at[pl.ds(pl.multiple_of(other * part1, part1), part1)]

    def start_shares(wanted):
        for other, device, step in near_ring:

            @pl.when((other >= LATE_ROW // part1) == wanted)
            def _(other=other, device=device, step=step):
                send(piece1(other), a1.at[at.near], s1.at[0, step], s1.at[1, at.near], device).start()

    def summed_slots(slots, count):
        partial = slots[0].astype(F32)
        for other in range(1, count):
            partial = partial + slots[other].astype(F32)
        return partial.astype(BF)

    start_shares(False)

    d_padding = jnp.zeros((CH, TC), F32)
    for b in range(KS):
        if b == RIM:
            continue
        found = jnp.zeros((CH, TC), F32)
        for a in range(KS):
            found = found + taps[a * KS + b] * pltpu.roll(d_edge, (a * 8 + b - RIM) % TC, 1)
        d_padding = d_padding + jnp.where(meets(b), found, 0.0)
    rim[...] = d_padding.astype(BF)

    def rim_before():
        return send(rim, rim_sides.at[1], near_back.at[0, 2], near_back.at[1, 2], before)

    def rim_after():
        return send(rim, rim_sides.at[0], near_back.at[0, 3], near_back.at[1, 3], after)

    @pl.when(has_before)
    def _():
        rim_before().start()

    @pl.when(has_after)
    def _():
        rim_after().start()

    @pl.when(at.col_edge)
    def _():
        start_ring(face_ring, at.f, lambda other: rim, rim_faces, rim_face_sem)

    def backward_kernel(g, carry):
        part = pl.ds(pl.multiple_of(g * 8, 8), 8)
        rows = back[:, part, :]
        found = jnp.zeros((8, TC), F32)
        for b in range(KS):
            for a in range(KS):
                terms = jnp.sum(rows * shifted[b, a : a + TR, part, :], axis=0)
                if b != RIM:
                    terms = terms + edge_back[part, :] * met[a * KS + b, part, :]
                found = jnp.where(lane2 == a * KS + b, jnp.sum(terms, axis=1, keepdims=True), found)
        gc[part, :] = found
        return carry

    lax.fori_loop(0, CH // 8, backward_kernel, 0)
    grads[448:512] = gc[...].astype(BF)
    start_shares(True)
    a1[at.near] = piece1(at.near)[...]

    lane_all = lax.broadcasted_iota(jnp.int32, (PR, 8, TC), 2)

    def backward(g, carry):
        part = pl.ds(pl.multiple_of(g * 8, 8), 8)
        rows = back[:, part, :]
        inner = jnp.zeros((PR, 8, TC), F32)
        for b in range(KS):
            d = b - RIM
            columns = [None] * PR
            for a in range(KS):
                product = taps[a * KS + b, part, :][None] * rows
                for y in range(TR):
                    columns[y + a] = product[y] if columns[y + a] is None else columns[y + a] + product[y]
            moved = jnp.stack(columns)
            if d:
                inside = lane_all < TC + d if d < 0 else lane_all >= d
                moved = jnp.where(inside, pltpu.roll(moved, d % TC, 2), 0.0)
            inner = inner + moved
        total[0:RIM, part, :] = inner[0:RIM]
        total[RIM : RIM + TR, part, :] = total[RIM : RIM + TR, part, :] + inner[RIM : RIM + TR]
        total[RIM + TR :, part, :] = inner[RIM + TR :]
        return carry

    lax.fori_loop(0, CH // 8, backward, 0)
    @pl.when(has_after)
    def _():
        rim_before().wait_recv()

    @pl.when(has_before)
    def _():
        rim_after().wait_recv()

    def add_columns(packed):
        ends = dot(packed, spread[...])
        for row in range(PR):
            total[row] = total[row] + ends[:, row * TC : (row + 1) * TC]

    add_columns(jnp.where(low, rim_sides[1].astype(F32), rim_sides[0].astype(F32)).astype(BF))

    def own_grad():
        return edges.at[at.row_kind]

    @pl.when(at.row_edge)
    def _():
        edges[at.row_kind] = total[pl.ds(jnp.where(at.top, 0, RIM + TR), RIM)].astype(BF)
        start_ring(face_ring, at.f, lambda other: own_grad(), row_faces, row_back_sem)

    wait_ring(near_ring, piece1, a1, s1)
    partial = summed_slots(a1, near_count)
    a2_src[...] = partial
    start_ring(z_ring, at.z, lambda other: a2_src, a2, s2)
    a2[at.z] = partial

    @pl.when(at.col_edge)
    def _():
        side = at.col_kind + 2
        rim_faces[at.f] = rim[...]
        wait_ring(face_ring, lambda other: rim, rim_faces, rim_face_sem)
        taker = partner_of(sf, side, at.f, nf)
        strip = rim_faces[taker].astype(F32)
        row = lax.broadcasted_iota(jnp.int32, (CH, TC), 1) // 8
        beyond = jnp.logical_or(
            jnp.logical_and(at.top, row < RIM), jnp.logical_and(at.bottom, row >= RIM + TR)
        )
        keep = jnp.logical_and(low == at.left, jnp.logical_not(beyond))
        strip = jnp.where(keep, strip, 0.0).astype(BF)
        turned = dot(strip, turns[1]).astype(BF)
        rim_chosen[...] = turned
        start_group(col_group, rim_chosen, rim_strips, group_back, 0)
        rim_strips[at.col_kind * 2] = turned

    @pl.when(is_corner)
    def _():
        packs = jnp.concatenate([rim_faces[other] for other in range(nf)], axis=1)
        blocks = dot(packs, picks[...])
        corner_out[...] = blocks.astype(BF)
        start_group(row_group, corner_out, corner_strips, corner_group_sem, 0)
        corner_strips[at.row_kind * 2] = blocks.astype(BF)

    wait_ring(z_ring, lambda other: a2_src, a2, s2)
    partial = summed_slots(a2, z_count)
    a3_src[...] = partial
    start_ring(face_ring, at.f, lambda other: a3_src, a3, s3)
    a3[at.f] = partial

    def seam_total(slots, kind, first_side):
        gathered = None
        for side_bit in range(2):
            taker = partner_of(sf, first_side + side_bit, at.f, nf)
            code = sc[first_side + side_bit, taker]
            mine = kind_of(side_bit, code) == kind
            for mirror in range(2):
                use = jnp.logical_and(mine, code // 2 == mirror)
                term = jnp.where(use, slots[side_bit * 2 + mirror].astype(F32), 0.0)
                gathered = term if gathered is None else gathered + term
        return gathered

    @pl.when(at.col_edge)
    def _():
        wait_group(col_group, rim_chosen, rim_strips, group_back, 0)
        back_rim = seam_total(rim_strips, at.col_kind, 2)
        add_columns(jnp.where(low == at.left, 0.0, back_rim).astype(BF))

    def grad_above():
        return send(edges.at[0], row_sides.at[1], near_back.at[0, 0], near_back.at[1, 0], above)

    def grad_below():
        return send(edges.at[1], row_sides.at[0], near_back.at[0, 1], near_back.at[1, 1], below)

    @pl.when(has_above)
    def _():
        edges[0] = total[0:RIM].astype(BF)
        grad_above().start()

    @pl.when(has_below)
    def _():
        edges[1] = total[RIM + TR : PR].astype(BF)
        grad_below().start()

    @pl.when(at.row_edge)
    def _():
        row_faces[at.f] = own_grad()[...]
        wait_ring(face_ring, lambda other: own_grad(), row_faces, row_back_sem)
        taker = partner_of(sf, at.row_kind, at.f, nf)
        strip = oriented(row_faces[taker].astype(F32), sc[at.row_kind, taker], flip_matrix())
        row_chosen[...] = strip
        start_group(row_group, row_chosen, row_strips, group_back, 2)
        row_strips[at.row_kind * 2] = strip

    wait_ring(face_ring, lambda other: a3_src, a3, s3)
    partial = summed_slots(a3, nf)
    a4_src[...] = partial
    start_ring(near_ring, at.near, lambda other: a4_src, a4, s4)
    a4[at.near] = partial

    @pl.when(has_below)
    def _():
        grad_above().wait_recv()
        total[TR : TR + RIM] = total[TR : TR + RIM] + row_sides[1].astype(F32)

    @pl.when(has_above)
    def _():
        grad_below().wait_recv()
        total[RIM : 2 * RIM] = total[RIM : 2 * RIM] + row_sides[0].astype(F32)

    @pl.when(at.row_edge)
    def _():
        wait_group(row_group, row_chosen, row_strips, group_back, 2)
        gathered = seam_total(row_strips, at.row_kind, 0)
        spot = pl.ds(jnp.where(at.top, RIM, TR), RIM)
        total[spot] = total[spot] + gathered

    @pl.when(is_corner)
    def _():
        wait_group(row_group, corner_out, corner_strips, corner_group_sem, 0)
        blocks = corner_strips[0].astype(F32)
        for slot in range(1, 4):
            blocks = blocks + corner_strips[slot].astype(F32)
        source = lax.broadcasted_iota(jnp.int32, (TC, TC), 0)
        lanes = lax.broadcasted_iota(jnp.int32, (TC, TC), 1)
        first = jnp.where(at.top, RIM, TR)
        for i in range(RIM):
            wanted = block_lanes(source, at.row_kind * 2 + at.col_kind, i)
            total[first + i] = total[first + i] + dot(blocks.astype(BF), one_hot(wanted == lanes))

    input_out[...] = total[RIM : RIM + TR].astype(BF)
    wait_ring(near_ring, lambda other: a4_src, a4, s4)
    for other in range(near_count):
        grads_out[other * part1 : (other + 1) * part1] = a4[other]

    @pl.when(has_above)
    def _():
        to_above().wait_send()
        grad_above().wait_send()

    @pl.when(has_below)
    def _():
        to_below().wait_send()
        grad_below().wait_send()

    @pl.when(has_before)
    def _():
        to_before().wait_send()
        rim_before().wait_send()

    @pl.when(has_after)
    def _():
        to_after().wait_send()
        rim_after().wait_send()

    @pl.when(at.row_edge)
    def _():
        done_group(row_group, own_edge(), strips, group_sem, 0)
        done_ring(face_ring, lambda other: chosen, faces, row_face_sem)
        done_ring(face_ring, lambda other: own_grad(), row_faces, row_back_sem)
        done_group(row_group, row_chosen, row_strips, group_back, 2)

        @pl.when(has_before)
        def _():
            late_before().wait_send()

        @pl.when(has_after)
        def _():
            late_after().wait_send()

    @pl.when(is_corner)
    def _():
        done_ring(face_ring, lambda other: corner_pack, corner_faces, corner_face_sem)
        done_group(row_group, corner_out, corner_strips, corner_group_sem, 0)

    @pl.when(at.col_edge)
    def _():
        done_group(col_group, pack, col_strips, group_sem, 2)
        done_ring(face_ring, lambda other: col_chosen, col_faces, col_face_sem)
        done_ring(face_ring, lambda other: rim, rim_faces, rim_face_sem)
        done_group(col_group, rim_chosen, rim_strips, group_back, 0)

    done_ring(near_ring, piece1, a1, s1)
    done_ring(z_ring, lambda other: a2_src, a2, s2)
    done_ring(face_ring, lambda other: a3_src, a3, s3)
    done_ring(near_ring, lambda other: a4_src, a4, s4)


def finish_kernel(
    grad_scale,
    next_rows,
    prior_rows,
    input_rows,
    grads,
    next_out,
    input_out,
    prior_out,
    kernel_out,
    expand_out,
    reduce_out,
    gates_out,
    candidate_out,
    natural,
):
    for rows, out in ((next_rows, next_out), (input_rows, input_out), (prior_rows, prior_out)):
        for y in range(TR):
            natural[pl.ds(y, CH, stride=TR), :] = rows[y].astype(F32)
        out[...] = natural[...].reshape(CH, TR, TC).astype(BF)
    scaled = grads[...].astype(F32) * grad_scale
    expand_out[:, :TC] = scaled[0:64]
    expand_out[:, TC:] = scaled[64:128]
    reduce_out[:, :TC] = scaled[128:192]
    reduce_out[:, TC:] = scaled[192:256]
    gates_out[...] = scaled[256:384]
    candidate_out[...] = scaled[384:448]
    kernel_out[...] = scaled[448:512].T[: KS * KS]


def dma(*shape):
    return pltpu.SemaphoreType.DMA(shape)


def whole_step(dims, *given):
    nf, nr, nc = dims
    near_count = nc * 2
    z_count = nr // 2
    part1 = PACK_ROWS // near_count
    wide = (PR, CH, TC)
    tile = (TR, CH, TC)
    strip = (RIM, CH, TC)
    flat = (CH * TR, TC)
    edge = (CH, TC)
    rows = jax.ShapeDtypeStruct(tile, BF)
    bf16_scratch = [
        wide,
        (4,) + strip,
        strip,
        (nf,) + strip,
        edge,
        (2,) + edge,
        (4,) + edge,
        edge,
        (nf,) + edge,
        (TC, PR * TC),
        edge,
    ]
    f32_scratch = [
        wide,
        (KS * KS, CH, TC),
        (KS,) + wide,
        (KS * KS, CH, TC),
        tile,
        tile,
        flat,
        flat,
        wide,
        edge,
        edge,
    ]
    back_scratch = [
        (PACK_ROWS, TC),
        edge,
        (2,) + strip,
        (2,) + edge,
        (nf,) + edge,
        edge,
        (4,) + edge,
        (2,) + strip,
        (nf,) + strip,
        strip,
        (4,) + strip,
        (near_count, part1, TC),
        (part1, TC),
    ]
    share = (part1, TC)
    sum_scratch = [(z_count,) + share, share, (nf,) + share, share, (near_count,) + share]
    return pl.pallas_call(
        functools.partial(step_kernel, dims),
        out_shape=(rows, rows, rows, jax.ShapeDtypeStruct((PACK_ROWS, TC), BF)),
        in_specs=[HBM] * 10,
        out_specs=(VMEM,) * 4,
        scratch_shapes=[pltpu.VMEM(value.shape, value.dtype) for value in given[:8]]
        + [pltpu.SMEM(value.shape, value.dtype) for value in given[8:]]
        + [dma(10)]
        + [pltpu.VMEM((2,) + edge, BF), pltpu.VMEM(edge, BF), pltpu.VMEM((nf,) + edge, BF)]
        + [pltpu.VMEM(edge, BF), pltpu.VMEM((4,) + edge, BF), dma(2, nf), dma(2, 4), pltpu.VMEM(edge, BF), pltpu.VMEM((RIM * TC, TC), BF)]
        + [pltpu.VMEM((3, TC, TC), BF), pltpu.VMEM((nf * TC, TC), BF)]
        + [pltpu.VMEM(flat, F32)]
        + [pltpu.VMEM(shape, BF) for shape in bf16_scratch]
        + [pltpu.VMEM(shape, F32) for shape in f32_scratch]
        + [pltpu.VMEM(shape, BF) for shape in back_scratch]
        + [pltpu.VMEM(shape, BF) for shape in sum_scratch]
        + [dma(2, 4), dma(2, 2), dma(4, 4), dma(2, nf), dma(2, nf)]
        + [dma(2, 4), dma(4, 4), dma(2, nf), dma(2, nf)]
        + [dma(2, near_count), dma(2, z_count), dma(2, nf), dma(2, near_count)],
        compiler_params=pltpu.CompilerParams(
            collective_id=0, has_side_effects=True, vmem_limit_bytes=LIMIT
        ),
        name="whole_step",
    )(*given)


def finish(grad_scale, next_rows, prior_rows, input_rows, grads):
    tile = jax.ShapeDtypeStruct((CH, TR, TC), BF)
    shapes = ((KS * KS, CH), (CH, HID), (CH, HID), (2 * CH, 2 * CH), (CH, 2 * CH))
    return pl.pallas_call(
        functools.partial(finish_kernel, grad_scale),
        out_shape=(tile,) * 3 + tuple(jax.ShapeDtypeStruct(shape, F32) for shape in shapes),
        in_specs=[VMEM] * 4,
        out_specs=(VMEM,) * 8,
        scratch_shapes=[pltpu.VMEM((CH * TR, TC), F32)],
        compiler_params=pltpu.CompilerParams(vmem_limit_bytes=LIMIT),
        name="finish",
    )(next_rows, prior_rows, input_rows, grads)


def body(dims, cell_total, block_in, hidden_state, state_cotangent, kernel, we, wr, wg, wc, sf, sc):
    rows = whole_step(
        dims, block_in[0], hidden_state[0], state_cotangent[0], kernel.T, we, wr.T, wg, wc.T, sf.T, sc.T
    )
    done = finish(1.0 / math.sqrt(cell_total), *rows)
    return (
        done[0][None],
        done[1][None],
        done[2][None],
        done[3].T,
        done[4],
        done[5].T,
        done[6],
        done[7].T,
    )


def solution(mesh):
    dims = tuple(mesh.shape[name] for name in AXES)
    cell_total = dims[0] * dims[1] * dims[2] * TR * TC
    tiles = P("face", None, "row", "col")
    return jax.shard_map(
        functools.partial(body, dims, cell_total),
        mesh=mesh,
        in_specs=(tiles,) * 3 + (P(),) * 7,
        out_specs=(tiles,) * 3 + (P(),) * 5,
        check_vma=False,
    )
```
